32 devices in a mesh: row: 8 (over y, x, core), col: 4 (over z).
Axes of the slice: x: 2, y: 2, z: 4, core: 2. Of those that a mesh axis runs over, the one named last changes fastest.
Arguments:
- forcing_right_hand: float32 [4, 128, 512], P(None, 'row', 'col'), may hold values from 0 to 2
- material: int32 [4, 128, 512], P(None, 'row', 'col'), may hold values from 0 to 7
- capacity: float32 [8], replicated, may hold values from 0.3 to 3
- conductivity: float32 [8], replicated, may hold values from 0.2 to 2
- vent_open: float32 [128, 512], P('row', 'col'), may hold values from 0.5 to 2
- partners: int32 [8, 4, 2], P('row', 'col'), may hold values from 0 to 7, as said below
- subspace_basis: bfloat16 [64, 4, 128, 512], P(None, None, 'row', 'col'), may hold values from -0.5 to 1.5
Outputs:
- thermal_iterate: float32 [4, 128, 512], P(None, 'row', 'col')
- defect_vector: float32 [4, 128, 512], P(None, 'row', 'col')
- restricted_operator_blocks: float32 [8, 4, 8, 64, 64], P('row', 'col')
The draws below stay inside these ranges and needn't reach their ends.
Inputs may be any that keep to these rules, and one draw needn't show every extreme that they name: In each round the row indices of one col index pair up: partners[q, c, k] = r whenever partners[r, c, k] = q, and q never equals r.
All inputs are finite; a program needn't handle non-finite values.
Results may differ from the reference program's by a relative error of at most 0.01.
Values may be sent and summed in bfloat16 or wider, within the bound.
No kernel may reach another device: no remote copies, remote signals or barrier semaphores. Data moves between devices by JAX's collectives and lax.ppermute only.
A program may use at most 64 MiB of HBM per device.

```python
import math
import jax
import jax.numpy as jnp
from jax import lax

GRID_WIDTH_EAST = 16
GRID_DEPTH_NORTH = 128
FLOOR_STRATA = 4
DEFL = 64
NCLASS = 8
NPAIR = 2
ITERS = 2
COARSE = 2
NX = 128
NY = 512
N_ROW = 8
N_COL = 4


def draw_partners(key, part):
    round_keys = jax.random.split(key, N_COL * NPAIR)

    def one_round(round_key):
        shuffled = jax.random.permutation(round_key, N_ROW).astype(jnp.int32)
        inverse = jnp.argsort(shuffled, stable=True).astype(jnp.int32)
        position = inverse + 1 - 2 * (inverse % 2)
        return shuffled[position]
    rounds = jax.vmap(one_round)(round_keys)
    return rounds.reshape(N_COL, NPAIR, N_ROW).transpose(2, 0, 1).astype(jnp.int32)


def set_ends(array, rng, smallest, high):
    place = [jax.random.randint(jax.random.fold_in(rng, axis), (), 0, length) for axis, length in enumerate(array.shape)]
    widest = array.shape.index(max(array.shape))
    beside = place[:widest] + [(place[widest] + 1) % array.shape[widest]] + place[widest + 1:]
    return array.at[tuple(place)].set(smallest).at[tuple(beside)].set(high)


def shard_levels(stream_key, shape, cuts, low, largest):
    factor_of, own = 1.0, jax.random.fold_in(stream_key, 6)
    for dim, shards_of in cuts:
        steps = jnp.exp(jax.random.uniform(jax.random.fold_in(own, dim), (shards_of,), jnp.float32, low / len(cuts), largest / len(cuts)))
        factor_of = factor_of * jnp.repeat(steps, shape[dim] // shards_of).reshape([-1 if axis == dim else 1 for axis in range(len(shape))])
    return factor_of


def setup_inputs(seed: int = 0) -> dict:
    streams_of = jax.random.split(jax.random.key(seed), 8)
    return {
        "forcing_right_hand": jnp.clip(2.0 * jax.random.uniform(streams_of[0], (FLOOR_STRATA, NX, NY), jnp.float32) ** shard_levels(streams_of[0], (FLOOR_STRATA, NX, NY), ((1, 8), (2, 4)), -0.2, 0.2), 0.0, 2.0),
        "material": set_ends(jax.random.randint(streams_of[1], (FLOOR_STRATA, NX, NY), 0, NCLASS), jax.random.fold_in(streams_of[1], 1), 0, NCLASS - 1).astype(jnp.int32),
        "capacity": jnp.clip(jnp.exp(jax.random.uniform(streams_of[2], (NCLASS,), jnp.float32, math.log(0.3), math.log(3.0))), 0.3, 3.0),
        "conductivity": jnp.clip(jnp.exp(jax.random.uniform(streams_of[3], (NCLASS,), jnp.float32, math.log(0.2), math.log(2.0))), 0.2, 2.0),
        "vent_open": jnp.clip(jnp.exp(math.log(2.0) - 1.3862944 * jax.random.uniform(streams_of[4], (NX, NY), jnp.float32) ** shard_levels(streams_of[4], (NX, NY), ((0, 8), (1, 4)), -0.2, 0.2)), 0.5, 2.0),
        "partners": draw_partners(jax.random.fold_in(streams_of[7], 71), 0),
        "subspace_basis": jnp.clip(-0.5 + 2.0 * jax.random.uniform(streams_of[6], (DEFL, FLOOR_STRATA, NX, NY), jnp.float32) ** shard_levels(streams_of[6], (DEFL, FLOOR_STRATA, NX, NY), ((2, 8), (3, 4)), -0.2, 0.2), -0.5, 1.5).astype(jnp.bfloat16),
    }


highest = lax.Precision.HIGHEST
plenum_gain = 1.0

def harmonic(left_side, right_side):
    return 2.0 * left_side * right_side / (left_side + right_side)

def partner_sum(values, partners):
    blocks = values.reshape(N_ROW, GRID_WIDTH_EAST, N_COL, GRID_DEPTH_NORTH).transpose(0, 2, 1, 3)
    columns = jnp.arange(N_COL, dtype=jnp.int32)[None, :]
    global_accumulate = jnp.zeros(blocks.shape, jnp.float32)
    for pair_round in range(NPAIR):
        global_accumulate = global_accumulate + blocks[partners[:, :, pair_round], columns]
    return global_accumulate.transpose(0, 2, 1, 3).reshape(N_ROW * GRID_WIDTH_EAST, N_COL * GRID_DEPTH_NORTH)

def coefficients(material, capacity, conductivity, vent_open, partners):
    conduct_field = jnp.take(conductivity, material)
    capacity_field = jnp.take(capacity, material)
    padded = jnp.pad(conduct_field, 1)
    upper_z = harmonic(conduct_field, padded[2:, 1:-1, 1:-1])
    lower_z = harmonic(conduct_field, padded[:-2, 1:-1, 1:-1])
    upper_x = harmonic(conduct_field, padded[1:-1, 2:, 1:-1])
    lower_x = harmonic(conduct_field, padded[1:-1, :-2, 1:-1])
    upper_y = harmonic(conduct_field, padded[1:-1, 1:-1, 2:])
    lower_y = harmonic(conduct_field, padded[1:-1, 1:-1, :-2])
    diagonal = capacity_field + upper_z + lower_z + upper_x + lower_x + upper_y + lower_y
    vent_sum = partner_sum(vent_open, partners)
    diagonal = diagonal.at[FLOOR_STRATA - 1].add(plenum_gain * vent_open * vent_sum)
    return (diagonal, upper_z, lower_z, upper_x, lower_x, upper_y, lower_y)

def operate(values, coef_parts, vent_open, partners):
    diagonal, upper_z, lower_z, upper_x, lower_x, upper_y, lower_y = coef_parts
    padded = jnp.pad(values, 1)
    beside_all = upper_z * padded[2:, 1:-1, 1:-1] + lower_z * padded[:-2, 1:-1, 1:-1]
    beside_all = beside_all + upper_x * padded[1:-1, 2:, 1:-1] + lower_x * padded[1:-1, :-2, 1:-1]
    beside_all = beside_all + upper_y * padded[1:-1, 1:-1, 2:] + lower_y * padded[1:-1, 1:-1, :-2]
    result = diagonal * values - beside_all
    coupled = partner_sum(vent_open * values[FLOOR_STRATA - 1], partners)
    return result.at[FLOOR_STRATA - 1].add(-plenum_gain * vent_open * coupled)

def local_apply(basis_block, coef_parts):
    diagonal, upper_z, lower_z, upper_x, lower_x, upper_y, lower_y = coef_parts
    padded = jnp.pad(basis_block, ((0, 0), (1, 1), (1, 1), (1, 1)))
    beside_all = upper_z * padded[:, 2:, 1:-1, 1:-1] + lower_z * padded[:, :-2, 1:-1, 1:-1]
    beside_all = beside_all + upper_x * padded[:, 1:-1, 2:, 1:-1] + lower_x * padded[:, 1:-1, :-2, 1:-1]
    beside_all = beside_all + upper_y * padded[:, 1:-1, 1:-1, 2:] + lower_y * padded[:, 1:-1, 1:-1, :-2]
    return diagonal * basis_block - beside_all

def galerkin_blocks(subspace_basis, coef_parts, vent_open, partners):
    upper_x = coef_parts[3]
    upper_y = coef_parts[5]
    rows_index = jnp.repeat(jnp.arange(N_ROW, dtype=jnp.int32), N_COL)
    cols_index = jnp.tile(jnp.arange(N_COL, dtype=jnp.int32), N_ROW)

    def own_block(position):
        start_x = position[0] * GRID_WIDTH_EAST
        start_y = position[1] * GRID_DEPTH_NORTH
        anchor = jnp.zeros((), jnp.int32)
        basis_block = lax.dynamic_slice(subspace_basis, (anchor, anchor, start_x, start_y), (DEFL, FLOOR_STRATA, GRID_WIDTH_EAST, GRID_DEPTH_NORTH)).astype(jnp.float32)
        block_parts = [lax.dynamic_slice(coef_part, (anchor, start_x, start_y), (FLOOR_STRATA, GRID_WIDTH_EAST, GRID_DEPTH_NORTH)) for coef_part in coef_parts]
        applied = local_apply(basis_block, block_parts)
        return jnp.dot(basis_block.reshape(DEFL, -1), applied.reshape(DEFL, -1).T, precision=highest)
    diagonal = lax.map(own_block, jnp.stack([rows_index, cols_index], axis=1)).reshape(N_ROW, N_COL, DEFL, DEFL)
    last_x = subspace_basis[:, :, GRID_WIDTH_EAST - 1::GRID_WIDTH_EAST, :].astype(jnp.float32)
    first_x = subspace_basis[:, :, 0::GRID_WIDTH_EAST, :].astype(jnp.float32)
    next_x = jnp.concatenate([first_x[:, :, 1:], jnp.zeros_like(first_x[:, :, :1])], axis=2)
    weighted_x = (last_x * upper_x[:, GRID_WIDTH_EAST - 1::GRID_WIDTH_EAST, :]).reshape(DEFL, FLOOR_STRATA, N_ROW, N_COL, GRID_DEPTH_NORTH)
    ahead_x = -jnp.einsum('azrcy,bzrcy->rcab', weighted_x, next_x.reshape(DEFL, FLOOR_STRATA, N_ROW, N_COL, GRID_DEPTH_NORTH), precision=highest)
    behind_x = jnp.concatenate([jnp.zeros_like(ahead_x[:1]), ahead_x[:-1]], axis=0).transpose(0, 1, 3, 2)
    last_y = subspace_basis[:, :, :, GRID_DEPTH_NORTH - 1::GRID_DEPTH_NORTH].astype(jnp.float32)
    first_y = subspace_basis[:, :, :, 0::GRID_DEPTH_NORTH].astype(jnp.float32)
    next_y = jnp.concatenate([first_y[:, :, :, 1:], jnp.zeros_like(first_y[:, :, :, :1])], axis=3)
    weighted_y = (last_y * upper_y[:, :, GRID_DEPTH_NORTH - 1::GRID_DEPTH_NORTH]).reshape(DEFL, FLOOR_STRATA, N_ROW, GRID_WIDTH_EAST, N_COL)
    upper_col = -jnp.einsum('azrxc,bzrxc->rcab', weighted_y, next_y.reshape(DEFL, FLOOR_STRATA, N_ROW, GRID_WIDTH_EAST, N_COL), precision=highest)
    lower_col = jnp.concatenate([jnp.zeros_like(upper_col[:, :1]), upper_col[:, :-1]], axis=1).transpose(0, 1, 3, 2)
    row_numbers = jnp.arange(N_ROW, dtype=jnp.int32)
    row_grid = row_numbers[:, None, None]
    own_hot = (row_grid == row_numbers).astype(jnp.float32)
    next_hot = (row_grid + 1 == row_numbers).astype(jnp.float32)
    prev_hot = (row_grid - 1 == row_numbers).astype(jnp.float32)
    global_accumulate = diagonal[:, :, None] * own_hot[..., None, None] + ahead_x[:, :, None] * next_hot[..., None, None]
    global_accumulate = global_accumulate + behind_x[:, :, None] * prev_hot[..., None, None]
    top_layer = subspace_basis[:, FLOOR_STRATA - 1].astype(jnp.float32) * vent_open
    top_blocks = top_layer.reshape(DEFL, N_ROW, GRID_WIDTH_EAST, N_COL, GRID_DEPTH_NORTH).transpose(1, 3, 0, 2, 4).reshape(N_ROW, N_COL, DEFL, GRID_WIDTH_EAST * GRID_DEPTH_NORTH)
    columns = jnp.arange(N_COL, dtype=jnp.int32)[None, :]
    for pair_round in range(NPAIR):
        target = partners[:, :, pair_round]
        partner_top = top_blocks[target, columns]
        coupled = -plenum_gain * jnp.einsum('rcas,rcbs->rcab', top_blocks, partner_top, precision=highest)
        target_hot = (target[:, :, None] == row_numbers).astype(jnp.float32)
        global_accumulate = global_accumulate + target_hot[..., None, None] * coupled[:, :, None]
    return (global_accumulate, diagonal, lower_col, upper_col)

def remove_subspace_part(subspace_basis, values):

    def one_row(row_number):
        basis_row = lax.dynamic_slice_in_dim(subspace_basis, row_number * GRID_WIDTH_EAST, GRID_WIDTH_EAST, 2).astype(jnp.float32)
        values_row = lax.dynamic_slice_in_dim(values, row_number * GRID_WIDTH_EAST, GRID_WIDTH_EAST, 1)
        return jnp.einsum('azxcy,zxcy->ca', basis_row.reshape(DEFL, FLOOR_STRATA, GRID_WIDTH_EAST, N_COL, GRID_DEPTH_NORTH), values_row.reshape(FLOOR_STRATA, GRID_WIDTH_EAST, N_COL, GRID_DEPTH_NORTH), precision=highest)
    return lax.map(one_row, jnp.arange(N_ROW, dtype=jnp.int32))

def extend_subspace_values(subspace_basis, coarse_vector):

    def one_row(row_number):
        basis_row = lax.dynamic_slice_in_dim(subspace_basis, row_number * GRID_WIDTH_EAST, GRID_WIDTH_EAST, 2).astype(jnp.float32)
        spread_subspace_values = jnp.einsum('azxcy,ca->zxcy', basis_row.reshape(DEFL, FLOOR_STRATA, GRID_WIDTH_EAST, N_COL, GRID_DEPTH_NORTH), coarse_vector[row_number], precision=highest)
        return spread_subspace_values.reshape(FLOOR_STRATA, GRID_WIDTH_EAST, N_COL * GRID_DEPTH_NORTH)
    stacked = lax.map(one_row, jnp.arange(N_ROW, dtype=jnp.int32))
    return stacked.transpose(1, 0, 2, 3).reshape(FLOOR_STRATA, N_ROW * GRID_WIDTH_EAST, N_COL * GRID_DEPTH_NORTH)

def solve_one(factor, right_side):
    return jax.scipy.linalg.cho_solve((factor, True), right_side)

def reference(forcing_right_hand, material, capacity, conductivity, vent_open, partners, subspace_basis):
    coef_parts = coefficients(material, capacity, conductivity, vent_open, partners)
    global_accumulate, diagonal, lower_col, upper_col = galerkin_blocks(subspace_basis, coef_parts, vent_open, partners)
    factors = jnp.linalg.cholesky(diagonal)
    solve_all = jax.vmap(jax.vmap(solve_one))

    def coarse_apply(values):
        along = jnp.einsum('rcqab,qcb->rca', global_accumulate, values, precision=highest)
        before = jnp.concatenate([jnp.zeros_like(values[:, :1]), values[:, :-1]], axis=1)
        after = jnp.concatenate([values[:, 1:], jnp.zeros_like(values[:, :1])], axis=1)
        along = along + jnp.einsum('rcab,rcb->rca', lower_col, before, precision=highest)
        return along + jnp.einsum('rcab,rcb->rca', upper_col, after, precision=highest)

    def invert_galerkin_operator(right_side):
        values = solve_all(factors, right_side)
        for sweep_count in range(COARSE - 1):
            values = values + solve_all(factors, right_side - coarse_apply(values))
        return values

    def operator_apply(values):
        return operate(values, coef_parts, vent_open, partners)
    thermal_iterate = extend_subspace_values(subspace_basis, invert_galerkin_operator(remove_subspace_part(subspace_basis, forcing_right_hand)))
    defect_vector = forcing_right_hand - operator_apply(thermal_iterate)
    conjugate_update = defect_vector - extend_subspace_values(subspace_basis, invert_galerkin_operator(remove_subspace_part(subspace_basis, operator_apply(defect_vector))))
    norm_now = jnp.sum(defect_vector * defect_vector)
    for iteration in range(ITERS):
        applied = operator_apply(conjugate_update)
        update_factor = norm_now / jnp.sum(conjugate_update * applied)
        thermal_iterate = thermal_iterate + update_factor * conjugate_update
        defect_vector = defect_vector - update_factor * applied
        if iteration + 1 < ITERS:
            norm_next = jnp.sum(defect_vector * defect_vector)
            correction = extend_subspace_values(subspace_basis, invert_galerkin_operator(remove_subspace_part(subspace_basis, operator_apply(defect_vector))))
            conjugate_update = norm_next / norm_now * conjugate_update + defect_vector - correction
            norm_now = norm_next
    return (thermal_iterate, defect_vector, global_accumulate / (FLOOR_STRATA * GRID_WIDTH_EAST * GRID_DEPTH_NORTH))
```

```python
import functools

import jax
import jax.numpy as jnp
from jax import lax
from jax.experimental import pallas as pl
from jax.experimental.pallas import tpu as pltpu
from jax.sharding import PartitionSpec as P

F32 = jnp.float32
BF16 = jnp.bfloat16
VMEM = pl.BlockSpec(memory_space=pltpu.VMEM)
SMEM = pl.BlockSpec(memory_space=pltpu.SMEM)
VMEM_LIMIT = 40 * 1024 * 1024


def harmonic(a, b):
    return 2.0 * a * b / (a + b)


def lookup(material, table):
    result = jnp.zeros(material.shape, F32)
    for class_id in range(table.shape[0]):
        result = jnp.where(material == class_id, table[class_id], result)
    return result


class Grid:
    def __init__(self, layers, width, depth):
        self.layers, self.width, self.depth = layers, width, depth
        self.rows = layers * width

    def masks(self):
        shape = (self.rows, self.depth)
        row = lax.broadcasted_iota(jnp.int32, shape, 0)
        lane = lax.broadcasted_iota(jnp.int32, shape, 1)
        return lax.rem(row, self.width), lane, row

    def spread(self, face):
        parts = [
            jnp.broadcast_to(face[z : z + 1], (self.width, self.depth)) for z in range(self.layers)
        ]
        return jnp.concatenate(parts, axis=0)

    def faces(self, v):
        w = self.width
        last = [v[z * w + w - 1 : z * w + w] for z in range(self.layers)]
        first = [v[z * w : z * w + 1] for z in range(self.layers)]
        return last + first

    def payload(self, top, v):
        return jnp.concatenate([top] + self.faces(v), axis=0)

    def around(self, v, low_x, high_x, low_y, high_y):
        xi, lane, _ = self.masks()
        n, d = self.rows, self.depth
        zero = jnp.zeros((n, d), F32)
        own = zero if v is None else v
        plus = zero if v is None else pltpu.roll(v, n - 1, 0)
        minus = zero if v is None else pltpu.roll(v, 1, 0)
        up_x = jnp.where(xi == self.width - 1, self.spread(high_x), plus)
        down_x = jnp.where(xi == 0, self.spread(low_x), minus)
        up_y = pltpu.roll(jnp.where(lane == 0, high_y, own), d - 1, 1)
        down_y = pltpu.roll(jnp.where(lane == d - 1, low_y, own), 1, 1)
        return up_x, down_x, up_y, down_y

    def shifted_z(self, v):
        w = self.width
        return jnp.concatenate([v[w:], v[:w]], axis=0), jnp.concatenate([v[-w:], v[:-w]], axis=0)


def received(grid, ids, pairs, rec):
    count = rec.shape[0]
    w, layers = grid.width, grid.layers
    coupled = rec[ids[0], 0:w, :]
    for k in range(1, pairs):
        coupled = coupled + rec[ids[k], 0:w, :]
    row_at = ids[pairs]
    low = rec[jnp.maximum(row_at - 1, 0), w : w + layers, :]
    high = rec[jnp.minimum(row_at + 1, count - 1), w + layers : w + 2 * layers, :]
    return coupled, low, high


def operate(grid, coef, vent, v, rest):
    coupled, low_x, high_x, low_y, high_y = rest
    up_x, down_x, up_y, down_y = grid.around(v, low_x, high_x, low_y, high_y)
    beside = coef[3] * up_x + coef[4] * down_x + coef[5] * up_y + coef[6] * down_y
    if v is None:
        xi, lane, _ = grid.masks()
        result = -beside
    else:
        up_z, down_z = grid.shifted_z(v)
        result = coef[0] * v - (beside + coef[1] * up_z + coef[2] * down_z)
    w = grid.width
    return jnp.concatenate([result[:-w], result[-w:] - vent * coupled], axis=0)


def project(grid, zm, v):
    d = grid.depth
    parts = [None, None]
    for row in range(grid.rows):
        term = zm[:, row * d : (row + 1) * d].astype(F32) * v[row : row + 1, :]
        k = row % 2
        parts[k] = term if parts[k] is None else parts[k] + term
    return jnp.sum(parts[0] + parts[1], axis=1, keepdims=True)


def solve_own(inverse, column):
    size = inverse.shape[0]
    along = jnp.sum(inverse[...] * column, axis=0, keepdims=True)
    eye = lax.broadcasted_iota(jnp.int32, (size, size), 0) == lax.broadcasted_iota(
        jnp.int32, (size, size), 1
    )
    return jnp.sum(jnp.where(eye, along, 0.0), axis=1, keepdims=True)


def expand(grid, zm, column, out):
    d = grid.depth
    wide = jnp.broadcast_to(column, (column.shape[0], d))
    for row in range(grid.rows):
        out[row : row + 1, :] = jnp.sum(
            zm[:, row * d : (row + 1) * d].astype(F32) * wide, axis=0, keepdims=True
        )


def to_all(grid, pay, top, v):
    block = grid.payload(top, v)
    for slot in range(pay.shape[0]):
        pay[slot] = block


def split3(w):
    hi = w.astype(BF16)
    rest = w - hi.astype(F32)
    mid = rest.astype(BF16)
    lo = (rest - mid.astype(F32)).astype(BF16)
    return hi, mid, lo


def dot_nt(a, b):
    return lax.dot_general(a, b, (((1,), (1,)), ((), ())), preferred_element_type=F32)


def fold3(stacked):
    size = stacked.shape[0] // 3
    return stacked[:size] + (stacked[size : 2 * size] + stacked[2 * size :])


def gram(grid, zm, w3, weights, first_row=0):
    d = grid.depth
    size = zm.shape[0]
    total = None
    group = 8
    rows = weights.shape[0]
    for start in range(0, rows, group):
        stop = min(start + group, rows)
        for row in range(start, stop):
            at = slice(row * d, (row + 1) * d)
            src = slice((first_row + row) * d, (first_row + row + 1) * d)
            hi, mid, lo = split3(zm[:, src].astype(F32) * weights[row : row + 1, :])
            w3[0:size, at] = hi
            w3[size : 2 * size, at] = mid
            w3[2 * size : 3 * size, at] = lo
        part = dot_nt(
            w3[:, start * d : stop * d],
            zm[:, (first_row + start) * d : (first_row + stop) * d],
        )
        total = part if total is None else total + part
    return fold3(total)


def invert_spd(m):
    size = m.shape[0]
    row_id = lax.broadcasted_iota(jnp.int32, (size, size), 0)
    col_id = lax.broadcasted_iota(jnp.int32, (size, size), 1)
    for k in range(size):
        row = m[k : k + 1, :]
        col = m[:, k : k + 1]
        inv = 1.0 / m[k : k + 1, k : k + 1]
        scaled_row = row * inv
        new = m - col * scaled_row
        new = jnp.where(col_id == k, col * inv, new)
        new = jnp.where(row_id == k, scaled_row, new)
        m = jnp.where((row_id == k) & (col_id == k), -inv, new)
    return -m


def k_first(grid, material, conductivity, vent, cond_out, pay):
    cond = lookup(material[...], conductivity)
    cond_out[...] = cond
    to_all(grid, pay, vent[...], cond)


def conductances(grid, cond, low_x, high_x, low_y, high_y):
    _, _, row = grid.masks()
    up_z, down_z = grid.shifted_z(cond)
    uz = jnp.where(row < grid.rows - grid.width, harmonic(cond, up_z), 0.0)
    lz = jnp.where(row >= grid.width, harmonic(cond, down_z), 0.0)
    ux, lx, uy, ly = [harmonic(cond, c) for c in grid.around(cond, low_x, high_x, low_y, high_y)]
    return uz, lz, ux, lx, uy, ly


def k_basis(
    grid, basis, rhs, material, conductivity, capacity,
    zm, own, projected, panel, face_last, face_first, zs, zr, w3, coef,
):
    n, d, w = grid.rows, grid.depth, grid.width
    size = basis.shape[0]
    cond = lookup(material[...], conductivity)
    zero_face = jnp.zeros((grid.layers, d), F32)
    zero = jnp.zeros((n, d), F32)
    uz, lz, ux, lx, uy, ly = conductances(grid, cond, zero_face, zero_face, zero, zero)
    coef[0] = lookup(material[...], capacity) + uz + lz + ux + lx + uy + ly
    for i, c in enumerate((uz, lz, ux, lx, uy, ly)):
        coef[i + 1] = c

    def unpack(a, _):
        zs[pl.ds(a * n, n), :] = basis[a].astype(F32)
        return 0

    lax.fori_loop(0, size, unpack, 0, unroll=4)
    parts = [None, None]
    for row in range(n):
        z = zs[pl.ds(row, size, stride=n), :]
        zr[row] = z
        packed = z.astype(BF16)
        zm[:, row * d : (row + 1) * d] = packed
        layer, x = divmod(row, w)
        if layer == grid.layers - 1:
            panel[:, x * d : (x + 1) * d] = packed
        if x == w - 1:
            face_last[:, layer * d : (layer + 1) * d] = packed
        if x == 0:
            face_first[:, layer * d : (layer + 1) * d] = packed
        term = z * rhs[row : row + 1, :]
        parts[row % 2] = term if parts[row % 2] is None else parts[row % 2] + term
    projected[...] = parts[0] + parts[1]
    total = None
    for start in range(0, n, 8):
        for row in range(start, start + 8):
            z = zr[row]

            def c(i):
                return coef[i, row : row + 1, :]

            acc = c(0) * z
            if row + w < n:
                acc = acc - c(1) * zr[row + w]
            if row >= w:
                acc = acc - c(2) * zr[row - w]
            if row % w < w - 1:
                acc = acc - c(3) * zr[row + 1]
            if row % w > 0:
                acc = acc - c(4) * zr[row - 1]
            acc = acc - c(5) * pltpu.roll(z, d - 1, 1) - c(6) * pltpu.roll(z, 1, 1)
            at = slice(row * d, (row + 1) * d)
            hi, mid, lo = split3(acc)
            w3[0:size, at] = hi
            w3[size : 2 * size, at] = mid
            w3[2 * size : 3 * size, at] = lo
        part = dot_nt(w3[:, start * d : (start + 8) * d], zm[:, start * d : (start + 8) * d])
        total = part if total is None else total + part
    own[...] = fold3(total)


def k_setup(
    grid, pairs, cols, ids, conductivity, capacity, material, vent, cond, cond_low, cond_high, rec,
    zm, own_inner, projected, coef, own, inverse, v0, pay, w3,
):
    n, d, w = grid.rows, grid.depth, grid.width
    count = rec.shape[0]
    vent_sum, low_x, high_x = received(grid, ids, pairs, rec)
    row_at, col_at = ids[pairs], ids[pairs + 1]
    low_x = jnp.where(row_at > 0, low_x, 0.0)
    high_x = jnp.where(row_at < count - 1, high_x, 0.0)
    low_y = jnp.where(col_at > 0, cond_low[...], 0.0)
    high_y = jnp.where(col_at < cols - 1, cond_high[...], 0.0)
    uz, lz, ux, lx, uy, ly = conductances(grid, cond[...], low_x, high_x, low_y, high_y)
    xi, lane, row = grid.masks()
    extra = (
        jnp.where(xi == w - 1, ux, 0.0)
        + jnp.where(xi == 0, lx, 0.0)
        + jnp.where(lane == d - 1, uy, 0.0)
        + jnp.where(lane == 0, ly, 0.0)
    )
    plenum = vent[...] * vent_sum
    extra = jnp.concatenate([extra[:-w], extra[-w:] + plenum], axis=0)
    diagonal = lookup(material[...], capacity) + uz + lz + ux + lx + uy + ly
    coef[0] = jnp.concatenate([diagonal[:-w], diagonal[-w:] + plenum], axis=0)
    for i, c in enumerate((uz, lz, ux, lx, uy, ly)):
        coef[i + 1] = c
    block = own_inner[...] + gram(grid, zm, w3, extra)
    own[...] = block
    inverse[...] = invert_spd(block)
    y0 = solve_own(inverse, jnp.sum(projected[...], axis=1, keepdims=True))
    expand(grid, zm, y0, v0)
    field = v0[...]
    to_all(grid, pay, vent[...] * field[-w:], field)


def incoming(grid, pairs, ids, rec, low, high):
    coupled, low_x, high_x = received(grid, ids, pairs, rec)
    return coupled, low_x, high_x, low[...], high[...]


def k_coarse(grid, pairs, base, ids, coef, vent, zm, inverse, field, rec, low, high, *outs):
    if base:
        base_ref, out, pay, scratch = outs
    else:
        out, pay, scratch = outs
    beside = operate(grid, coef, vent[...], None, incoming(grid, pairs, ids, rec, low, high))
    expand(grid, zm, solve_own(inverse, project(grid, zm, beside)), scratch)
    result = field[...] - scratch[...]
    if base:
        result = base_ref[...] - result
    out[...] = result
    to_all(grid, pay, vent[...] * result[-grid.width :], result)


def k_apply(grid, pairs, base, ids, coef, vent, field, rec, low, high, *outs):
    image = operate(grid, coef, vent[...], field[...], incoming(grid, pairs, ids, rec, low, high))
    if base:
        base_ref, out, pay = outs
        image = base_ref[...] - image
    else:
        out, pay = outs
    out[...] = image
    to_all(grid, pay, vent[...] * image[-grid.width :], image)


def k_apply_solve(grid, pairs, ids, coef, vent, zm, inverse, field, rec, low, high, out, pay):
    image = operate(grid, coef, vent[...], field[...], incoming(grid, pairs, ids, rec, low, high))
    expand(grid, zm, solve_own(inverse, project(grid, zm, image)), out)
    result = out[...]
    to_all(grid, pay, vent[...] * result[-grid.width :], result)


def k_dots(grid, pairs, ids, coef, vent, field, rec, low, high, r0, p0, i0, out, pay):
    image = operate(grid, coef, vent[...], field[...], incoming(grid, pairs, ids, rec, low, high))
    out[...] = image
    d, r, p, i = field[...], r0[...], p0[...], i0[...]
    products = (r * r, p * i, r * i, i * i, d * i, d * image)
    parts = [jnp.sum(q, axis=0, keepdims=True) for q in products]
    parts.append(jnp.zeros((8 - len(parts), grid.depth), F32))
    block = jnp.concatenate(parts, axis=0)
    for slot in range(pay.shape[0]):
        pay[slot] = block


def k_last(rec, x0, r0, p0, i0, d, image, x2, r2):
    total = rec[0]
    for slot in range(1, rec.shape[0]):
        total = total + rec[slot]
    sums = jnp.sum(total, axis=1, keepdims=True)
    rr, pi, ri, ii, di, dd = [sums[k : k + 1, :] for k in range(6)]
    a1 = rr / pi
    new = rr - 2.0 * a1 * ri + a1 * a1 * ii
    grow = 1.0 + new / rr
    a2 = new / (grow * grow * pi - 2.0 * grow * a1 * di + a1 * a1 * dd)
    x2[...] = x0[...] + (a1 + a2 * grow) * p0[...] - (a2 * a1) * d[...]
    r2[...] = r0[...] - (a1 + a2 * grow) * i0[...] + (a2 * a1) * image[...]


def k_blocks(
    grid, pairs, scale, ids, vent, coef, rec, panel, panels, own, face_last, face_first,
    next_first, prev_last, out, w3,
):
    n, d, w, layers = grid.rows, grid.depth, grid.width, grid.layers
    count, size = out.shape[0], out.shape[1]
    row_at = ids[pairs]
    for slot in range(count):
        out[slot] = jnp.zeros((size, size), F32)
    out[row_at] = own[...] * scale

    def weighted(src, weights, other):
        rows = weights.shape[0]
        for row in range(rows):
            at = slice(row * d, (row + 1) * d)
            hi, mid, lo = split3(src[:, at].astype(F32) * weights[row : row + 1, :])
            w3[0:size, at] = hi
            w3[size : 2 * size, at] = mid
            w3[2 * size : 3 * size, at] = lo
        return fold3(dot_nt(w3[:, : rows * d], other)) * (-scale)

    ux = coef[3]
    lx = coef[4]
    high = jnp.concatenate([ux[z * w + w - 1 : z * w + w] for z in range(layers)], axis=0)
    low = jnp.concatenate([lx[z * w : z * w + 1] for z in range(layers)], axis=0)
    ahead = weighted(face_last, high, next_first[...])
    up = jnp.minimum(row_at + 1, count - 1)
    out[up] = out[up] + jnp.where(row_at < count - 1, ahead, 0.0)
    behind = weighted(face_first, low, prev_last[...])
    down = jnp.maximum(row_at - 1, 0)
    out[down] = out[down] + jnp.where(row_at > 0, behind, 0.0)
    for k in range(pairs):
        at = ids[k]
        block = weighted(panel, vent[...] * rec[at, 0:w, :], panels[at])
        out[at] = out[at] + block


def call(kernel, outs, operands, scratch=(), smem=0, cost=None):
    specs = [SMEM] * smem + [VMEM] * (len(operands) - smem)
    return pl.pallas_call(
        kernel,
        out_shape=tuple(jax.ShapeDtypeStruct(s, t) for s, t in outs),
        in_specs=specs,
        out_specs=tuple([VMEM] * len(outs)),
        scratch_shapes=list(scratch),
        compiler_params=pltpu.CompilerParams(vmem_limit_bytes=VMEM_LIMIT),
        cost_estimate=cost,
    )(*operands)


def body(forcing_right_hand, material, capacity, conductivity, vent_open, partners, subspace_basis):
    layers, width, depth = forcing_right_hand.shape
    size = subspace_basis.shape[0]
    grid = Grid(layers, width, depth)
    n, cells = grid.rows, forcing_right_hand.size
    row_count, col_count = lax.axis_size("row"), lax.axis_size("col")
    pairs = partners.shape[-1]
    ids = jnp.concatenate(
        [
            partners.reshape(-1),
            jnp.stack([lax.axis_index("row"), lax.axis_index("col")]).astype(jnp.int32),
        ]
    )
    rhs = forcing_right_hand.reshape(n, depth)
    classes = material.reshape(n, depth)
    basis = subspace_basis.reshape(size, n, depth)
    field = ((n, depth), F32)
    pay = ((row_count, width + 2 * layers, depth), F32)
    small = ((size, size), F32)

    def cyclic(value, axis, step):
        count = lax.axis_size(axis)
        return lax.ppermute(value, axis, [(i, (i + step) % count) for i in range(count)])

    def exchange(value, payload):
        low = cyclic(value, "col", 1)
        high = cyclic(value, "col", -1)
        rec = lax.all_to_all(payload, "row", 0, 0)
        return rec, low, high

    cond, pay0 = call(
        lambda c, m, v, o, p: k_first(grid, m, c, v, o, p),
        (field, pay),
        (conductivity, classes, vent_open),
        smem=1,
    )
    rec0, cond_low, cond_high = exchange(cond, pay0)

    zm, own_inner, projected, panel, face_last, face_first = call(
        lambda c, k, b, f, m, *rest: k_basis(grid, b, f, m, c, k, *rest),
        (
            ((size, n * depth), BF16),
            small,
            ((size, depth), F32),
            ((size, width * depth), BF16),
            ((size, layers * depth), BF16),
            ((size, layers * depth), BF16),
        ),
        (conductivity, capacity, basis, rhs, classes),
        scratch=(
            pltpu.VMEM((size * n, depth), F32),
            pltpu.VMEM((n, size, depth), F32),
            pltpu.VMEM((3 * size, n * depth), BF16),
            pltpu.VMEM((7, n, depth), F32),
        ),
        smem=2,
        cost=pl.CostEstimate(flops=200_000_000, bytes_accessed=8_000_000, transcendentals=0),
    )
    panels = lax.all_gather(panel, "row", axis=0)
    prev_last = cyclic(face_last, "row", 1)
    next_first = cyclic(face_first, "row", -1)

    coef, own, inverse, v0, pay1 = call(
        functools.partial(k_setup, grid, pairs, col_count),
        (((7, n, depth), F32), small, small, field, pay),
        (
            ids, conductivity, capacity, classes, vent_open, cond, cond_low, cond_high, rec0,
            zm, own_inner, projected,
        ),
        scratch=(pltpu.VMEM((3 * size, n * depth), BF16),),
        smem=3,
    )
    rec, low, high = exchange(v0, pay1)
    x0, pay2 = call(
        functools.partial(k_coarse, grid, pairs, False),
        (field, pay),
        (ids, coef, vent_open, zm, inverse, v0, rec, low, high),
        scratch=(pltpu.VMEM((n, depth), F32),),
        smem=1,
    )
    rec, low, high = exchange(x0, pay2)
    r0, pay3 = call(
        functools.partial(k_apply, grid, pairs, True),
        (field, pay),
        (ids, coef, vent_open, x0, rec, low, high, rhs),
        smem=1,
    )
    rec, low, high = exchange(r0, pay3)
    u0, pay4 = call(
        functools.partial(k_apply_solve, grid, pairs),
        (field, pay),
        (ids, coef, vent_open, zm, inverse, r0, rec, low, high),
        smem=1,
    )
    rec, low, high = exchange(u0, pay4)
    p0, pay5 = call(
        functools.partial(k_coarse, grid, pairs, True),
        (field, pay),
        (ids, coef, vent_open, zm, inverse, u0, rec, low, high, r0),
        scratch=(pltpu.VMEM((n, depth), F32),),
        smem=1,
    )
    rec, low, high = exchange(p0, pay5)
    i0, pay6 = call(
        functools.partial(k_apply, grid, pairs, False),
        (field, pay),
        (ids, coef, vent_open, p0, rec, low, high),
        smem=1,
    )
    rec, low, high = exchange(i0, pay6)
    s0, pay7 = call(
        functools.partial(k_apply_solve, grid, pairs),
        (field, pay),
        (ids, coef, vent_open, zm, inverse, i0, rec, low, high),
        smem=1,
    )
    rec, low, high = exchange(s0, pay7)
    d0, pay8 = call(
        functools.partial(k_coarse, grid, pairs, True),
        (field, pay),
        (ids, coef, vent_open, zm, inverse, s0, rec, low, high, i0),
        scratch=(pltpu.VMEM((n, depth), F32),),
        smem=1,
    )
    rec, low, high = exchange(d0, pay8)
    image, pay9 = call(
        functools.partial(k_dots, grid, pairs),
        (field, ((row_count * col_count, 8, depth), F32)),
        (ids, coef, vent_open, d0, rec, low, high, r0, p0, i0),
        smem=1,
    )
    rec9 = lax.all_to_all(pay9, ("row", "col"), 0, 0)
    x2, r2 = call(k_last, (field, field), (rec9, x0, r0, p0, i0, d0, image))

    (blocks,) = call(
        functools.partial(k_blocks, grid, pairs, 1.0 / cells),
        (((row_count, size, size), F32),),
        (
            ids, vent_open, coef, rec0, panel, panels, own, face_last, face_first,
            next_first, prev_last,
        ),
        scratch=(pltpu.VMEM((3 * size, width * depth), BF16),),
        smem=1,
        cost=pl.CostEstimate(flops=100_000_000, bytes_accessed=4_000_000, transcendentals=0),
    )
    shape = forcing_right_hand.shape
    return x2.reshape(shape), r2.reshape(shape), blocks[None, None]


def solution(mesh):
    return jax.shard_map(
        body,
        mesh=mesh,
        in_specs=(
            P(None, "row", "col"),
            P(None, "row", "col"),
            P(),
            P(),
            P("row", "col"),
            P("row", "col", None),
            P(None, None, "row", "col"),
        ),
        out_specs=(P(None, "row", "col"), P(None, "row", "col"), P("row", "col", None, None, None)),
        check_vma=False,
    )
```

```python
import functools

import jax
import jax.numpy as jnp
from jax import lax
from jax.experimental import pallas as pl
from jax.experimental.pallas import tpu as pltpu
from jax.sharding import PartitionSpec as P

F32 = jnp.float32
BF16 = jnp.bfloat16
VMEM = pl.BlockSpec(memory_space=pltpu.VMEM)
SMEM = pl.BlockSpec(memory_space=pltpu.SMEM)
HBM = pl.BlockSpec(memory_space=pltpu.HBM)
ANY = pl.BlockSpec(memory_space=pl.ANY)
VMEM_LIMIT = 40 * 1024 * 1024


def harmonic(a, b):
    return 2.0 * a * b / (a + b)


def lookup(material, table):
    result = jnp.zeros(material.shape, F32)
    for class_id in range(table.shape[0]):
        result = jnp.where(material == class_id, table[class_id], result)
    return result


class Grid:
    def __init__(self, layers, width, depth):
        self.layers, self.width, self.depth = layers, width, depth
        self.rows = layers * width

    def masks(self):
        shape = (self.rows, self.depth)
        row = lax.broadcasted_iota(jnp.int32, shape, 0)
        lane = lax.broadcasted_iota(jnp.int32, shape, 1)
        return lax.rem(row, self.width), lane, row

    def spread(self, face):
        parts = [
            jnp.broadcast_to(face[z : z + 1], (self.width, self.depth)) for z in range(self.layers)
        ]
        return jnp.concatenate(parts, axis=0)

    def faces(self, v):
        w = self.width
        last = [v[z * w + w - 1 : z * w + w] for z in range(self.layers)]
        first = [v[z * w : z * w + 1] for z in range(self.layers)]
        return last + first

    def payload(self, top, v):
        return jnp.concatenate([top] + self.faces(v), axis=0)

    def around(self, v, low_x, high_x, low_y, high_y):
        xi, lane, _ = self.masks()
        n, d = self.rows, self.depth
        zero = jnp.zeros((n, d), F32)
        own = zero if v is None else v
        plus = zero if v is None else pltpu.roll(v, n - 1, 0)
        minus = zero if v is None else pltpu.roll(v, 1, 0)
        up_x = jnp.where(xi == self.width - 1, self.spread(high_x), plus)
        down_x = jnp.where(xi == 0, self.spread(low_x), minus)
        up_y = pltpu.roll(jnp.where(lane == 0, high_y, own), d - 1, 1)
        down_y = pltpu.roll(jnp.where(lane == d - 1, low_y, own), 1, 1)
        return up_x, down_x, up_y, down_y

    def shifted_z(self, v):
        w = self.width
        return jnp.concatenate([v[w:], v[:w]], axis=0), jnp.concatenate([v[-w:], v[:-w]], axis=0)


def received(grid, ids, pairs, rec):
    count = rec.shape[0]
    w, layers = grid.width, grid.layers
    coupled = rec[ids[0], 0:w, :]
    for k in range(1, pairs):
        coupled = coupled + rec[ids[k], 0:w, :]
    row_at = ids[pairs]
    low = rec[jnp.maximum(row_at - 1, 0), w : w + layers, :]
    high = rec[jnp.minimum(row_at + 1, count - 1), w + layers : w + 2 * layers, :]
    return coupled, low, high


def operate(grid, coef, vent, v, rest):
    coupled, low_x, high_x, low_y, high_y = rest
    up_x, down_x, up_y, down_y = grid.around(v, low_x, high_x, low_y, high_y)
    beside = coef[3] * up_x + coef[4] * down_x + coef[5] * up_y + coef[6] * down_y
    if v is None:
        xi, lane, _ = grid.masks()
        result = -beside
    else:
        up_z, down_z = grid.shifted_z(v)
        result = coef[0] * v - (beside + coef[1] * up_z + coef[2] * down_z)
    w = grid.width
    return jnp.concatenate([result[:-w], result[-w:] - vent * coupled], axis=0)


def project(grid, zm, v):
    d = grid.depth
    parts = [None, None]
    for row in range(grid.rows):
        term = zm[:, row * d : (row + 1) * d].astype(F32) * v[row : row + 1, :]
        k = row % 2
        parts[k] = term if parts[k] is None else parts[k] + term
    return jnp.sum(parts[0] + parts[1], axis=1, keepdims=True)


def solve_own(inverse, column):
    size = inverse.shape[0]
    along = jnp.sum(inverse[...] * column, axis=0, keepdims=True)
    eye = lax.broadcasted_iota(jnp.int32, (size, size), 0) == lax.broadcasted_iota(
        jnp.int32, (size, size), 1
    )
    return jnp.sum(jnp.where(eye, along, 0.0), axis=1, keepdims=True)


def expand(grid, zm, column, out):
    d = grid.depth
    wide = jnp.broadcast_to(column, (column.shape[0], d))
    for row in range(grid.rows):
        out[row : row + 1, :] = jnp.sum(
            zm[:, row * d : (row + 1) * d].astype(F32) * wide, axis=0, keepdims=True
        )


def to_all(grid, pay, top, v, *more):
    block = jnp.concatenate([grid.payload(top, v), *more], axis=0)
    for slot in range(pay.shape[0]):
        pay[slot] = block


def split3(w):
    hi = w.astype(BF16)
    rest = w - hi.astype(F32)
    mid = rest.astype(BF16)
    lo = (rest - mid.astype(F32)).astype(BF16)
    return hi, mid, lo


def dot_nt(a, b):
    return lax.dot_general(a, b, (((1,), (1,)), ((), ())), preferred_element_type=F32)


def fold3(stacked):
    size = stacked.shape[0] // 3
    return stacked[:size] + (stacked[size : 2 * size] + stacked[2 * size :])


def gram(grid, zm, w3, weights, first_row=0):
    d = grid.depth
    size = zm.shape[0]
    total = None
    group = 8
    rows = weights.shape[0]
    for start in range(0, rows, group):
        stop = min(start + group, rows)
        for row in range(start, stop):
            at = slice(row * d, (row + 1) * d)
            src = slice((first_row + row) * d, (first_row + row + 1) * d)
            hi, mid, lo = split3(zm[:, src].astype(F32) * weights[row : row + 1, :])
            w3[0:size, at] = hi
            w3[size : 2 * size, at] = mid
            w3[2 * size : 3 * size, at] = lo
        part = dot_nt(
            w3[:, start * d : stop * d],
            zm[:, (first_row + start) * d : (first_row + stop) * d],
        )
        total = part if total is None else total + part
    return fold3(total)


def invert_spd(m, ahead=5):
    size = m.shape[0]
    row_id = lax.broadcasted_iota(jnp.int32, (size, size), 0)
    col_id = lax.broadcasted_iota(jnp.int32, (size, size), 1)

    def column(k):
        return jnp.broadcast_to(m[:, k : k + 1], (size, size))

    waiting = {k: column(k) for k in range(min(ahead + 1, size))}
    for k in range(size):
        col = waiting.pop(k)
        inv = 1.0 / col[k : k + 1, :]
        for j in list(waiting):
            at_row = col[j : j + 1, :] * inv
            waiting[j] = jnp.where(row_id == k, at_row, waiting[j] - col * at_row)
        scaled_row = jnp.where(col_id[:1] == k, -inv, m[k : k + 1, :] * inv)
        m = jnp.where(row_id == k, scaled_row, jnp.where(col_id == k, 0.0, m) - col * scaled_row)
        if k + ahead + 1 < size:
            waiting[k + ahead + 1] = column(k + ahead + 1)
    return -m


def opposite(place):
    return {1: 2, 2: 1, 3: 4, 4: 3}.get(place, place)


def k_first(
    grid, material, conductivity, capacity, vent, partners, cond_out, cap_out, vent_out, pay,
    classes, cond_table, cap_table, pair_table, sems,
):
    copies = [
        pltpu.make_async_copy(src, dst, sems.at[i])
        for i, (src, dst) in enumerate(
            (
                (material, classes),
                (conductivity, cond_table),
                (capacity, cap_table),
                (vent, vent_out),
                (partners, pair_table),
            )
        )
    ]
    for copy in copies:
        copy.start()
    for copy in copies:
        copy.wait()
    cond = lookup(classes[...], cond_table)
    lane = lax.broadcasted_iota(jnp.int32, (8, grid.depth), 1)
    names = jnp.zeros((8, grid.depth), F32)
    for k in range(pair_table.shape[0]):
        names = jnp.where(lane == k, pair_table[k].astype(F32), names)
    cond_out[0 : grid.rows, :] = cond
    cond_out[grid.rows :, :] = names
    cap_out[...] = lookup(classes[...], cap_table)
    to_all(grid, pay, vent_out[...], cond, names)


def conductances(grid, cond, low_x, high_x, low_y, high_y):
    _, _, row = grid.masks()
    up_z, down_z = grid.shifted_z(cond)
    uz = jnp.where(row < grid.rows - grid.width, harmonic(cond, up_z), 0.0)
    lz = jnp.where(row >= grid.width, harmonic(cond, down_z), 0.0)
    ux, lx, uy, ly = [harmonic(cond, c) for c in grid.around(cond, low_x, high_x, low_y, high_y)]
    return uz, lz, ux, lx, uy, ly


def k_panel(grid, basis, _, panel, top, wide, sem):
    w, d = grid.width, grid.depth
    size = basis.shape[0]
    copy = pltpu.make_async_copy(basis.at[:, pl.ds(grid.rows - w, w), :], top, sem)
    copy.start()
    copy.wait()

    def unpack(a, _):
        wide[pl.ds(a * w, w), :] = top[a].astype(F32)
        return 0

    lax.fori_loop(0, size, unpack, 0, unroll=8)
    for x in range(w):
        panel[:, x * d : (x + 1) * d] = wide[pl.ds(x, size, stride=w), :].astype(BF16)


def k_basis(
    grid, basis, rhs_in, cond_ref, cap_ref,
    zm, own, projected, face_last, face_first, face_y, rhs, zs, zr, w3, coef, packed_basis, sems,
):
    n, d, w = grid.rows, grid.depth, grid.width
    size = basis.shape[0]
    pieces = sems.shape[0] - 1
    step = size // pieces
    copies = [
        pltpu.make_async_copy(
            basis.at[pl.ds(i * step, step)], packed_basis.at[pl.ds(i * step, step)], sems.at[i]
        )
        for i in range(pieces)
    ]
    copies.append(pltpu.make_async_copy(rhs_in, rhs, sems.at[pieces]))
    for copy in copies:
        copy.start()
    cond = cond_ref[0:n, :]
    zero_face = jnp.zeros((grid.layers, d), F32)
    zero = jnp.zeros((n, d), F32)
    uz, lz, ux, lx, uy, ly = conductances(grid, cond, zero_face, zero_face, zero, zero)
    coef[0] = cap_ref[...] + uz + lz + ux + lx + uy + ly
    for i, c in enumerate((uz, lz, ux, lx, uy, ly)):
        coef[i + 1] = c

    def unpack(a, _):
        zs[pl.ds(a * n, n), :] = packed_basis[a].astype(F32)
        return 0

    for i in range(pieces):
        copies[i].wait()
        lax.fori_loop(i * step, (i + 1) * step, unpack, 0, unroll=4)
    copies[pieces].wait()
    parts = [None, None]
    lane = lax.broadcasted_iota(jnp.int32, (size, d), 1)
    sides = jnp.zeros((size, d), F32)
    for row in range(n):
        z = zs[pl.ds(row, size, stride=n), :]
        zr[row] = z
        packed = z.astype(BF16)
        zm[:, row * d : (row + 1) * d] = packed
        layer, x = divmod(row, w)
        if x == w - 1:
            face_last[:, layer * d : (layer + 1) * d] = packed
        if x == 0:
            face_first[:, layer * d : (layer + 1) * d] = packed
        sides = jnp.where(lane == row, z[:, 0:1], sides)
        sides = jnp.where(lane == n + row, z[:, d - 1 : d], sides)
        term = z * rhs[row : row + 1, :]
        parts[row % 2] = term if parts[row % 2] is None else parts[row % 2] + term
    projected[...] = parts[0] + parts[1]
    face_y[...] = sides.astype(BF16)
    total = None
    for start in range(0, n, 8):
        for row in range(start, start + 8):
            z = zr[row]

            def c(i):
                return coef[i, row : row + 1, :]

            acc = c(0) * z
            if row + w < n:
                acc = acc - c(1) * zr[row + w]
            if row >= w:
                acc = acc - c(2) * zr[row - w]
            if row % w < w - 1:
                acc = acc - c(3) * zr[row + 1]
            if row % w > 0:
                acc = acc - c(4) * zr[row - 1]
            acc = acc - c(5) * pltpu.roll(z, d - 1, 1) - c(6) * pltpu.roll(z, 1, 1)
            at = slice(row * d, (row + 1) * d)
            hi, mid, lo = split3(acc)
            w3[0:size, at] = hi
            w3[size : 2 * size, at] = mid
            w3[2 * size : 3 * size, at] = lo
        part = dot_nt(w3[:, start * d : (start + 8) * d], zm[:, start * d : (start + 8) * d])
        total = part if total is None else total + part
    own[...] = fold3(total)


def k_setup(
    grid, pairs, cols, ids, cap, vent, cond, cond_low, cond_high, rec,
    zm, own_inner, projected, coef, own, inverse, sent, pay, w3, v0,
):
    n, d, w = grid.rows, grid.depth, grid.width
    count = rec.shape[0]
    vent_sum, low_x, high_x = received(grid, ids, pairs, rec)
    row_at, col_at = ids[pairs], ids[pairs + 1]
    low_x = jnp.where(row_at > 0, low_x, 0.0)
    high_x = jnp.where(row_at < count - 1, high_x, 0.0)
    low_y = jnp.where(col_at > 0, cond_low[0:n, :], 0.0)
    high_y = jnp.where(col_at < cols - 1, cond_high[0:n, :], 0.0)
    uz, lz, ux, lx, uy, ly = conductances(grid, cond[0:n, :], low_x, high_x, low_y, high_y)
    xi, lane, row = grid.masks()
    extra = (
        jnp.where(xi == w - 1, ux, 0.0)
        + jnp.where(xi == 0, lx, 0.0)
        + jnp.where(lane == d - 1, uy, 0.0)
        + jnp.where(lane == 0, ly, 0.0)
    )
    plenum = vent[...] * vent_sum
    extra = jnp.concatenate([extra[:-w], extra[-w:] + plenum], axis=0)
    diagonal = cap[...] + uz + lz + ux + lx + uy + ly
    coef[0] = jnp.concatenate([diagonal[:-w], diagonal[-w:] + plenum], axis=0)
    for i, c in enumerate((uz, lz, ux, lx, uy, ly)):
        coef[i + 1] = c
    block = own_inner[...] + gram(grid, zm, w3, extra)
    own[...] = block
    inverse[...] = invert_spd(block)
    y0 = solve_own(inverse, jnp.sum(projected[...], axis=1, keepdims=True))
    expand(grid, zm, y0, v0)
    field = v0[...]
    half = zm.shape[0] // 2
    folded = jnp.concatenate([inverse[0:half, :], inverse[half:, :]], axis=1)
    sent[0:n, :] = field
    sent[n:, :] = folded
    to_all(grid, pay, vent[...] * field[-w:], field, folded)


def incoming(grid, pairs, ids, rec, low, high):
    coupled, low_x, high_x = received(grid, ids, pairs, rec)
    n = grid.rows
    return coupled, low_x, high_x, low[0:n, :], high[0:n, :]


def k_coarse(grid, pairs, base, ids, coef, vent, zm, inverse, field, rec, low, high, *outs):
    if base:
        base_ref, out, pay, scratch = outs
    else:
        out, pay, scratch = outs
    beside = operate(grid, coef, vent[...], None, incoming(grid, pairs, ids, rec, low, high))
    expand(grid, zm, solve_own(inverse, project(grid, zm, beside)), scratch)
    result = field[0 : grid.rows, :] - scratch[...]
    if base:
        result = base_ref[...] - result
    out[...] = result
    to_all(grid, pay, vent[...] * result[-grid.width :], result)


def k_apply(grid, pairs, base, ids, coef, vent, field, rec, low, high, *outs):
    image = operate(grid, coef, vent[...], field[...], incoming(grid, pairs, ids, rec, low, high))
    if base:
        base_ref, out, pay = outs
        image = base_ref[...] - image
    else:
        out, pay = outs
    out[...] = image
    to_all(grid, pay, vent[...] * image[-grid.width :], image)


def k_partials(
    grid, pairs, base, pick, ids, coef, vent, field, rec, low, high, rec0, zm,
    next_first, prev_last, y_low, y_high, panels, *rest,
):
    rest = list(rest)
    base_ref = rest.pop(0) if base else None
    out, pay = rest[:2]
    n, d, w, layers = grid.rows, grid.depth, grid.width, grid.layers
    size = zm.shape[0]
    if pick:
        chosen, sems = rest[2:]
        copies = [
            pltpu.make_async_copy(panels.at[ids[k]], chosen.at[k], sems.at[k])
            for k in range(pairs)
        ]
        for copy in copies:
            copy.start()
    else:
        chosen = panels
    v = operate(grid, coef, vent[...], field[...], incoming(grid, pairs, ids, rec, low, high))
    if base:
        v = base_ref[...] - v
    out[...] = v
    face, zero = jnp.zeros((layers, d), F32), jnp.zeros((n, d), F32)
    own = operate(grid, coef, vent[...], v, (jnp.zeros((w, d), F32), face, face, zero, zero))

    def along(basis, weights):
        total = None
        for i, weight in enumerate(weights):
            term = basis[:, i * d : (i + 1) * d].astype(F32) * weight
            total = term if total is None else total + term
        return total

    even = along(zm, [own[i : i + 1] for i in range(n)])
    ux, lx, uy, ly = [coef[i] * v for i in (3, 4, 5, 6)]
    sums = [
        even,
        -along(next_first, [ux[z * w + w - 1 : z * w + w] for z in range(layers)]),
        -along(prev_last, [lx[z * w : z * w + 1] for z in range(layers)]),
    ]
    row = lax.broadcasted_iota(jnp.int32, (n, d), 0)
    lane = lax.broadcasted_iota(jnp.int32, (n, d), 1)
    up = jnp.sum(jnp.where(lane == row, uy[:, d - 1 : d], 0.0), axis=0, keepdims=True)
    down = jnp.sum(jnp.where(lane == n + row, ly[:, 0:1], 0.0), axis=0, keepdims=True)
    sums.append(-(y_high[...].astype(F32) * up))
    sums.append(-(y_low[...].astype(F32) * down))
    if pick:
        for copy in copies:
            copy.wait()
    top = vent[...] * v[-w:]
    for k in range(pairs):
        weight = rec0[ids[k], 0:w, :] * top
        sums.append(-along(chosen.at[k], [weight[i : i + 1] for i in range(w)]))
    ones = jnp.ones((8, d), F32)
    rows = [
        lax.dot_general(
            ones, q, (((1,), (1,)), ((), ())),
            precision=lax.Precision.HIGHEST, preferred_element_type=F32,
        )[0:1]
        for q in sums
    ]
    block = jnp.concatenate(rows + [jnp.zeros((8 - len(rows), size), F32)], axis=0)
    block = jnp.concatenate([block, jnp.zeros((8, d - size), F32)], axis=1)
    for slot in range(pay.shape[0]):
        pay[slot] = block


def k_combine(grid, table, rec, weights, zm, base, vent, out, pay, scratch):
    size = zm.shape[0]
    count = weights.shape[0]
    total = None
    for j in range(count):
        g = None
        for i in range(count):
            at = table[j * count + i]
            back = opposite(i)
            term = rec[jnp.maximum(at, 0), back : back + 1, :]
            term = jnp.where(at >= 0, term, 0.0)
            g = term if g is None else g + term
        term = weights[j] * g[:, 0:size]
        total = term if total is None else total + term
    expand(grid, zm, jnp.sum(total, axis=1, keepdims=True), scratch)
    result = base[...] - scratch[...]
    out[...] = result
    to_all(grid, pay, vent[...] * result[-grid.width :], result)


def k_dots(grid, pairs, ids, coef, vent, field, rec, low, high, r0, p0, i0, out, pay):
    image = operate(grid, coef, vent[...], field[...], incoming(grid, pairs, ids, rec, low, high))
    out[...] = image
    d, r, p, i = field[...], r0[...], p0[...], i0[...]
    products = (r * r, p * i, r * i, i * i, d * i, d * image)
    parts = [jnp.sum(q, axis=0, keepdims=True) for q in products]
    parts.append(jnp.zeros((8 - len(parts), grid.depth), F32))
    block = jnp.concatenate(parts, axis=0)
    for slot in range(pay.shape[0]):
        pay[slot] = block


def k_last(rec, x0, r0, p0, i0, d, image, x2, r2):
    total = rec[0]
    for slot in range(1, rec.shape[0]):
        total = total + rec[slot]
    sums = jnp.sum(total, axis=1, keepdims=True)
    rr, pi, ri, ii, di, dd = [sums[k : k + 1, :] for k in range(6)]
    a1 = rr / pi
    new = rr - 2.0 * a1 * ri + a1 * a1 * ii
    grow = 1.0 + new / rr
    a2 = new / (grow * grow * pi - 2.0 * grow * a1 * di + a1 * a1 * dd)
    x2[...] = x0[...] + (a1 + a2 * grow) * p0[...] - (a2 * a1) * d[...]
    r2[...] = r0[...] - (a1 + a2 * grow) * i0[...] + (a2 * a1) * image[...]


def k_blocks(
    grid, pairs, rows, cols, scale, ids, vent, coef, rec0, cond_low, cond_high, rec, low, high,
    panel, chosen, own, inverse, face_last, face_first, next_first, prev_last,
    face_y, y_low, y_high, _, out, weights, table, w3,
):
    n, d, w, layers = grid.rows, grid.depth, grid.width, grid.layers
    size = out.shape[1]
    row_at, col_at = ids[pairs], ids[pairs + 1]
    up, down = jnp.minimum(row_at + 1, rows - 1), jnp.maximum(row_at - 1, 0)

    lane = lax.broadcasted_iota(jnp.int32, (1, d), 1)

    def names(line):
        return [
            jnp.sum(jnp.where(lane == k, line, 0.0)).astype(jnp.int32) for k in range(pairs)
        ]

    line = w + 2 * layers

    def at_row(r):
        return names(rec0[r, line : line + 1, :])

    near = [
        (row_at, col_at, [ids[k] for k in range(pairs)]),
        (row_at + 1, col_at, at_row(up)),
        (row_at - 1, col_at, at_row(down)),
        (row_at, col_at + 1, names(cond_high[n : n + 1, :])),
        (row_at, col_at - 1, names(cond_low[n : n + 1, :])),
    ]
    near += [(ids[k], col_at, at_row(ids[k])) for k in range(pairs)]
    count = len(near)
    for j, (r, c, others) in enumerate(near):
        places = [(r, c), (r + 1, c), (r - 1, c), (r, c + 1), (r, c - 1)]
        places += [(q, c) for q in others]
        there = (r >= 0) & (r < rows) & (c >= 0) & (c < cols)
        for i, (pr, pc) in enumerate(places):
            good = there & (pr >= 0) & (pr < rows) & (pc >= 0) & (pc < cols)
            table[j * count + i] = jnp.where(good, pr * cols + pc, -1)

    def weighted(src, row_weights, other):
        m = len(row_weights)
        k = other.shape[1] // m
        for i, weight in enumerate(row_weights):
            at = slice(i * k, (i + 1) * k)
            hi, mid, lo = split3(src[:, at].astype(F32) * weight)
            w3[0:size, at] = hi
            w3[size : 2 * size, at] = mid
            w3[2 * size : 3 * size, at] = lo
        return -fold3(dot_nt(w3[:, : m * k], other))

    def dot(a, b):
        return lax.dot_general(
            a, b, (((1,), (0,)), ((), ())),
            precision=lax.Precision.HIGHEST, preferred_element_type=F32,
        )

    ux, lx, uy, ly = coef[3], coef[4], coef[5], coef[6]
    found = [
        weighted(
            face_last, [ux[z * w + w - 1 : z * w + w] for z in range(layers)], next_first[...]
        ),
        weighted(face_first, [lx[z * w : z * w + 1] for z in range(layers)], prev_last[...]),
    ]
    row = lax.broadcasted_iota(jnp.int32, (n, d), 0)
    wide = lax.broadcasted_iota(jnp.int32, (n, d), 1)
    high_weight = jnp.sum(jnp.where(wide == row, uy[:, d - 1 : d], 0.0), axis=0, keepdims=True)
    low_weight = jnp.sum(jnp.where(wide == n + row, ly[:, 0:1], 0.0), axis=0, keepdims=True)
    sides = face_y[...].astype(F32)
    swapped = pltpu.roll(sides, n, 1)
    found.append(weighted(swapped, [high_weight], y_high[...]))
    found.append(weighted(swapped, [low_weight], y_low[...]))
    top = vent[...]
    for k in range(pairs):
        weight = top * rec0[ids[k], 0:w, :]
        found.append(weighted(panel, [weight[i : i + 1] for i in range(w)], chosen[k]))

    for slot in range(rows):
        out[slot] = jnp.zeros((size, size), F32)
    out[row_at] = own[...] * scale
    out[up] = out[up] + jnp.where(row_at < rows - 1, found[0] * scale, 0.0)
    out[down] = out[down] + jnp.where(row_at > 0, found[1] * scale, 0.0)
    for k in range(pairs):
        out[ids[k]] = out[ids[k]] + found[4 + k] * scale

    half = size // 2
    first = w + 2 * layers

    def unfold(folded):
        return jnp.concatenate([folded[:, 0:size], folded[:, size:]], axis=0)

    theirs = [
        unfold(rec[up, first : first + half, :]),
        unfold(rec[down, first : first + half, :]),
        unfold(high[n : n + half, :]),
        unfold(low[n : n + half, :]),
    ]
    theirs += [unfold(rec[ids[k], first : first + half, :]) for k in range(pairs)]
    weights[0] = inverse[...]
    for j, (block, solve) in enumerate(zip(found, theirs)):
        weights[j + 1] = -dot(inverse[...], dot(block, solve))


def call(kernel, outs, operands, scratch=(), smem=0, hbm=(), smem_outs=(), cost=None):
    specs = [
        SMEM if i < smem else HBM if i in hbm else VMEM for i in range(len(operands))
    ]
    return pl.pallas_call(
        kernel,
        out_shape=tuple(jax.ShapeDtypeStruct(s, t) for s, t in outs),
        in_specs=specs,
        out_specs=tuple(SMEM if i in smem_outs else VMEM for i in range(len(outs))),
        scratch_shapes=list(scratch),
        compiler_params=pltpu.CompilerParams(vmem_limit_bytes=VMEM_LIMIT),
        cost_estimate=cost,
    )(*operands)


def body(forcing_right_hand, material, capacity, conductivity, vent_open, partners, subspace_basis):
    layers, width, depth = forcing_right_hand.shape
    size = subspace_basis.shape[0]
    grid = Grid(layers, width, depth)
    n, cells = grid.rows, forcing_right_hand.size
    row_count, col_count = lax.axis_size("row"), lax.axis_size("col")
    pairs = partners.shape[-1]
    ids = jnp.concatenate(
        [
            partners.reshape(-1),
            jnp.stack([lax.axis_index("row"), lax.axis_index("col")]).astype(jnp.int32),
        ]
    )
    rhs = forcing_right_hand.reshape(n, depth)
    classes = material.reshape(n, depth)
    basis = subspace_basis.reshape(size, n, depth)
    field = ((n, depth), F32)
    pay = ((row_count, width + 2 * layers, depth), F32)
    small = ((size, size), F32)

    def cyclic(value, axis, step):
        count = lax.axis_size(axis)
        return lax.ppermute(value, axis, [(i, (i + step) % count) for i in range(count)])

    def exchange(value, payload):
        low = cyclic(value, "col", 1)
        high = cyclic(value, "col", -1)
        rec = lax.all_to_all(payload, "row", 0, 0)
        return rec, low, high

    def rows_of(count):
        return ((row_count, width + 2 * layers + count, depth), F32)

    cond, cap, vent, pay0 = call(
        functools.partial(k_first, grid),
        (((n + 8, depth), F32), field, ((width, depth), F32), rows_of(8)),
        (classes, conductivity, capacity, vent_open, partners.reshape(-1)),
        scratch=(
            pltpu.VMEM((n, depth), jnp.int32),
            pltpu.SMEM(conductivity.shape, F32),
            pltpu.SMEM(capacity.shape, F32),
            pltpu.SMEM((pairs,), jnp.int32),
            pltpu.SemaphoreType.DMA((5,)),
        ),
        hbm=(0, 1, 2, 3, 4),
    )
    rec0, cond_low, cond_high = exchange(cond, pay0)
    (panel,) = call(
        functools.partial(k_panel, grid),
        (((size, width * depth), BF16),),
        (basis, cond),
        scratch=(
            pltpu.VMEM((size, width, depth), BF16),
            pltpu.VMEM((size * width, depth), F32),
            pltpu.SemaphoreType.DMA,
        ),
        hbm=(0, 1),
    )
    panels = lax.all_gather(panel, "row", axis=0)

    zm, own_inner, projected, face_last, face_first, face_y, rhs = call(
        functools.partial(k_basis, grid),
        (
            ((size, n * depth), BF16),
            small,
            ((size, depth), F32),
            ((size, layers * depth), BF16),
            ((size, layers * depth), BF16),
            ((size, depth), BF16),
            field,
        ),
        (basis, rhs, cond, cap),
        scratch=(
            pltpu.VMEM((size * n, depth), F32),
            pltpu.VMEM((n, size, depth), F32),
            pltpu.VMEM((3 * size, n * depth), BF16),
            pltpu.VMEM((7, n, depth), F32),
            pltpu.VMEM((size, n, depth), BF16),
            pltpu.SemaphoreType.DMA((5,)),
        ),
        hbm=(0, 1),
        cost=pl.CostEstimate(flops=200_000_000, bytes_accessed=8_000_000, transcendentals=0),
    )

    coef, own, inverse, sent, pay1 = call(
        functools.partial(k_setup, grid, pairs, col_count),
        (((7, n, depth), F32), small, small, ((n + size // 2, depth), F32), rows_of(size // 2)),
        (ids, cap, vent, cond, cond_low, cond_high, rec0, zm, own_inner, projected),
        scratch=(
            pltpu.VMEM((3 * size, n * depth), BF16),
            pltpu.VMEM((n, depth), F32),
        ),
        smem=1,
    )
    rec1, low1, high1 = exchange(sent, pay1)
    face_last_, face_first_, face_y_, _ = lax.optimization_barrier(
        (face_last, face_first, face_y, pay1)
    )
    prev_last = cyclic(face_last_, "row", 1)
    next_first = cyclic(face_first_, "row", -1)
    y_low = cyclic(face_y_, "col", 1)
    y_high = cyclic(face_y_, "col", -1)
    x0, pay2 = call(
        functools.partial(k_coarse, grid, pairs, False),
        (field, pay),
        (ids, coef, vent, zm, inverse, sent, rec1, low1, high1),
        scratch=(pltpu.VMEM((n, depth), F32),),
        smem=1,
    )
    rec, low, high = exchange(x0, pay2)
    everyone = ((row_count * col_count, 8, depth), F32)
    r0, pay3, chosen = call(
        functools.partial(k_partials, grid, pairs, True, True),
        (field, everyone, ((pairs, size, width * depth), BF16)),
        (
            ids, coef, vent, x0, rec, low, high, rec0, zm, next_first, prev_last, y_low, y_high,
            panels, rhs,
        ),
        scratch=(pltpu.SemaphoreType.DMA((pairs,)),),
        smem=1,
        hbm=(13,),
    )
    places = 5 + pairs
    blocks, weights, table = call(
        functools.partial(k_blocks, grid, pairs, row_count, col_count, 1.0 / cells),
        (
            ((row_count, size, size), F32),
            ((places, size, size), F32),
            ((places * places,), jnp.int32),
        ),
        (
            ids, vent, coef, rec0, cond_low, cond_high, rec1, low1, high1, panel, chosen, own,
            inverse, face_last, face_first, next_first, prev_last, face_y, y_low, y_high, pay3,
        ),
        scratch=(pltpu.VMEM((3 * size, width * depth), BF16),),
        smem=1,
        hbm=(20,),
        smem_outs=(2,),
        cost=pl.CostEstimate(flops=100_000_000, bytes_accessed=4_000_000, transcendentals=0),
    )
    sums = lax.all_to_all(pay3, ("row", "col"), 0, 0)
    p0, pay4 = call(
        functools.partial(k_combine, grid),
        (field, pay),
        (table, sums, weights, zm, r0, vent),
        scratch=(pltpu.VMEM((n, depth), F32),),
        smem=1,
    )
    rec, low, high = exchange(p0, pay4)
    i0, pay5 = call(
        functools.partial(k_partials, grid, pairs, False, False),
        (field, everyone),
        (
            ids, coef, vent, p0, rec, low, high, rec0, zm, next_first, prev_last, y_low, y_high,
            chosen,
        ),
        smem=1,
    )
    sums = lax.all_to_all(pay5, ("row", "col"), 0, 0)
    d0, pay6 = call(
        functools.partial(k_combine, grid),
        (field, pay),
        (table, sums, weights, zm, i0, vent),
        scratch=(pltpu.VMEM((n, depth), F32),),
        smem=1,
    )
    rec, low, high = exchange(d0, pay6)
    image, pay7 = call(
        functools.partial(k_dots, grid, pairs),
        (field, everyone),
        (ids, coef, vent, d0, rec, low, high, r0, p0, i0),
        smem=1,
    )
    total = lax.all_to_all(pay7, ("row", "col"), 0, 0)
    x2, r2 = call(k_last, (field, field), (total, x0, r0, p0, i0, d0, image))
    shape = forcing_right_hand.shape
    return x2.reshape(shape), r2.reshape(shape), blocks[None, None]


def solution(mesh):
    return jax.shard_map(
        body,
        mesh=mesh,
        in_specs=(
            P(None, "row", "col"),
            P(None, "row", "col"),
            P(),
            P(),
            P("row", "col"),
            P("row", "col", None),
            P(None, None, "row", "col"),
        ),
        out_specs=(P(None, "row", "col"), P(None, "row", "col"), P("row", "col", None, None, None)),
        check_vma=False,
    )
```

```python
import functools

import jax
import jax.numpy as jnp
from jax import lax
from jax.experimental import pallas as pl
from jax.experimental.pallas import tpu as pltpu
from jax.sharding import PartitionSpec as P

F32 = jnp.float32
BF16 = jnp.bfloat16
VMEM = pl.BlockSpec(memory_space=pltpu.VMEM)
SMEM = pl.BlockSpec(memory_space=pltpu.SMEM)
ANY = pl.BlockSpec(memory_space=pl.ANY)
VMEM_LIMIT = 16 * 1024 * 1024


def harmonic(a, b):
    return 2.0 * a * b / (a + b)


def lookup(material, table):
    result = jnp.zeros(material.shape, F32)
    for class_id in range(table.shape[0]):
        result = jnp.where(material == class_id, table[class_id], result)
    return result


class Grid:
    def __init__(self, layers, width, depth):
        self.layers, self.width, self.depth = layers, width, depth
        self.rows = layers * width

    def masks(self):
        shape = (self.rows, self.depth)
        row = lax.broadcasted_iota(jnp.int32, shape, 0)
        lane = lax.broadcasted_iota(jnp.int32, shape, 1)
        return lax.rem(row, self.width), lane, row

    def spread(self, face):
        parts = [
            jnp.broadcast_to(face[z : z + 1], (self.width, self.depth)) for z in range(self.layers)
        ]
        return jnp.concatenate(parts, axis=0)

    def faces(self, v):
        w = self.width
        last = [v[z * w + w - 1 : z * w + w] for z in range(self.layers)]
        first = [v[z * w : z * w + 1] for z in range(self.layers)]
        return last + first

    def payload(self, top, v):
        return jnp.concatenate([top] + self.faces(v), axis=0)

    def around(self, v, low_x, high_x, low_y, high_y):
        xi, lane, _ = self.masks()
        n, d = self.rows, self.depth
        zero = jnp.zeros((n, d), F32)
        own = zero if v is None else v
        plus = zero if v is None else pltpu.roll(v, n - 1, 0)
        minus = zero if v is None else pltpu.roll(v, 1, 0)
        up_x = jnp.where(xi == self.width - 1, self.spread(high_x), plus)
        down_x = jnp.where(xi == 0, self.spread(low_x), minus)
        up_y = pltpu.roll(jnp.where(lane == 0, high_y, own), d - 1, 1)
        down_y = pltpu.roll(jnp.where(lane == d - 1, low_y, own), 1, 1)
        return up_x, down_x, up_y, down_y

    def shifted_z(self, v):
        w = self.width
        return jnp.concatenate([v[w:], v[:w]], axis=0), jnp.concatenate([v[-w:], v[:-w]], axis=0)


def received(grid, ids, pairs, rec):
    count = rec.shape[0]
    w, layers = grid.width, grid.layers
    coupled = rec[ids[0], 0:w, :]
    for k in range(1, pairs):
        coupled = coupled + rec[ids[k], 0:w, :]
    row_at = ids[pairs]
    low = rec[jnp.maximum(row_at - 1, 0), w : w + layers, :]
    high = rec[jnp.minimum(row_at + 1, count - 1), w + layers : w + 2 * layers, :]
    return coupled, low, high


def operate(grid, coef, vent, v, rest):
    coupled, low_x, high_x, low_y, high_y = rest
    up_x, down_x, up_y, down_y = grid.around(v, low_x, high_x, low_y, high_y)
    beside = coef[3] * up_x + coef[4] * down_x + coef[5] * up_y + coef[6] * down_y
    if v is None:
        xi, lane, _ = grid.masks()
        result = -beside
    else:
        up_z, down_z = grid.shifted_z(v)
        result = coef[0] * v - (beside + coef[1] * up_z + coef[2] * down_z)
    w = grid.width
    return jnp.concatenate([result[:-w], result[-w:] - vent * coupled], axis=0)


def project(grid, zm, v):
    d = grid.depth
    parts = [None, None]
    for row in range(grid.rows):
        term = zm[:, row * d : (row + 1) * d].astype(F32) * v[row : row + 1, :]
        k = row % 2
        parts[k] = term if parts[k] is None else parts[k] + term
    return jnp.sum(parts[0] + parts[1], axis=1, keepdims=True)


def solve_own(inverse, column):
    size = inverse.shape[0]
    along = jnp.sum(inverse[...] * column, axis=0, keepdims=True)
    eye = lax.broadcasted_iota(jnp.int32, (size, size), 0) == lax.broadcasted_iota(
        jnp.int32, (size, size), 1
    )
    return jnp.sum(jnp.where(eye, along, 0.0), axis=1, keepdims=True)


def expand(grid, zm, column, out):
    d = grid.depth
    wide = jnp.broadcast_to(column, (column.shape[0], d))
    for row in range(grid.rows):
        out[row : row + 1, :] = jnp.sum(
            zm[:, row * d : (row + 1) * d].astype(F32) * wide, axis=0, keepdims=True
        )


def to_all(grid, pay, top, v, *more):
    block = jnp.concatenate([grid.payload(top, v), *more], axis=0)
    for slot in range(pay.shape[0]):
        pay[slot] = block


def split3(w):
    hi = w.astype(BF16)
    rest = w - hi.astype(F32)
    mid = rest.astype(BF16)
    lo = (rest - mid.astype(F32)).astype(BF16)
    return hi, mid, lo


def dot_nt(a, b):
    return lax.dot_general(a, b, (((1,), (1,)), ((), ())), preferred_element_type=F32)


def fold3(stacked):
    size = stacked.shape[0] // 3
    return stacked[:size] + (stacked[size : 2 * size] + stacked[2 * size :])


def gram(grid, zm, w3, weights, first_row=0):
    d = grid.depth
    size = zm.shape[0]
    total = None
    group = 8
    rows = weights.shape[0]
    for start in range(0, rows, group):
        stop = min(start + group, rows)
        for row in range(start, stop):
            at = slice(row * d, (row + 1) * d)
            src = slice((first_row + row) * d, (first_row + row + 1) * d)
            hi, mid, lo = split3(zm[:, src].astype(F32) * weights[row : row + 1, :])
            w3[0:size, at] = hi
            w3[size : 2 * size, at] = mid
            w3[2 * size : 3 * size, at] = lo
        part = dot_nt(
            w3[:, start * d : stop * d],
            zm[:, (first_row + start) * d : (first_row + stop) * d],
        )
        total = part if total is None else total + part
    return fold3(total)


def invert_spd(m, ahead=5):
    size = m.shape[0]
    row_id = lax.broadcasted_iota(jnp.int32, (size, size), 0)
    col_id = lax.broadcasted_iota(jnp.int32, (size, size), 1)

    def column(k):
        return jnp.broadcast_to(m[:, k : k + 1], (size, size))

    waiting = {k: column(k) for k in range(min(ahead + 1, size))}
    for k in range(size):
        col = waiting.pop(k)
        inv = 1.0 / col[k : k + 1, :]
        for j in list(waiting):
            at_row = col[j : j + 1, :] * inv
            waiting[j] = jnp.where(row_id == k, at_row, waiting[j] - col * at_row)
        scaled_row = jnp.where(col_id[:1] == k, -inv, m[k : k + 1, :] * inv)
        m = jnp.where(row_id == k, scaled_row, jnp.where(col_id == k, 0.0, m) - col * scaled_row)
        if k + ahead + 1 < size:
            waiting[k + ahead + 1] = column(k + ahead + 1)
    return -m


def opposite(place):
    return {1: 2, 2: 1, 3: 4, 4: 3}.get(place, place)


def k_first(
    grid, material, conductivity, capacity, vent, partners, cond_out, cap_out, vent_out, pay,
    classes, cond_table, cap_table, pair_table, sems,
):
    copies = [
        pltpu.make_async_copy(src, dst, sems.at[i])
        for i, (src, dst) in enumerate(
            (
                (material, classes),
                (conductivity, cond_table),
                (capacity, cap_table),
                (vent, vent_out),
                (partners, pair_table),
            )
        )
    ]
    for copy in copies:
        copy.start()
    for copy in copies:
        copy.wait()
    cond = lookup(classes[...], cond_table)
    lane = lax.broadcasted_iota(jnp.int32, (8, grid.depth), 1)
    names = jnp.zeros((8, grid.depth), F32)
    for k in range(pair_table.shape[0]):
        names = jnp.where(lane == k, pair_table[k].astype(F32), names)
    cond_out[0 : grid.rows, :] = cond
    cond_out[grid.rows :, :] = names
    cap_out[...] = lookup(classes[...], cap_table)
    to_all(grid, pay, vent_out[...], cond, names)


def conductances(grid, cond, low_x, high_x, low_y, high_y):
    _, _, row = grid.masks()
    up_z, down_z = grid.shifted_z(cond)
    uz = jnp.where(row < grid.rows - grid.width, harmonic(cond, up_z), 0.0)
    lz = jnp.where(row >= grid.width, harmonic(cond, down_z), 0.0)
    ux, lx, uy, ly = [harmonic(cond, c) for c in grid.around(cond, low_x, high_x, low_y, high_y)]
    return uz, lz, ux, lx, uy, ly


def k_order(grid, basis, zm, panel, faces, wide):
    n, d, w, layers = grid.rows, grid.depth, grid.width, grid.layers
    size = basis.shape[0]

    def unpack(a, _):
        wide[pl.ds(a * n, n), :] = basis[a].astype(F32)
        return 0

    lax.fori_loop(0, size, unpack, 0, unroll=4)
    for row in range(n):
        packed = wide[pl.ds(row, size, stride=n), :].astype(BF16)
        zm[:, row * d : (row + 1) * d] = packed
        layer, x = divmod(row, w)
        if layer == layers - 1:
            panel[:, x * d : (x + 1) * d] = packed
        if x == 0:
            faces[:, layer * d : (layer + 1) * d] = packed
        if x == w - 1:
            faces[:, (layers + layer) * d : (layers + layer + 1) * d] = packed


def k_basis(grid, zm, rhs, cond_ref, cap_ref, own, projected, face_y, zr, w3, coef):
    n, d, w = grid.rows, grid.depth, grid.width
    size = zm.shape[0]
    cond = cond_ref[0:n, :]
    zero_face = jnp.zeros((grid.layers, d), F32)
    zero = jnp.zeros((n, d), F32)
    uz, lz, ux, lx, uy, ly = conductances(grid, cond, zero_face, zero_face, zero, zero)
    coef[0] = cap_ref[...] + uz + lz + ux + lx + uy + ly
    for i, c in enumerate((uz, lz, ux, lx, uy, ly)):
        coef[i + 1] = c

    parts = [None, None]
    lane = lax.broadcasted_iota(jnp.int32, (size, d), 1)
    sides = jnp.zeros((size, d), F32)
    for row in range(n):
        z = zm[:, row * d : (row + 1) * d].astype(F32)
        zr[row] = z
        sides = jnp.where(lane == row, z[:, 0:1], sides)
        sides = jnp.where(lane == n + row, z[:, d - 1 : d], sides)
        term = z * rhs[row : row + 1, :]
        parts[row % 2] = term if parts[row % 2] is None else parts[row % 2] + term
    projected[...] = parts[0] + parts[1]
    face_y[...] = sides
    total = None
    for start in range(0, n, 8):
        for row in range(start, start + 8):
            z = zr[row]

            def c(i):
                return coef[i, row : row + 1, :]

            acc = c(0) * z
            if row + w < n:
                acc = acc - c(1) * zr[row + w]
            if row >= w:
                acc = acc - c(2) * zr[row - w]
            if row % w < w - 1:
                acc = acc - c(3) * zr[row + 1]
            if row % w > 0:
                acc = acc - c(4) * zr[row - 1]
            acc = acc - c(5) * pltpu.roll(z, d - 1, 1) - c(6) * pltpu.roll(z, 1, 1)
            at = slice(row * d, (row + 1) * d)
            hi, mid, lo = split3(acc)
            w3[0:size, at] = hi
            w3[size : 2 * size, at] = mid
            w3[2 * size : 3 * size, at] = lo
        part = dot_nt(w3[:, start * d : (start + 8) * d], zm[:, start * d : (start + 8) * d])
        total = part if total is None else total + part
    own[...] = fold3(total)


def k_setup(
    grid, pairs, cols, ids, cap, vent, cond, cond_low, cond_high, rec,
    zm, own_inner, projected, face_y, faces, *rest,
):
    held = rest[:-12]
    coef, own, inverse, sent, pay, mine, wanted, vents, names, w3, v0, sems = rest[-12:]
    n, d, w, layers = grid.rows, grid.depth, grid.width, grid.layers
    count = rec.shape[0]
    panel = w * d
    line = w + 2 * layers
    sibling = lax.bitwise_xor(ids[pairs], 1)
    names_lane = lax.broadcasted_iota(jnp.int32, (1, d), 1)
    targets = []
    for k in range(pairs):
        theirs = jnp.where(names_lane == k, rec[sibling, line : line + 1, :], 0.0)
        targets += [
            (ids[k], mine.at[k]),
            (jnp.sum(theirs).astype(jnp.int32), wanted.at[:, pl.ds(k * panel, panel)]),
        ]
    for i, (partner, target) in enumerate(targets):
        index = lax.shift_right_logical(lax.bitwise_xor(partner, ids[pairs]), 1)
        for j, source in enumerate(held):

            @pl.when(index == j)
            def _(source=source, target=target, i=i):
                pltpu.make_async_copy(source, target, sems.at[i]).start()

    half = layers * d
    upward = lax.bitwise_and(ids[pairs], 1) == 0
    wanted[:, pairs * panel :] = jnp.where(upward, faces[:, half:], faces[:, :half])
    for k in range(pairs):
        vents[k] = vent[...] * rec[ids[k], 0:w, :]
    up, down = jnp.minimum(ids[pairs] + 1, count - 1), jnp.maximum(ids[pairs] - 1, 0)
    lines = [rec[r, line : line + 1, :] for r in (up, down)]
    lines += [cond_high[n : n + 1, :], cond_low[n : n + 1, :]]
    lines += [rec[ids[k], line : line + 1, :] for k in range(pairs)]
    names[...] = jnp.concatenate(lines, axis=0)
    vent_sum, low_x, high_x = received(grid, ids, pairs, rec)
    row_at, col_at = ids[pairs], ids[pairs + 1]
    low_x = jnp.where(row_at > 0, low_x, 0.0)
    high_x = jnp.where(row_at < count - 1, high_x, 0.0)
    low_y = jnp.where(col_at > 0, cond_low[0:n, :], 0.0)
    high_y = jnp.where(col_at < cols - 1, cond_high[0:n, :], 0.0)
    uz, lz, ux, lx, uy, ly = conductances(grid, cond[0:n, :], low_x, high_x, low_y, high_y)
    xi, lane, row = grid.masks()
    extra = (
        jnp.where(xi == w - 1, ux, 0.0)
        + jnp.where(xi == 0, lx, 0.0)
        + jnp.where(lane == d - 1, uy, 0.0)
        + jnp.where(lane == 0, ly, 0.0)
    )
    plenum = vent[...] * vent_sum
    extra = jnp.concatenate([extra[:-w], extra[-w:] + plenum], axis=0)
    diagonal = cap[...] + uz + lz + ux + lx + uy + ly
    coef[0] = jnp.concatenate([diagonal[:-w], diagonal[-w:] + plenum], axis=0)
    for i, c in enumerate((uz, lz, ux, lx, uy, ly)):
        coef[i + 1] = c
    block = own_inner[...] + gram(grid, zm, w3, extra)
    own[...] = block
    inverse[...] = invert_spd(block)
    y0 = solve_own(inverse, jnp.sum(projected[...], axis=1, keepdims=True))
    expand(grid, zm, y0, v0)
    field = v0[...]
    half = zm.shape[0] // 2
    folded = jnp.concatenate([inverse[0:half, :], inverse[half:, :]], axis=1)
    sent[0:n, :] = field
    sent[n : n + half, :] = folded
    sent[n + half :, :] = face_y[...]
    to_all(grid, pay, vent[...] * field[-w:], field, folded)
    for i, (_, target) in enumerate(targets):
        pltpu.make_async_copy(held[0], target, sems.at[i]).wait()


def incoming(grid, pairs, ids, rec, low, high):
    coupled, low_x, high_x = received(grid, ids, pairs, rec)
    n = grid.rows
    return coupled, low_x, high_x, low[0:n, :], high[0:n, :]


def k_coarse(
    grid, pairs, ids, coef, vent, zm, inverse, field, rec, low, high, out, pay, solves, y_faces, scratch
):
    n, w = grid.rows, grid.width
    beside = operate(grid, coef, vent[...], None, incoming(grid, pairs, ids, rec, low, high))
    expand(grid, zm, solve_own(inverse, project(grid, zm, beside)), scratch)
    result = field[0:n, :] - scratch[...]
    out[...] = result
    to_all(grid, pay, vent[...] * result[-w:], result)
    half = solves.shape[1]
    first = w + 2 * grid.layers
    row_at = ids[pairs]
    solves[0] = rec[jnp.minimum(row_at + 1, rec.shape[0] - 1), first : first + half, :]
    solves[1] = rec[jnp.maximum(row_at - 1, 0), first : first + half, :]
    solves[2] = high[n : n + half, :]
    solves[3] = low[n : n + half, :]
    for k in range(pairs):
        solves[4 + k] = rec[ids[k], first : first + half, :]
    y_faces[0] = high[n + half :, :]
    y_faces[1] = low[n + half :, :]


def chosen(grid, pairs, ids, mine, others, k, at):
    panel = grid.width * grid.depth
    same = lax.bitwise_and(lax.bitwise_xor(ids[k], ids[pairs]), 1) == 0
    there = slice(k * panel + at.start, k * panel + at.stop)
    return jnp.where(same, mine[k, :, at].astype(F32), others[:, there].astype(F32))


def x_faces(grid, pairs, ids, others, far):
    half = grid.layers * grid.depth
    near = others[:, pairs * grid.width * grid.depth :].astype(F32)
    upward = lax.bitwise_and(ids[pairs], 1) == 0
    return (
        jnp.where(upward, near, far[:, :half].astype(F32)),
        jnp.where(upward, far[:, half:].astype(F32), near),
    )


def k_partials(
    grid, pairs, base, ids, coef, vent, field, rec, low, high, vents, zm,
    far, y_faces, mine, others, *rest,
):
    base_ref = rest[0] if base else None
    out, pay = rest[-2:]
    n, d, w, layers = grid.rows, grid.depth, grid.width, grid.layers
    size = zm.shape[0]
    v = operate(grid, coef, vent[...], field[...], incoming(grid, pairs, ids, rec, low, high))
    if base:
        v = base_ref[...] - v
    out[...] = v
    face, zero = jnp.zeros((layers, d), F32), jnp.zeros((n, d), F32)
    own = operate(grid, coef, vent[...], v, (jnp.zeros((w, d), F32), face, face, zero, zero))

    def along(basis, weights):
        total = None
        for i, weight in enumerate(weights):
            term = basis[:, i * d : (i + 1) * d].astype(F32) * weight
            total = term if total is None else total + term
        return total

    even = along(zm, [own[i : i + 1] for i in range(n)])
    ux, lx, uy, ly = [coef[i] * v for i in (3, 4, 5, 6)]
    next_first, prev_last = x_faces(grid, pairs, ids, others, far)
    sums = [
        even,
        -along(next_first, [ux[z * w + w - 1 : z * w + w] for z in range(layers)]),
        -along(prev_last, [lx[z * w : z * w + 1] for z in range(layers)]),
    ]
    row = lax.broadcasted_iota(jnp.int32, (n, d), 0)
    lane = lax.broadcasted_iota(jnp.int32, (n, d), 1)
    up = jnp.sum(jnp.where(lane == row, uy[:, d - 1 : d], 0.0), axis=0, keepdims=True)
    down = jnp.sum(jnp.where(lane == n + row, ly[:, 0:1], 0.0), axis=0, keepdims=True)
    sums.append(-(y_faces[0] * up))
    sums.append(-(y_faces[1] * down))
    top = v[-w:]
    for k in range(pairs):
        weight = vents[k] * top
        total = None
        for x in range(w):
            at = slice(x * d, (x + 1) * d)
            term = chosen(grid, pairs, ids, mine, others, k, at) * weight[x : x + 1]
            total = term if total is None else total + term
        sums.append(-total)
    ones = jnp.ones((8, d), F32)
    rows = [
        lax.dot_general(
            ones, q, (((1,), (1,)), ((), ())),
            precision=lax.Precision.HIGHEST, preferred_element_type=F32,
        )[0:1]
        for q in sums
    ]
    if len(rows) % 2:
        rows.append(jnp.zeros((1, size), F32))
    block = jnp.concatenate(
        [jnp.concatenate(rows[i : i + 2], axis=1) for i in range(0, len(rows), 2)], axis=0
    )
    for slot in range(pay.shape[0]):
        pay[slot] = block


def k_combine(grid, table, rec, weights, zm, base, vent, out, pay, scratch):
    size = zm.shape[0]
    count = weights.shape[0]
    total = None
    for j in range(count):
        sides = [None, None]
        for i in range(count):
            at = table[j * count + i]
            line, side = divmod(opposite(i), 2)
            term = rec[jnp.maximum(at, 0), line : line + 1, :]
            term = jnp.where(at >= 0, term, 0.0)
            sides[side] = term if sides[side] is None else sides[side] + term
        term = weights[j] * (sides[0][:, 0:size] + sides[1][:, size : 2 * size])
        total = term if total is None else total + term
    expand(grid, zm, jnp.sum(total, axis=1, keepdims=True), scratch)
    result = base[...] - scratch[...]
    out[...] = result
    to_all(grid, pay, vent[...] * result[-grid.width :], result)


def k_dots(grid, pairs, ids, coef, vent, field, rec, low, high, r0, p0, i0, out, pay):
    image = operate(grid, coef, vent[...], field[...], incoming(grid, pairs, ids, rec, low, high))
    out[...] = image
    d, r, p, i = field[...], r0[...], p0[...], i0[...]
    products = (r * r, p * i, r * i, i * i, d * i, d * image)
    lane = lax.broadcasted_iota(jnp.int32, pay.shape[1:], 1)
    block = jnp.zeros(pay.shape[1:], F32)
    for k, q in enumerate(products):
        total = jnp.sum(jnp.sum(q, axis=0, keepdims=True), axis=1, keepdims=True)
        block = jnp.where(lane == k, total, block)
    for slot in range(pay.shape[0]):
        pay[slot] = block


def k_last(rec, x0, r0, p0, i0, d, image, x2, r2):
    total = rec[0]
    for slot in range(1, rec.shape[0]):
        total = total + rec[slot]
    rr, pi, ri, ii, di, dd = [total[0:1, k : k + 1] for k in range(6)]
    a1 = rr / pi
    new = rr - 2.0 * a1 * ri + a1 * a1 * ii
    grow = 1.0 + new / rr
    a2 = new / (grow * grow * pi - 2.0 * grow * a1 * di + a1 * a1 * dd)
    x2[...] = x0[...] + (a1 + a2 * grow) * p0[...] - (a2 * a1) * d[...]
    r2[...] = r0[...] - (a1 + a2 * grow) * i0[...] + (a2 * a1) * image[...]


def k_blocks(
    grid, pairs, cols, scale, ids, coef, vents, names, zm, mine, others, own, inverse, far,
    face_y, y_faces, solves, _, out, weights, table, w3,
):
    n, d, w, layers = grid.rows, grid.depth, grid.width, grid.layers
    rows, size = out.shape[0], out.shape[1]
    row_at = ids[pairs]
    up, down = jnp.minimum(row_at + 1, rows - 1), jnp.maximum(row_at - 1, 0)

    col_at = ids[pairs + 1]
    lane = lax.broadcasted_iota(jnp.int32, (1, d), 1)
    near = [(row_at, col_at), (row_at + 1, col_at), (row_at - 1, col_at)]
    near += [(row_at, col_at + 1), (row_at, col_at - 1)]
    near += [(ids[k], col_at) for k in range(pairs)]
    count = len(near)
    for j, (r, c) in enumerate(near):
        places = [(r, c), (r + 1, c), (r - 1, c), (r, c + 1), (r, c - 1)]
        for k in range(pairs):
            met = ids[k]
            if j > 0:
                met = jnp.sum(jnp.where(lane == k, names[j - 1 : j, :], 0.0)).astype(jnp.int32)
            places.append((met, c))
        there = (r >= 0) & (r < rows) & (c >= 0) & (c < cols)
        for i, (pr, pc) in enumerate(places):
            good = there & (pr >= 0) & (pr < rows) & (pc >= 0) & (pc < cols)
            table[j * count + i] = jnp.where(good, pr * cols + pc, -1)

    def weighted(parts, row_weights, other):
        m = len(row_weights)
        k = other.shape[1] // m
        for i, (part, weight) in enumerate(zip(parts, row_weights)):
            at = slice(i * k, (i + 1) * k)
            hi, mid, lo = split3(part.astype(F32) * weight)
            w3[0:size, at] = hi
            w3[size : 2 * size, at] = mid
            w3[2 * size : 3 * size, at] = lo
        return -fold3(dot_nt(w3[:, : m * k], other))

    def dot(a, b):
        return lax.dot_general(
            a, b, (((1,), (0,)), ((), ())),
            precision=lax.Precision.HIGHEST, preferred_element_type=F32,
        )

    ux, lx, uy, ly = coef[3], coef[4], coef[5], coef[6]
    last = [z * w + w - 1 for z in range(layers)]
    first = [z * w for z in range(layers)]

    def basis_rows(at):
        return [zm[:, i * d : (i + 1) * d] for i in at]

    next_first, prev_last = x_faces(grid, pairs, ids, others, far)
    found = [
        weighted(basis_rows(last), [ux[i : i + 1] for i in last], next_first.astype(BF16)),
        weighted(basis_rows(first), [lx[i : i + 1] for i in first], prev_last.astype(BF16)),
    ]
    row = lax.broadcasted_iota(jnp.int32, (n, d), 0)
    wide = lax.broadcasted_iota(jnp.int32, (n, d), 1)
    high_weight = jnp.sum(jnp.where(wide == row, uy[:, d - 1 : d], 0.0), axis=0, keepdims=True)
    low_weight = jnp.sum(jnp.where(wide == n + row, ly[:, 0:1], 0.0), axis=0, keepdims=True)
    swapped = pltpu.roll(face_y[...], n, 1)
    found.append(weighted([swapped], [high_weight], y_faces[0].astype(BF16)))
    found.append(weighted([swapped], [low_weight], y_faces[1].astype(BF16)))
    top = basis_rows(range(n - w, n))
    for k in range(pairs):
        panel = chosen(grid, pairs, ids, mine, others, k, slice(0, w * d)).astype(BF16)
        found.append(weighted(top, [vents[k, i : i + 1, :] for i in range(w)], panel))

    for slot in range(rows):
        out[slot] = jnp.zeros((size, size), F32)
    out[row_at] = own[...] * scale
    out[up] = out[up] + jnp.where(row_at < rows - 1, found[0] * scale, 0.0)
    out[down] = out[down] + jnp.where(row_at > 0, found[1] * scale, 0.0)
    for k in range(pairs):
        out[ids[k]] = out[ids[k]] + found[4 + k] * scale

    weights[0] = inverse[...]
    for j, block in enumerate(found):
        theirs = jnp.concatenate([solves[j, :, 0:size], solves[j, :, size:]], axis=0)
        weights[j + 1] = -dot(inverse[...], dot(block, theirs))


def call(kernel, outs, operands, scratch=(), smem=0, free=(), smem_outs=(), cost=None):
    specs = [
        SMEM if i < smem else ANY if i in free else VMEM for i in range(len(operands))
    ]
    return pl.pallas_call(
        kernel,
        out_shape=tuple(jax.ShapeDtypeStruct(s, t) for s, t in outs),
        in_specs=specs,
        out_specs=tuple(SMEM if i in smem_outs else VMEM for i in range(len(outs))),
        scratch_shapes=list(scratch),
        compiler_params=pltpu.CompilerParams(vmem_limit_bytes=VMEM_LIMIT),
        cost_estimate=cost,
    )(*operands)


def body(forcing_right_hand, material, capacity, conductivity, vent_open, partners, subspace_basis):
    layers, width, depth = forcing_right_hand.shape
    size = subspace_basis.shape[0]
    grid = Grid(layers, width, depth)
    n, cells = grid.rows, forcing_right_hand.size
    row_count, col_count = lax.axis_size("row"), lax.axis_size("col")
    pairs = partners.shape[-1]
    ids = jnp.concatenate(
        [
            partners.reshape(-1),
            jnp.stack([lax.axis_index("row"), lax.axis_index("col")]).astype(jnp.int32),
        ]
    )
    rhs = forcing_right_hand.reshape(n, depth)
    classes = material.reshape(n, depth)
    basis = subspace_basis.reshape(size, n, depth)
    field = ((n, depth), F32)
    pay = ((row_count, width + 2 * layers, depth), F32)
    small = ((size, size), F32)

    def cyclic(value, axis, step):
        count = lax.axis_size(axis)
        return lax.ppermute(value, axis, [(i, (i + step) % count) for i in range(count)])

    def xor_step(value, axis, k):
        count = lax.axis_size(axis)
        return lax.ppermute(value, axis, [(i, i ^ k) for i in range(count)])

    def exchange(value, payload):
        low = cyclic(value, "col", 1)
        high = cyclic(value, "col", -1)
        rec = lax.all_to_all(payload, "row", 0, 0)
        return rec, low, high

    def rows_of(count):
        return ((row_count, width + 2 * layers + count, depth), F32)

    zm, panel, faces = call(
        functools.partial(k_order, grid),
        (
            ((size, n * depth), BF16),
            ((size, width * depth), BF16),
            ((size, 2 * layers * depth), BF16),
        ),
        (basis,),
        scratch=(pltpu.VMEM((size * n, depth), F32),),
    )
    held = [panel] + [xor_step(panel, "row", k) for k in range(2, row_count, 2)]
    far = lax.ppermute(
        faces,
        "row",
        [(i, (i + 1 if i % 2 else i - 1) % row_count) for i in range(row_count)],
    )
    cond, cap, vent, pay0 = call(
        functools.partial(k_first, grid),
        (((n + 8, depth), F32), field, ((width, depth), F32), rows_of(8)),
        (classes, conductivity, capacity, vent_open, partners.reshape(-1)),
        scratch=(
            pltpu.VMEM((n, depth), jnp.int32),
            pltpu.SMEM(conductivity.shape, F32),
            pltpu.SMEM(capacity.shape, F32),
            pltpu.SMEM((pairs,), jnp.int32),
            pltpu.SemaphoreType.DMA((5,)),
        ),
        free=(0, 1, 2, 3, 4),
    )
    rec0, cond_low, cond_high = exchange(cond, pay0)

    own_inner, projected, face_y = call(
        functools.partial(k_basis, grid),
        (small, ((size, depth), F32), ((size, depth), F32)),
        (zm, rhs, cond, cap),
        scratch=(
            pltpu.VMEM((n, size, depth), F32),
            pltpu.VMEM((3 * size, n * depth), BF16),
            pltpu.VMEM((7, n, depth), F32),
        ),
        cost=pl.CostEstimate(flops=200_000_000, bytes_accessed=8_000_000, transcendentals=0),
    )

    panels = ((pairs, size, width * depth), BF16)
    coef, own, inverse, sent, pay1, mine, wanted, vents, names = call(
        functools.partial(k_setup, grid, pairs, col_count),
        (
            ((7, n, depth), F32),
            small,
            small,
            ((n + size // 2 + size, depth), F32),
            rows_of(size // 2),
            panels,
            ((size, (pairs * width + layers) * depth), BF16),
            ((pairs, width, depth), F32),
            ((4 + pairs, depth), F32),
        ),
        (
            ids, cap, vent, cond, cond_low, cond_high, rec0, zm, own_inner, projected, face_y,
            faces, *held,
        ),
        scratch=(
            pltpu.VMEM((3 * size, n * depth), BF16),
            pltpu.VMEM((n, depth), F32),
            pltpu.SemaphoreType.DMA((2 * pairs,)),
        ),
        smem=1,
        free=range(12, 12 + len(held)),
    )
    others = xor_step(wanted, "row", 1)
    rec1, low1, high1 = exchange(sent, pay1)
    places = 5 + pairs
    x0, pay2, solves, y_faces = call(
        functools.partial(k_coarse, grid, pairs),
        (field, pay, ((4 + pairs, size // 2, depth), F32), ((2, size, depth), F32)),
        (ids, coef, vent, zm, inverse, sent, rec1, low1, high1),
        scratch=(pltpu.VMEM((n, depth), F32),),
        smem=1,
    )
    rec, low, high = exchange(x0, pay2)

    def everyone(lines):
        return ((row_count * col_count, lines, depth), F32)

    r0, pay3 = call(
        functools.partial(k_partials, grid, pairs, True),
        (field, everyone((places + 1) // 2)),
        (
            ids, coef, vent, x0, rec, low, high, vents, zm, far, y_faces,
            mine, others, rhs,
        ),
        smem=1,
    )
    blocks, weights, table = call(
        functools.partial(k_blocks, grid, pairs, col_count, 1.0 / cells),
        (
            ((row_count, size, size), F32),
            ((places, size, size), F32),
            ((places * places,), jnp.int32),
        ),
        (
            ids, coef, vents, names, zm, mine, others, own, inverse, far, face_y, y_faces,
            solves, pay3,
        ),
        scratch=(pltpu.VMEM((3 * size, width * depth), BF16),),
        smem=1,
        free=(13,),
        smem_outs=(2,),
        cost=pl.CostEstimate(flops=100_000_000, bytes_accessed=4_000_000, transcendentals=0),
    )
    sums = lax.all_to_all(pay3, ("row", "col"), 0, 0)
    p0, pay4 = call(
        functools.partial(k_combine, grid),
        (field, pay),
        (table, sums, weights, zm, r0, vent),
        scratch=(pltpu.VMEM((n, depth), F32),),
        smem=1,
    )
    rec, low, high = exchange(p0, pay4)
    i0, pay5 = call(
        functools.partial(k_partials, grid, pairs, False),
        (field, everyone((places + 1) // 2)),
        (
            ids, coef, vent, p0, rec, low, high, vents, zm, far, y_faces,
            mine, others,
        ),
        smem=1,
    )
    sums = lax.all_to_all(pay5, ("row", "col"), 0, 0)
    d0, pay6 = call(
        functools.partial(k_combine, grid),
        (field, pay),
        (table, sums, weights, zm, i0, vent),
        scratch=(pltpu.VMEM((n, depth), F32),),
        smem=1,
    )
    rec, low, high = exchange(d0, pay6)
    image, pay7 = call(
        functools.partial(k_dots, grid, pairs),
        (field, everyone(2)),
        (ids, coef, vent, d0, rec, low, high, r0, p0, i0),
        smem=1,
    )
    total = lax.all_to_all(pay7, ("row", "col"), 0, 0)
    x2, r2 = call(k_last, (field, field), (total, x0, r0, p0, i0, d0, image))
    shape = forcing_right_hand.shape
    return x2.reshape(shape), r2.reshape(shape), blocks[None, None]


def solution(mesh):
    return jax.shard_map(
        body,
        mesh=mesh,
        in_specs=(
            P(None, "row", "col"),
            P(None, "row", "col"),
            P(),
            P(),
            P("row", "col"),
            P("row", "col", None),
            P(None, None, "row", "col"),
        ),
        out_specs=(P(None, "row", "col"), P(None, "row", "col"), P("row", "col", None, None, None)),
        check_vma=False,
    )
```

```python
import functools

import jax
import jax.numpy as jnp
from jax import lax
from jax.experimental import pallas as pl
from jax.experimental.pallas import tpu as pltpu
from jax.sharding import PartitionSpec as P

F32 = jnp.float32
BF16 = jnp.bfloat16
VMEM = pl.BlockSpec(memory_space=pltpu.VMEM)
SMEM = pl.BlockSpec(memory_space=pltpu.SMEM)
ANY = pl.BlockSpec(memory_space=pl.ANY)
VMEM_LIMIT = 16 * 1024 * 1024


def harmonic(a, b):
    return 2.0 * a * b / (a + b)


def lookup(material, table):
    result = jnp.zeros(material.shape, F32)
    for class_id in range(table.shape[0]):
        result = jnp.where(material == class_id, table[class_id], result)
    return result


class Grid:
    def __init__(self, layers, width, depth):
        self.layers, self.width, self.depth = layers, width, depth
        self.rows = layers * width

    def masks(self):
        shape = (self.rows, self.depth)
        row = lax.broadcasted_iota(jnp.int32, shape, 0)
        lane = lax.broadcasted_iota(jnp.int32, shape, 1)
        return lax.rem(row, self.width), lane, row

    def spread(self, face):
        parts = [
            jnp.broadcast_to(face[z : z + 1], (self.width, self.depth)) for z in range(self.layers)
        ]
        return jnp.concatenate(parts, axis=0)

    def faces(self, v):
        w = self.width
        last = [v[z * w + w - 1 : z * w + w] for z in range(self.layers)]
        first = [v[z * w : z * w + 1] for z in range(self.layers)]
        return last + first

    def payload(self, top, v):
        return jnp.concatenate([top] + self.faces(v), axis=0)

    def around(self, v, low_x, high_x, low_y, high_y):
        xi, lane, _ = self.masks()
        n, d = self.rows, self.depth
        zero = jnp.zeros((n, d), F32)
        own = zero if v is None else v
        plus = zero if v is None else pltpu.roll(v, n - 1, 0)
        minus = zero if v is None else pltpu.roll(v, 1, 0)
        up_x = jnp.where(xi == self.width - 1, self.spread(high_x), plus)
        down_x = jnp.where(xi == 0, self.spread(low_x), minus)
        up_y = pltpu.roll(jnp.where(lane == 0, high_y, own), d - 1, 1)
        down_y = pltpu.roll(jnp.where(lane == d - 1, low_y, own), 1, 1)
        return up_x, down_x, up_y, down_y

    def shifted_z(self, v):
        w = self.width
        return jnp.concatenate([v[w:], v[:w]], axis=0), jnp.concatenate([v[-w:], v[:-w]], axis=0)


def received(grid, ids, pairs, rec):
    count = rec.shape[0]
    w, layers = grid.width, grid.layers
    coupled = rec[ids[0], 0:w, :]
    for k in range(1, pairs):
        coupled = coupled + rec[ids[k], 0:w, :]
    row_at = ids[pairs]
    low = rec[jnp.maximum(row_at - 1, 0), w : w + layers, :]
    high = rec[jnp.minimum(row_at + 1, count - 1), w + layers : w + 2 * layers, :]
    return coupled, low, high


def operate(grid, coef, vent, v, rest):
    coupled, low_x, high_x, low_y, high_y = rest
    up_x, down_x, up_y, down_y = grid.around(v, low_x, high_x, low_y, high_y)
    beside = coef[3] * up_x + coef[4] * down_x + coef[5] * up_y + coef[6] * down_y
    if v is None:
        xi, lane, _ = grid.masks()
        result = -beside
    else:
        up_z, down_z = grid.shifted_z(v)
        result = coef[0] * v - (beside + coef[1] * up_z + coef[2] * down_z)
    w = grid.width
    return jnp.concatenate([result[:-w], result[-w:] - vent * coupled], axis=0)


def project(grid, zm, v):
    d = grid.depth
    parts = [None, None]
    for row in range(grid.rows):
        term = zm[:, row * d : (row + 1) * d].astype(F32) * v[row : row + 1, :]
        k = row % 2
        parts[k] = term if parts[k] is None else parts[k] + term
    return jnp.sum(parts[0] + parts[1], axis=1, keepdims=True)


def solve_own(inverse, column):
    size = inverse.shape[0]
    along = jnp.sum(inverse[...] * column, axis=0, keepdims=True)
    eye = lax.broadcasted_iota(jnp.int32, (size, size), 0) == lax.broadcasted_iota(
        jnp.int32, (size, size), 1
    )
    return jnp.sum(jnp.where(eye, along, 0.0), axis=1, keepdims=True)


def expand(grid, zm, column, out):
    d = grid.depth
    wide = jnp.broadcast_to(column, (column.shape[0], d))
    for row in range(grid.rows):
        out[row : row + 1, :] = jnp.sum(
            zm[:, row * d : (row + 1) * d].astype(F32) * wide, axis=0, keepdims=True
        )


def to_all(grid, pay, top, v, *more):
    block = jnp.concatenate([grid.payload(top, v), *more], axis=0)
    for slot in range(pay.shape[0]):
        pay[slot] = block


def split3(w):
    hi = w.astype(BF16)
    rest = w - hi.astype(F32)
    mid = rest.astype(BF16)
    lo = (rest - mid.astype(F32)).astype(BF16)
    return hi, mid, lo


def dot_nt(a, b):
    return lax.dot_general(a, b, (((1,), (1,)), ((), ())), preferred_element_type=F32)


def fold3(stacked):
    size = stacked.shape[0] // 3
    return stacked[:size] + (stacked[size : 2 * size] + stacked[2 * size :])


def weighted_gram(w3, parts, weights, other):
    size = other.shape[0]
    k = other.shape[1] // len(weights)
    for i, (part, weight) in enumerate(zip(parts, weights)):
        at = slice(i * k, (i + 1) * k)
        hi, mid, lo = split3(part.astype(F32) * weight)
        w3[0:size, at] = hi
        w3[size : 2 * size, at] = mid
        w3[2 * size : 3 * size, at] = lo
    return fold3(dot_nt(w3[:, : len(weights) * k], other))


def y_weights(grid, first, last):
    n, d = grid.rows, grid.depth
    row = lax.broadcasted_iota(jnp.int32, (n, d), 0)
    lane = lax.broadcasted_iota(jnp.int32, (n, d), 1)
    wide = jnp.where(lane == row, first[:, 0:1], 0.0)
    wide = wide + jnp.where(lane == n + row, last[:, d - 1 : d], 0.0)
    return jnp.sum(wide, axis=0, keepdims=True)


def invert_spd(m, ahead=5):
    size = m.shape[0]
    row_id = lax.broadcasted_iota(jnp.int32, (size, size), 0)
    col_id = lax.broadcasted_iota(jnp.int32, (size, size), 1)

    def column(k):
        return jnp.broadcast_to(m[:, k : k + 1], (size, size))

    waiting = {k: column(k) for k in range(min(ahead + 1, size))}
    for k in range(size):
        col = waiting.pop(k)
        inv = 1.0 / col[k : k + 1, :]
        for j in list(waiting):
            at_row = col[j : j + 1, :] * inv
            waiting[j] = jnp.where(row_id == k, at_row, waiting[j] - col * at_row)
        scaled_row = jnp.where(col_id[:1] == k, -inv, m[k : k + 1, :] * inv)
        m = jnp.where(row_id == k, scaled_row, jnp.where(col_id == k, 0.0, m) - col * scaled_row)
        if k + ahead + 1 < size:
            waiting[k + ahead + 1] = column(k + ahead + 1)
    return -m


def opposite(place):
    return {1: 2, 2: 1, 3: 4, 4: 3}.get(place, place)


def k_first(
    grid, material, conductivity, capacity, vent, partners, cond_out, cap_out, vent_out, pay,
    classes, cond_table, cap_table, pair_table, sems,
):
    copies = [
        pltpu.make_async_copy(src, dst, sems.at[i])
        for i, (src, dst) in enumerate(
            (
                (material, classes),
                (conductivity, cond_table),
                (capacity, cap_table),
                (vent, vent_out),
                (partners, pair_table),
            )
        )
    ]
    for copy in copies:
        copy.start()
    for copy in copies:
        copy.wait()
    cond = lookup(classes[...], cond_table)
    lane = lax.broadcasted_iota(jnp.int32, (8, grid.depth), 1)
    names = jnp.zeros((8, grid.depth), F32)
    for k in range(pair_table.shape[0]):
        names = jnp.where(lane == k, pair_table[k].astype(F32), names)
    cond_out[0 : grid.rows, :] = cond
    cond_out[grid.rows :, :] = names
    cap_out[...] = lookup(classes[...], cap_table)
    to_all(grid, pay, vent_out[...], cond, names)


def conductances(grid, cond, low_x, high_x, low_y, high_y):
    _, _, row = grid.masks()
    up_z, down_z = grid.shifted_z(cond)
    uz = jnp.where(row < grid.rows - grid.width, harmonic(cond, up_z), 0.0)
    lz = jnp.where(row >= grid.width, harmonic(cond, down_z), 0.0)
    ux, lx, uy, ly = [harmonic(cond, c) for c in grid.around(cond, low_x, high_x, low_y, high_y)]
    return uz, lz, ux, lx, uy, ly


def k_order(grid, basis, zm, panel, faces, wide):
    n, d, w, layers = grid.rows, grid.depth, grid.width, grid.layers
    size = basis.shape[0]

    def unpack(a, _):
        wide[pl.ds(a * n, n), :] = basis[a].astype(F32)
        return 0

    lax.fori_loop(0, size, unpack, 0, unroll=4)
    for row in range(n):
        packed = wide[pl.ds(row, size, stride=n), :].astype(BF16)
        zm[:, row * d : (row + 1) * d] = packed
        layer, x = divmod(row, w)
        if layer == layers - 1:
            panel[:, x * d : (x + 1) * d] = packed
        if x == 0:
            faces[:, layer * d : (layer + 1) * d] = packed
        if x == w - 1:
            faces[:, (layers + layer) * d : (layers + layer + 1) * d] = packed


def k_basis(grid, zm, rhs, cond_ref, cap_ref, own, projected, face_y, zr, w3, coef):
    n, d, w = grid.rows, grid.depth, grid.width
    size = zm.shape[0]
    cond = cond_ref[0:n, :]
    zero_face = jnp.zeros((grid.layers, d), F32)
    zero = jnp.zeros((n, d), F32)
    uz, lz, ux, lx, uy, ly = conductances(grid, cond, zero_face, zero_face, zero, zero)
    coef[0] = cap_ref[...] + uz + lz + ux + lx + uy + ly
    for i, c in enumerate((uz, lz, ux, lx, uy, ly)):
        coef[i + 1] = c

    parts = [None, None]
    lane = lax.broadcasted_iota(jnp.int32, (size, d), 1)
    sides = jnp.zeros((size, d), F32)
    for row in range(n):
        z = zm[:, row * d : (row + 1) * d].astype(F32)
        zr[row] = z
        sides = jnp.where(lane == row, z[:, 0:1], sides)
        sides = jnp.where(lane == n + row, z[:, d - 1 : d], sides)
        term = z * rhs[row : row + 1, :]
        parts[row % 2] = term if parts[row % 2] is None else parts[row % 2] + term
    projected[...] = parts[0] + parts[1]
    face_y[...] = sides
    total = None
    for start in range(0, n, 8):
        for row in range(start, start + 8):
            z = zr[row]

            def c(i):
                return coef[i, row : row + 1, :]

            acc = c(0) * z
            if row + w < n:
                acc = acc - c(1) * zr[row + w]
            if row >= w:
                acc = acc - c(2) * zr[row - w]
            if row % w < w - 1:
                acc = acc - c(3) * zr[row + 1]
            if row % w > 0:
                acc = acc - c(4) * zr[row - 1]
            acc = acc - c(5) * pltpu.roll(z, d - 1, 1) - c(6) * pltpu.roll(z, 1, 1)
            at = slice(row * d, (row + 1) * d)
            hi, mid, lo = split3(acc)
            w3[0:size, at] = hi
            w3[size : 2 * size, at] = mid
            w3[2 * size : 3 * size, at] = lo
        part = dot_nt(w3[:, start * d : (start + 8) * d], zm[:, start * d : (start + 8) * d])
        total = part if total is None else total + part
    own[...] = fold3(total)


def pick(sources, targets, sems):
    for i, (index, target) in enumerate(targets):
        for j, source in enumerate(sources):

            @pl.when(index == j)
            def _(source=source, target=target, i=i):
                pltpu.make_async_copy(source, target, sems.at[i]).start()


def await_picks(sources, targets, sems):
    for i, (_, target) in enumerate(targets):
        pltpu.make_async_copy(sources[0], target, sems.at[i]).wait()


def k_setup(
    grid, pairs, cols, ids, cap, vent, cond, cond_low, cond_high, rec,
    zm, own_inner, projected, face_y, *rest,
):
    n, d, w, layers = grid.rows, grid.depth, grid.width, grid.layers
    held = [zm.at[:, pl.ds((n - w) * d, w * d)], *rest[:-12]]
    coef, own, inverse, sent, pay, mine, wanted, vents, names, w3, v0, sems = rest[-12:]
    count = rec.shape[0]
    panel = w * d
    line = w + 2 * layers
    sibling = lax.bitwise_xor(ids[pairs], 1)
    names_lane = lax.broadcasted_iota(jnp.int32, (1, d), 1)
    targets = []
    for k in range(pairs):
        theirs = jnp.where(names_lane == k, rec[sibling, line : line + 1, :], 0.0)
        for partner, target in (
            (ids[k], mine.at[k]),
            (jnp.sum(theirs).astype(jnp.int32), wanted.at[:, pl.ds(k * panel, panel)]),
        ):
            index = lax.shift_right_logical(lax.bitwise_xor(partner, ids[pairs]), 1)
            targets.append((index, target))
    pick(held, targets, sems)

    upward = lax.bitwise_and(ids[pairs], 1) == 0
    for z in range(layers):
        low_face = zm[:, z * panel : z * panel + d]
        high_face = zm[:, (z + 1) * panel - d : (z + 1) * panel]
        at = slice(pairs * panel + z * d, pairs * panel + (z + 1) * d)
        wanted[:, at] = jnp.where(upward, high_face.astype(F32), low_face.astype(F32)).astype(BF16)
    for k in range(pairs):
        vents[k] = vent[...] * rec[ids[k], 0:w, :]
    up, down = jnp.minimum(ids[pairs] + 1, count - 1), jnp.maximum(ids[pairs] - 1, 0)
    lines = [rec[r, line : line + 1, :] for r in (up, down)]
    lines += [cond_high[n : n + 1, :], cond_low[n : n + 1, :]]
    lines += [rec[ids[k], line : line + 1, :] for k in range(pairs)]
    names[...] = jnp.concatenate(lines, axis=0)
    vent_sum, low_x, high_x = received(grid, ids, pairs, rec)
    row_at, col_at = ids[pairs], ids[pairs + 1]
    low_x = jnp.where(row_at > 0, low_x, 0.0)
    high_x = jnp.where(row_at < count - 1, high_x, 0.0)
    low_y = jnp.where(col_at > 0, cond_low[0:n, :], 0.0)
    high_y = jnp.where(col_at < cols - 1, cond_high[0:n, :], 0.0)
    uz, lz, ux, lx, uy, ly = conductances(grid, cond[0:n, :], low_x, high_x, low_y, high_y)
    plenum = vent[...] * vent_sum
    diagonal = cap[...] + uz + lz + ux + lx + uy + ly
    coef[0] = jnp.concatenate([diagonal[:-w], diagonal[-w:] + plenum], axis=0)
    for i, c in enumerate((uz, lz, ux, lx, uy, ly)):
        coef[i + 1] = c
    last, first = [ux[z * w + w - 1 :][:1] for z in range(layers)], [lx[z * w :][:1] for z in range(layers)]
    top = [plenum[x : x + 1] for x in range(w)]
    top[0] = top[0] + first[-1]
    top[-1] = top[-1] + last[-1]
    row = n - w
    tops = zm[:, row * d :]
    block = own_inner[...] + weighted_gram(
        w3, [tops[:, x * d : (x + 1) * d] for x in range(w)], top, tops
    )
    for at, weights in ((0, first[:-1]), (panel - d, last[:-1])):
        parts = [zm[:, z * panel + at : z * panel + at + d] for z in range(layers - 1)]
        block = block + weighted_gram(w3, parts, weights, jnp.concatenate(parts, axis=1))
    sides = face_y[...].astype(BF16)
    block = block + weighted_gram(w3, [sides], [y_weights(grid, ly, uy)], sides)
    own[...] = block
    inverse[...] = invert_spd(block)
    y0 = solve_own(inverse, jnp.sum(projected[...], axis=1, keepdims=True))
    expand(grid, zm, y0, v0)
    field = v0[...]
    half = zm.shape[0] // 2
    folded = jnp.concatenate([inverse[0:half, :], inverse[half:, :]], axis=1)
    sent[0:n, :] = field
    sent[n : n + half, :] = folded
    sent[n + half :, :] = face_y[...]
    to_all(grid, pay, vent[...] * field[-w:], field, folded)
    await_picks(held, targets, sems)


def incoming(grid, pairs, ids, rec, low, high):
    coupled, low_x, high_x = received(grid, ids, pairs, rec)
    n = grid.rows
    return coupled, low_x, high_x, low[0:n, :], high[0:n, :]


def k_coarse(
    grid, pairs, ids, coef, vent, zm, inverse, field, rec, low, high, out, pay, solves, y_faces, scratch
):
    n, w = grid.rows, grid.width
    beside = operate(grid, coef, vent[...], None, incoming(grid, pairs, ids, rec, low, high))
    expand(grid, zm, solve_own(inverse, project(grid, zm, beside)), scratch)
    result = field[0:n, :] - scratch[...]
    out[...] = result
    to_all(grid, pay, vent[...] * result[-w:], result)
    half = solves.shape[1]
    first = w + 2 * grid.layers
    row_at = ids[pairs]
    solves[0] = rec[jnp.minimum(row_at + 1, rec.shape[0] - 1), first : first + half, :]
    solves[1] = rec[jnp.maximum(row_at - 1, 0), first : first + half, :]
    solves[2] = high[n : n + half, :]
    solves[3] = low[n : n + half, :]
    for k in range(pairs):
        solves[4 + k] = rec[ids[k], first : first + half, :]
    y_faces[0] = high[n + half :, :]
    y_faces[1] = low[n + half :, :]


def chosen(grid, pairs, ids, mine, others, k, at):
    panel = grid.width * grid.depth
    same = lax.bitwise_and(lax.bitwise_xor(ids[k], ids[pairs]), 1) == 0
    there = slice(k * panel + at.start, k * panel + at.stop)
    return jnp.where(same, mine[k, :, at].astype(F32), others[:, there].astype(F32))


def x_faces(grid, pairs, ids, others, far):
    half = grid.layers * grid.depth
    near = others[:, pairs * grid.width * grid.depth :].astype(F32)
    upward = lax.bitwise_and(ids[pairs], 1) == 0
    return (
        jnp.where(upward, near, far[:, :half].astype(F32)),
        jnp.where(upward, far[:, half:].astype(F32), near),
    )


def k_partials(
    grid, pairs, base, ids, coef, vent, field, rec, low, high, vents, zm, y_faces, mine, others,
    far, *rest,
):
    n, d, w, layers = grid.rows, grid.depth, grid.width, grid.layers
    size = zm.shape[0]
    base_ref = rest[0] if base else None
    out, pay = rest[-2:]
    next_first, prev_last = x_faces(grid, pairs, ids, others, far)
    v = operate(grid, coef, vent[...], field[...], incoming(grid, pairs, ids, rec, low, high))
    if base:
        v = base_ref[...] - v
    out[...] = v
    face, zero = jnp.zeros((layers, d), F32), jnp.zeros((n, d), F32)
    own = operate(grid, coef, vent[...], v, (jnp.zeros((w, d), F32), face, face, zero, zero))

    def along(basis, weights):
        total = None
        for i, weight in enumerate(weights):
            term = basis[:, i * d : (i + 1) * d].astype(F32) * weight
            total = term if total is None else total + term
        return total

    even = along(zm, [own[i : i + 1] for i in range(n)])
    ux, lx, uy, ly = [coef[i] * v for i in (3, 4, 5, 6)]
    sums = [
        even,
        -along(next_first, [ux[z * w + w - 1 : z * w + w] for z in range(layers)]),
        -along(prev_last, [lx[z * w : z * w + 1] for z in range(layers)]),
    ]
    toward = pltpu.roll(y_weights(grid, ly, uy), n, 1)
    lane = lax.broadcasted_iota(jnp.int32, (1, d), 1)
    sums.append(-(y_faces[0] * jnp.where(lane < n, toward, 0.0)))
    sums.append(-(y_faces[1] * jnp.where(lane < n, 0.0, toward)))
    top = v[-w:]
    for k in range(pairs):
        weight = vents[k] * top
        total = None
        for x in range(w):
            part = chosen(grid, pairs, ids, mine, others, k, slice(x * d, (x + 1) * d))
            term = part * weight[x : x + 1]
            total = term if total is None else total + term
        sums.append(-total)
    ones = jnp.ones((8, d), F32)
    rows = [
        lax.dot_general(
            ones, q, (((1,), (1,)), ((), ())),
            precision=lax.Precision.HIGHEST, preferred_element_type=F32,
        )[0:1]
        for q in sums
    ]
    if len(rows) % 2:
        rows.append(jnp.zeros((1, size), F32))
    block = jnp.concatenate(
        [jnp.concatenate(rows[i : i + 2], axis=1) for i in range(0, len(rows), 2)], axis=0
    )
    for slot in range(pay.shape[0]):
        pay[slot] = block


def k_combine(grid, table, rec, weights, zm, base, vent, out, pay, scratch):
    size = zm.shape[0]
    count = weights.shape[0]
    total = None
    for j in range(count):
        sides = [None, None]
        for i in range(count):
            at = table[j * count + i]
            line, side = divmod(opposite(i), 2)
            term = rec[jnp.maximum(at, 0), line : line + 1, :]
            term = jnp.where(at >= 0, term, 0.0)
            sides[side] = term if sides[side] is None else sides[side] + term
        term = weights[j] * (sides[0][:, 0:size] + sides[1][:, size : 2 * size])
        total = term if total is None else total + term
    expand(grid, zm, jnp.sum(total, axis=1, keepdims=True), scratch)
    result = base[...] - scratch[...]
    out[...] = result
    to_all(grid, pay, vent[...] * result[-grid.width :], result)


def k_dots(grid, pairs, ids, coef, vent, field, rec, low, high, r0, p0, i0, out, pay):
    image = operate(grid, coef, vent[...], field[...], incoming(grid, pairs, ids, rec, low, high))
    out[...] = image
    d, r, p, i = field[...], r0[...], p0[...], i0[...]
    products = (r * r, p * i, r * i, i * i, d * i, d * image)
    lane = lax.broadcasted_iota(jnp.int32, pay.shape[1:], 1)
    block = jnp.zeros(pay.shape[1:], F32)
    for k, q in enumerate(products):
        total = jnp.sum(jnp.sum(q, axis=0, keepdims=True), axis=1, keepdims=True)
        block = jnp.where(lane == k, total, block)
    for slot in range(pay.shape[0]):
        pay[slot] = block


def k_last(rec, x0, r0, p0, i0, d, image, x2, r2):
    total = rec[0]
    for slot in range(1, rec.shape[0]):
        total = total + rec[slot]
    rr, pi, ri, ii, di, dd = [total[0:1, k : k + 1] for k in range(6)]
    a1 = rr / pi
    new = rr - 2.0 * a1 * ri + a1 * a1 * ii
    grow = 1.0 + new / rr
    a2 = new / (grow * grow * pi - 2.0 * grow * a1 * di + a1 * a1 * dd)
    x2[...] = x0[...] + (a1 + a2 * grow) * p0[...] - (a2 * a1) * d[...]
    r2[...] = r0[...] - (a1 + a2 * grow) * i0[...] + (a2 * a1) * image[...]


def k_blocks(
    grid, pairs, cols, scale, ids, coef, vents, names, zm, mine, others, far, own, inverse,
    face_y, y_faces, solves, _, out, weights, table, w3,
):
    n, d, w, layers = grid.rows, grid.depth, grid.width, grid.layers
    rows, size = out.shape[0], out.shape[1]
    row_at = ids[pairs]
    up, down = jnp.minimum(row_at + 1, rows - 1), jnp.maximum(row_at - 1, 0)

    col_at = ids[pairs + 1]
    lane = lax.broadcasted_iota(jnp.int32, (1, d), 1)
    near = [(row_at, col_at), (row_at + 1, col_at), (row_at - 1, col_at)]
    near += [(row_at, col_at + 1), (row_at, col_at - 1)]
    near += [(ids[k], col_at) for k in range(pairs)]
    count = len(near)
    for j, (r, c) in enumerate(near):
        places = [(r, c), (r + 1, c), (r - 1, c), (r, c + 1), (r, c - 1)]
        for k in range(pairs):
            met = ids[k]
            if j > 0:
                met = jnp.sum(jnp.where(lane == k, names[j - 1 : j, :], 0.0)).astype(jnp.int32)
            places.append((met, c))
        there = (r >= 0) & (r < rows) & (c >= 0) & (c < cols)
        for i, (pr, pc) in enumerate(places):
            good = there & (pr >= 0) & (pr < rows) & (pc >= 0) & (pc < cols)
            table[j * count + i] = jnp.where(good, pr * cols + pc, -1)

    def dot(a, b):
        return lax.dot_general(
            a, b, (((1,), (0,)), ((), ())),
            precision=lax.Precision.HIGHEST, preferred_element_type=F32,
        )

    ux, lx, uy, ly = coef[3], coef[4], coef[5], coef[6]
    last = [z * w + w - 1 for z in range(layers)]
    first = [z * w for z in range(layers)]

    def basis_rows(at):
        return [zm[:, i * d : (i + 1) * d] for i in at]

    next_first, prev_last = [f.astype(BF16) for f in x_faces(grid, pairs, ids, others, far)]
    found = [
        weighted_gram(w3, basis_rows(last), [-ux[i : i + 1] for i in last], next_first),
        weighted_gram(w3, basis_rows(first), [-lx[i : i + 1] for i in first], prev_last),
    ]
    toward = -pltpu.roll(y_weights(grid, ly, uy), n, 1)
    swapped = pltpu.roll(face_y[...], n, 1)
    for k, there in ((0, lane < n), (1, lane >= n)):
        weight = jnp.where(there, toward, 0.0)
        found.append(weighted_gram(w3, [swapped], [weight], y_faces[k].astype(BF16)))
    top = basis_rows(range(n - w, n))
    for k in range(pairs):
        panel = chosen(grid, pairs, ids, mine, others, k, slice(0, w * d)).astype(BF16)
        found.append(weighted_gram(w3, top, [-vents[k, i : i + 1, :] for i in range(w)], panel))

    for slot in range(rows):
        out[slot] = jnp.zeros((size, size), F32)
    out[row_at] = own[...] * scale
    out[up] = out[up] + jnp.where(row_at < rows - 1, found[0] * scale, 0.0)
    out[down] = out[down] + jnp.where(row_at > 0, found[1] * scale, 0.0)
    for k in range(pairs):
        out[ids[k]] = out[ids[k]] + found[4 + k] * scale

    weights[0] = inverse[...]
    for j, block in enumerate(found):
        theirs = jnp.concatenate([solves[j, :, 0:size], solves[j, :, size:]], axis=0)
        weights[j + 1] = -dot(inverse[...], dot(block, theirs))


def call(kernel, outs, operands, scratch=(), smem=0, free=(), smem_outs=(), cost=None):
    specs = [
        SMEM if i < smem else ANY if i in free else VMEM for i in range(len(operands))
    ]
    return pl.pallas_call(
        kernel,
        out_shape=tuple(jax.ShapeDtypeStruct(s, t) for s, t in outs),
        in_specs=specs,
        out_specs=tuple(SMEM if i in smem_outs else VMEM for i in range(len(outs))),
        scratch_shapes=list(scratch),
        compiler_params=pltpu.CompilerParams(vmem_limit_bytes=VMEM_LIMIT),
        cost_estimate=cost,
    )(*operands)


def body(forcing_right_hand, material, capacity, conductivity, vent_open, partners, subspace_basis):
    layers, width, depth = forcing_right_hand.shape
    size = subspace_basis.shape[0]
    grid = Grid(layers, width, depth)
    n, cells = grid.rows, forcing_right_hand.size
    row_count, col_count = lax.axis_size("row"), lax.axis_size("col")
    pairs = partners.shape[-1]
    ids = jnp.concatenate(
        [
            partners.reshape(-1),
            jnp.stack([lax.axis_index("row"), lax.axis_index("col")]).astype(jnp.int32),
        ]
    )
    rhs = forcing_right_hand.reshape(n, depth)
    classes = material.reshape(n, depth)
    basis = subspace_basis.reshape(size, n, depth)
    field = ((n, depth), F32)
    pay = ((row_count, width + 2 * layers, depth), F32)
    small = ((size, size), F32)

    def cyclic(value, axis, step):
        count = lax.axis_size(axis)
        return lax.ppermute(value, axis, [(i, (i + step) % count) for i in range(count)])

    def xor_step(value, axis, k):
        count = lax.axis_size(axis)
        return lax.ppermute(value, axis, [(i, i ^ k) for i in range(count)])

    def exchange(value, payload):
        low = cyclic(value, "col", 1)
        high = cyclic(value, "col", -1)
        rec = lax.all_to_all(payload, "row", 0, 0)
        return rec, low, high

    def rows_of(count):
        return ((row_count, width + 2 * layers + count, depth), F32)

    zm, panel, faces = call(
        functools.partial(k_order, grid),
        (
            ((size, n * depth), BF16),
            ((size, width * depth), BF16),
            ((size, 2 * layers * depth), BF16),
        ),
        (basis,),
        scratch=(pltpu.VMEM((size * n, depth), F32),),
        cost=pl.CostEstimate(flops=1000, bytes_accessed=1000, transcendentals=0),
    )
    held = [xor_step(panel, "row", k) for k in range(2, row_count, 2)]
    far = lax.ppermute(
        faces,
        "row",
        [(i, (i + 1 if i % 2 else i - 1) % row_count) for i in range(row_count)],
    )
    cond, cap, vent, pay0 = call(
        functools.partial(k_first, grid),
        (((n + 8, depth), F32), field, ((width, depth), F32), rows_of(8)),
        (classes, conductivity, capacity, vent_open, partners.reshape(-1)),
        scratch=(
            pltpu.VMEM((n, depth), jnp.int32),
            pltpu.SMEM(conductivity.shape, F32),
            pltpu.SMEM(capacity.shape, F32),
            pltpu.SMEM((pairs,), jnp.int32),
            pltpu.SemaphoreType.DMA((5,)),
        ),
        free=(0, 1, 2, 3, 4),
    )
    rec0, cond_low, cond_high = exchange(cond, pay0)

    own_inner, projected, face_y = call(
        functools.partial(k_basis, grid),
        (small, ((size, depth), F32), ((size, depth), F32)),
        (zm, rhs, cond, cap),
        scratch=(
            pltpu.VMEM((n, size, depth), F32),
            pltpu.VMEM((3 * size, n * depth), BF16),
            pltpu.VMEM((7, n, depth), F32),
        ),
        cost=pl.CostEstimate(flops=1000, bytes_accessed=1000, transcendentals=0),
    )

    panels = ((pairs, size, width * depth), BF16)
    coef, own, inverse, sent, pay1, mine, wanted, vents, names = call(
        functools.partial(k_setup, grid, pairs, col_count),
        (
            ((7, n, depth), F32),
            small,
            small,
            ((n + size // 2 + size, depth), F32),
            rows_of(size // 2),
            panels,
            ((size, (pairs * width + layers) * depth), BF16),
            ((pairs, width, depth), F32),
            ((4 + pairs, depth), F32),
        ),
        (
            ids, cap, vent, cond, cond_low, cond_high, rec0, zm, own_inner, projected, face_y,
            *held,
        ),
        scratch=(
            pltpu.VMEM((3 * size, n * depth), BF16),
            pltpu.VMEM((n, depth), F32),
            pltpu.SemaphoreType.DMA((2 * pairs,)),
        ),
        smem=1,
        free=range(11, 11 + len(held)),
    )
    others = xor_step(wanted, "row", 1)
    rec1, low1, high1 = exchange(sent, pay1)
    places = 5 + pairs
    x0, pay2, solves, y_faces = call(
        functools.partial(k_coarse, grid, pairs),
        (field, pay, ((4 + pairs, size // 2, depth), F32), ((2, size, depth), F32)),
        (ids, coef, vent, zm, inverse, sent, rec1, low1, high1),
        scratch=(pltpu.VMEM((n, depth), F32),),
        smem=1,
    )
    rec, low, high = exchange(x0, pay2)

    def everyone(lines):
        return ((row_count * col_count, lines, depth), F32)

    r0, pay3 = call(
        functools.partial(k_partials, grid, pairs, True),
        (field, everyone((places + 1) // 2)),
        (
            ids, coef, vent, x0, rec, low, high, vents, zm, y_faces, mine, others, far, rhs,
        ),
        smem=1,
    )
    blocks, weights, table = call(
        functools.partial(k_blocks, grid, pairs, col_count, 1.0 / cells),
        (
            ((row_count, size, size), F32),
            ((places, size, size), F32),
            ((places * places,), jnp.int32),
        ),
        (
            ids, coef, vents, names, zm, mine, others, far, own, inverse, face_y, y_faces,
            solves, pay3,
        ),
        scratch=(pltpu.VMEM((3 * size, width * depth), BF16),),
        smem=1,
        free=(13,),
        smem_outs=(2,),
        cost=pl.CostEstimate(flops=100_000_000, bytes_accessed=4_000_000, transcendentals=0),
    )
    sums = lax.all_to_all(pay3, ("row", "col"), 0, 0)
    p0, pay4 = call(
        functools.partial(k_combine, grid),
        (field, pay),
        (table, sums, weights, zm, r0, vent),
        scratch=(pltpu.VMEM((n, depth), F32),),
        smem=1,
    )
    rec, low, high = exchange(p0, pay4)
    i0, pay5 = call(
        functools.partial(k_partials, grid, pairs, False),
        (field, everyone((places + 1) // 2)),
        (
            ids, coef, vent, p0, rec, low, high, vents, zm, y_faces, mine, others, far,
        ),
        smem=1,
    )
    sums = lax.all_to_all(pay5, ("row", "col"), 0, 0)
    d0, pay6 = call(
        functools.partial(k_combine, grid),
        (field, pay),
        (table, sums, weights, zm, i0, vent),
        scratch=(pltpu.VMEM((n, depth), F32),),
        smem=1,
    )
    rec, low, high = exchange(d0, pay6)
    image, pay7 = call(
        functools.partial(k_dots, grid, pairs),
        (field, everyone(2)),
        (ids, coef, vent, d0, rec, low, high, r0, p0, i0),
        smem=1,
    )
    total = lax.all_to_all(pay7, ("row", "col"), 0, 0)
    x2, r2 = call(k_last, (field, field), (total, x0, r0, p0, i0, d0, image))
    shape = forcing_right_hand.shape
    return x2.reshape(shape), r2.reshape(shape), blocks[None, None]


def solution(mesh):
    return jax.shard_map(
        body,
        mesh=mesh,
        in_specs=(
            P(None, "row", "col"),
            P(None, "row", "col"),
            P(),
            P(),
            P("row", "col"),
            P("row", "col", None),
            P(None, None, "row", "col"),
        ),
        out_specs=(P(None, "row", "col"), P(None, "row", "col"), P("row", "col", None, None, None)),
        check_vma=False,
    )
```

```python
import functools

import jax
import jax.numpy as jnp
from jax import lax
from jax.experimental import pallas as pl
from jax.experimental.pallas import tpu as pltpu
from jax.sharding import PartitionSpec as P

F32 = jnp.float32
BF16 = jnp.bfloat16
VMEM = pl.BlockSpec(memory_space=pltpu.VMEM)
SMEM = pl.BlockSpec(memory_space=pltpu.SMEM)
ANY = pl.BlockSpec(memory_space=pl.ANY)
VMEM_LIMIT = 16 * 1024 * 1024


def harmonic(a, b):
    return 2.0 * a * b / (a + b)


def lookup(material, table):
    result = jnp.zeros(material.shape, F32)
    for class_id in range(table.shape[0]):
        result = jnp.where(material == class_id, table[class_id], result)
    return result


class Grid:
    def __init__(self, layers, width, depth):
        self.layers, self.width, self.depth = layers, width, depth
        self.rows = layers * width

    def masks(self):
        shape = (self.rows, self.depth)
        row = lax.broadcasted_iota(jnp.int32, shape, 0)
        lane = lax.broadcasted_iota(jnp.int32, shape, 1)
        return lax.rem(row, self.width), lane, row

    def spread(self, face):
        parts = [
            jnp.broadcast_to(face[z : z + 1], (self.width, self.depth)) for z in range(self.layers)
        ]
        return jnp.concatenate(parts, axis=0)

    def faces(self, v):
        w = self.width
        last = [v[z * w + w - 1 : z * w + w] for z in range(self.layers)]
        first = [v[z * w : z * w + 1] for z in range(self.layers)]
        return last + first

    def payload(self, top, v):
        return jnp.concatenate([top] + self.faces(v), axis=0)

    def around(self, v, low_x, high_x, low_y, high_y):
        xi, lane, _ = self.masks()
        n, d = self.rows, self.depth
        zero = jnp.zeros((n, d), F32)
        own = zero if v is None else v
        plus = zero if v is None else pltpu.roll(v, n - 1, 0)
        minus = zero if v is None else pltpu.roll(v, 1, 0)
        up_x = jnp.where(xi == self.width - 1, self.spread(high_x), plus)
        down_x = jnp.where(xi == 0, self.spread(low_x), minus)
        up_y = pltpu.roll(jnp.where(lane == 0, high_y, own), d - 1, 1)
        down_y = pltpu.roll(jnp.where(lane == d - 1, low_y, own), 1, 1)
        return up_x, down_x, up_y, down_y

    def shifted_z(self, v):
        w = self.width
        return jnp.concatenate([v[w:], v[:w]], axis=0), jnp.concatenate([v[-w:], v[:-w]], axis=0)


def received(grid, ids, pairs, rec):
    count = rec.shape[0]
    w, layers = grid.width, grid.layers
    coupled = rec[ids[0], 0:w, :]
    for k in range(1, pairs):
        coupled = coupled + rec[ids[k], 0:w, :]
    row_at = ids[pairs]
    low = rec[jnp.maximum(row_at - 1, 0), w : w + layers, :]
    high = rec[jnp.minimum(row_at + 1, count - 1), w + layers : w + 2 * layers, :]
    return coupled, low, high


def operate(grid, coef, vent, v, rest):
    coupled, low_x, high_x, low_y, high_y = rest
    up_x, down_x, up_y, down_y = grid.around(v, low_x, high_x, low_y, high_y)
    beside = coef[3] * up_x + coef[4] * down_x + coef[5] * up_y + coef[6] * down_y
    if v is None:
        xi, lane, _ = grid.masks()
        result = -beside
    else:
        up_z, down_z = grid.shifted_z(v)
        result = coef[0] * v - (beside + coef[1] * up_z + coef[2] * down_z)
    w = grid.width
    return jnp.concatenate([result[:-w], result[-w:] - vent * coupled], axis=0)


def project(grid, zm, v):
    d = grid.depth
    parts = [None, None]
    for row in range(grid.rows):
        term = zm[:, row * d : (row + 1) * d].astype(F32) * v[row : row + 1, :]
        k = row % 2
        parts[k] = term if parts[k] is None else parts[k] + term
    return jnp.sum(parts[0] + parts[1], axis=1, keepdims=True)


def solve_own(inverse, column):
    size = inverse.shape[0]
    along = jnp.sum(inverse[...] * column, axis=0, keepdims=True)
    eye = lax.broadcasted_iota(jnp.int32, (size, size), 0) == lax.broadcasted_iota(
        jnp.int32, (size, size), 1
    )
    return jnp.sum(jnp.where(eye, along, 0.0), axis=1, keepdims=True)


def expand(grid, zm, column, out):
    d = grid.depth
    wide = jnp.broadcast_to(column, (column.shape[0], d))
    for row in range(grid.rows):
        out[row : row + 1, :] = jnp.sum(
            zm[:, row * d : (row + 1) * d].astype(F32) * wide, axis=0, keepdims=True
        )


def to_all(grid, pay, top, v, *more):
    block = jnp.concatenate([grid.payload(top, v), *more], axis=0)
    for slot in range(pay.shape[0]):
        pay[slot] = block


def split3(w):
    hi = w.astype(BF16)
    rest = w - hi.astype(F32)
    mid = rest.astype(BF16)
    lo = (rest - mid.astype(F32)).astype(BF16)
    return hi, mid, lo


def dot_nt(a, b):
    return lax.dot_general(a, b, (((1,), (1,)), ((), ())), preferred_element_type=F32)


def fold3(stacked):
    size = stacked.shape[0] // 3
    return stacked[:size] + (stacked[size : 2 * size] + stacked[2 * size :])


def weighted_gram(w3, parts, weights, other):
    size = other.shape[0]
    k = other.shape[1] // len(weights)
    for i, (part, weight) in enumerate(zip(parts, weights)):
        at = slice(i * k, (i + 1) * k)
        hi, mid, lo = split3(part.astype(F32) * weight)
        w3[0:size, at] = hi
        w3[size : 2 * size, at] = mid
        w3[2 * size : 3 * size, at] = lo
    return fold3(dot_nt(w3[:, : len(weights) * k], other))


def y_weights(grid, first, last):
    n, d = grid.rows, grid.depth
    row = lax.broadcasted_iota(jnp.int32, (n, d), 0)
    lane = lax.broadcasted_iota(jnp.int32, (n, d), 1)
    wide = jnp.where(lane == row, first[:, 0:1], 0.0)
    wide = wide + jnp.where(lane == n + row, last[:, d - 1 : d], 0.0)
    return jnp.sum(wide, axis=0, keepdims=True)


def invert_spd(m, ahead=5):
    size = m.shape[0]
    row_id = lax.broadcasted_iota(jnp.int32, (size, size), 0)
    col_id = lax.broadcasted_iota(jnp.int32, (size, size), 1)

    def column(k):
        return jnp.broadcast_to(m[:, k : k + 1], (size, size))

    waiting = {k: column(k) for k in range(min(ahead + 1, size))}
    for k in range(size):
        col = waiting.pop(k)
        inv = 1.0 / col[k : k + 1, :]
        for j in list(waiting):
            at_row = col[j : j + 1, :] * inv
            waiting[j] = jnp.where(row_id == k, at_row, waiting[j] - col * at_row)
        scaled_row = jnp.where(col_id[:1] == k, -inv, m[k : k + 1, :] * inv)
        m = jnp.where(row_id == k, scaled_row, jnp.where(col_id == k, 0.0, m) - col * scaled_row)
        if k + ahead + 1 < size:
            waiting[k + ahead + 1] = column(k + ahead + 1)
    return -m


def opposite(place):
    return {1: 2, 2: 1, 3: 4, 4: 3}.get(place, place)


def k_first(
    grid, material, conductivity, capacity, vent, partners, cond_out, cap_out, vent_out, pay,
    classes, cond_table, cap_table, pair_table, sems,
):
    copies = [
        pltpu.make_async_copy(src, dst, sems.at[i])
        for i, (src, dst) in enumerate(
            (
                (material, classes),
                (conductivity, cond_table),
                (capacity, cap_table),
                (vent, vent_out),
                (partners, pair_table),
            )
        )
    ]
    for copy in copies:
        copy.start()
    for copy in copies:
        copy.wait()
    cond = lookup(classes[...], cond_table)
    lane = lax.broadcasted_iota(jnp.int32, (8, grid.depth), 1)
    names = jnp.zeros((8, grid.depth), F32)
    for k in range(pair_table.shape[0]):
        names = jnp.where(lane == k, pair_table[k].astype(F32), names)
    cond_out[0 : grid.rows, :] = cond
    cond_out[grid.rows :, :] = names
    cap_out[...] = lookup(classes[...], cap_table)
    to_all(grid, pay, vent_out[...], cond, names)


def conductances(grid, cond, low_x, high_x, low_y, high_y):
    _, _, row = grid.masks()
    up_z, down_z = grid.shifted_z(cond)
    uz = jnp.where(row < grid.rows - grid.width, harmonic(cond, up_z), 0.0)
    lz = jnp.where(row >= grid.width, harmonic(cond, down_z), 0.0)
    ux, lx, uy, ly = [harmonic(cond, c) for c in grid.around(cond, low_x, high_x, low_y, high_y)]
    return uz, lz, ux, lx, uy, ly


def k_order(grid, basis, zm, panel, face, wide):
    n, d, w, layers = grid.rows, grid.depth, grid.width, grid.layers
    size = basis.shape[0]
    odd = lax.bitwise_and(lax.axis_index("row"), 1) == 1

    def unpack(a, _):
        wide[pl.ds(a * n, n), :] = basis[a].astype(F32)
        return 0

    lax.fori_loop(0, size, unpack, 0, unroll=4)
    for row in range(n):
        packed = wide[pl.ds(row, size, stride=n), :].astype(BF16)
        zm[:, row * d : (row + 1) * d] = packed
        layer, x = divmod(row, w)
        if layer == layers - 1:
            panel[:, x * d : (x + 1) * d] = packed
    for z in range(layers):
        x = jnp.where(odd, w - 1, 0)
        face[:, z * d : (z + 1) * d] = wide[pl.ds(z * w + x, size, stride=n), :].astype(BF16)


def k_basis(grid, zm, rhs, cond_ref, cap_ref, own, projected, face_y, zr, w3, coef):
    n, d, w = grid.rows, grid.depth, grid.width
    size = zm.shape[0]
    cond = cond_ref[0:n, :]
    zero_face = jnp.zeros((grid.layers, d), F32)
    zero = jnp.zeros((n, d), F32)
    uz, lz, ux, lx, uy, ly = conductances(grid, cond, zero_face, zero_face, zero, zero)
    coef[0] = cap_ref[...] + uz + lz + ux + lx + uy + ly
    for i, c in enumerate((uz, lz, ux, lx, uy, ly)):
        coef[i + 1] = c

    parts = [None, None]
    lane = lax.broadcasted_iota(jnp.int32, (size, d), 1)
    sides = jnp.zeros((size, d), F32)
    for row in range(n):
        z = zm[:, row * d : (row + 1) * d].astype(F32)
        zr[row] = z
        sides = jnp.where(lane == row, z[:, 0:1], sides)
        sides = jnp.where(lane == n + row, z[:, d - 1 : d], sides)
        term = z * rhs[row : row + 1, :]
        parts[row % 2] = term if parts[row % 2] is None else parts[row % 2] + term
    projected[...] = parts[0] + parts[1]
    face_y[...] = sides
    total = None
    for start in range(0, n, 8):
        for row in range(start, start + 8):
            z = zr[row]

            def c(i):
                return coef[i, row : row + 1, :]

            acc = c(0) * z
            if row + w < n:
                acc = acc - c(1) * zr[row + w]
            if row >= w:
                acc = acc - c(2) * zr[row - w]
            if row % w < w - 1:
                acc = acc - c(3) * zr[row + 1]
            if row % w > 0:
                acc = acc - c(4) * zr[row - 1]
            acc = acc - c(5) * pltpu.roll(z, d - 1, 1) - c(6) * pltpu.roll(z, 1, 1)
            at = slice(row * d, (row + 1) * d)
            hi, mid, lo = split3(acc)
            w3[0:size, at] = hi
            w3[size : 2 * size, at] = mid
            w3[2 * size : 3 * size, at] = lo
        part = dot_nt(w3[:, start * d : (start + 8) * d], zm[:, start * d : (start + 8) * d])
        total = part if total is None else total + part
    own[...] = fold3(total)


def pick(sources, targets, sems):
    for i, (index, target) in enumerate(targets):
        for j, source in enumerate(sources):

            @pl.when(index == j)
            def _(source=source, target=target, i=i):
                pltpu.make_async_copy(source, target, sems.at[i]).start()


def await_picks(sources, targets, sems):
    for i, (_, target) in enumerate(targets):
        pltpu.make_async_copy(sources[0], target, sems.at[i]).wait()


def fold(inverse):
    half = inverse.shape[0] // 2
    return jnp.concatenate([inverse[0:half, :], inverse[half:, :]], axis=1)


def unfold(folded):
    size = folded.shape[1] // 2
    return jnp.concatenate([folded[:, :size], folded[:, size:]], axis=0)


def k_setup(
    grid, pairs, cols, ids, cap, vent, cond, cond_low, cond_high, rec,
    zm, own_inner, projected, face_y, *rest,
):
    n, d, w, layers = grid.rows, grid.depth, grid.width, grid.layers
    held = [zm.at[:, pl.ds((n - w) * d, w * d)], *rest[:-12]]
    coef, own, inverse, sent, pay, mine, wanted, vents, names, w3, v0, sems = rest[-12:]
    count = rec.shape[0]
    panel = w * d
    line = w + 2 * layers
    sibling = lax.bitwise_xor(ids[pairs], 1)
    names_lane = lax.broadcasted_iota(jnp.int32, (1, d), 1)
    targets = []
    for k in range(pairs):
        theirs = jnp.where(names_lane == k, rec[sibling, line : line + 1, :], 0.0)
        for partner, target in (
            (ids[k], mine.at[k]),
            (jnp.sum(theirs).astype(jnp.int32), wanted.at[:, pl.ds(k * panel, panel)]),
        ):
            index = lax.shift_right_logical(lax.bitwise_xor(partner, ids[pairs]), 1)
            targets.append((index, target))
    pick(held, targets, sems)

    upward = lax.bitwise_and(ids[pairs], 1) == 0
    for z in range(layers):
        low_face = zm[:, z * panel : z * panel + d]
        high_face = zm[:, (z + 1) * panel - d : (z + 1) * panel]
        at = slice(pairs * panel + z * d, pairs * panel + (z + 1) * d)
        wanted[:, at] = jnp.where(upward, high_face.astype(F32), low_face.astype(F32)).astype(BF16)
    for k in range(pairs):
        vents[k] = vent[...] * rec[ids[k], 0:w, :]
    up, down = jnp.minimum(ids[pairs] + 1, count - 1), jnp.maximum(ids[pairs] - 1, 0)
    lines = [rec[r, line : line + 1, :] for r in (up, down)]
    lines += [cond_high[n : n + 1, :], cond_low[n : n + 1, :]]
    lines += [rec[ids[k], line : line + 1, :] for k in range(pairs)]
    names[...] = jnp.concatenate(lines, axis=0)
    vent_sum, low_x, high_x = received(grid, ids, pairs, rec)
    row_at, col_at = ids[pairs], ids[pairs + 1]
    low_x = jnp.where(row_at > 0, low_x, 0.0)
    high_x = jnp.where(row_at < count - 1, high_x, 0.0)
    low_y = jnp.where(col_at > 0, cond_low[0:n, :], 0.0)
    high_y = jnp.where(col_at < cols - 1, cond_high[0:n, :], 0.0)
    uz, lz, ux, lx, uy, ly = conductances(grid, cond[0:n, :], low_x, high_x, low_y, high_y)
    plenum = vent[...] * vent_sum
    diagonal = cap[...] + uz + lz + ux + lx + uy + ly
    coef[0] = jnp.concatenate([diagonal[:-w], diagonal[-w:] + plenum], axis=0)
    for i, c in enumerate((uz, lz, ux, lx, uy, ly)):
        coef[i + 1] = c
    last, first = [ux[z * w + w - 1 :][:1] for z in range(layers)], [lx[z * w :][:1] for z in range(layers)]
    top = [plenum[x : x + 1] for x in range(w)]
    top[0] = top[0] + first[-1]
    top[-1] = top[-1] + last[-1]
    row = n - w
    tops = zm[:, row * d :]
    block = own_inner[...] + weighted_gram(
        w3, [tops[:, x * d : (x + 1) * d] for x in range(w)], top, tops
    )
    for at, weights in ((0, first[:-1]), (panel - d, last[:-1])):
        parts = [zm[:, z * panel + at : z * panel + at + d] for z in range(layers - 1)]
        block = block + weighted_gram(w3, parts, weights, jnp.concatenate(parts, axis=1))
    sides = face_y[...].astype(BF16)
    block = block + weighted_gram(w3, [sides], [y_weights(grid, ly, uy)], sides)
    own[...] = block
    inverse[...] = invert_spd(block)
    y0 = solve_own(inverse, jnp.sum(projected[...], axis=1, keepdims=True))
    expand(grid, zm, y0, v0)
    field = v0[...]
    sent[...] = field
    to_all(grid, pay, vent[...] * field[-w:], field, fold(inverse))
    await_picks(held, targets, sems)


def incoming(grid, pairs, ids, rec, low, high):
    coupled, low_x, high_x = received(grid, ids, pairs, rec)
    n = grid.rows
    return coupled, low_x, high_x, low[0:n, :], high[0:n, :]


def k_coarse(
    grid, pairs, ids, coef, vent, zm, inverse, field, rec, low, high, face_y, _, __,
    out, wide, pay, solves, scratch,
):
    n, w = grid.rows, grid.width
    beside = operate(grid, coef, vent[...], None, incoming(grid, pairs, ids, rec, low, high))
    expand(grid, zm, solve_own(inverse, project(grid, zm, beside)), scratch)
    result = field[0:n, :] - scratch[...]
    out[...] = result
    size, half = zm.shape[0], solves.shape[1]
    wide[0:n, :] = result
    wide[n : n + size, :] = face_y[...]
    wide[n + size : n + size + half, :] = fold(inverse)
    to_all(grid, pay, vent[...] * result[-w:], result)
    first = w + 2 * grid.layers
    row_at = ids[pairs]
    solves[0] = rec[jnp.minimum(row_at + 1, rec.shape[0] - 1), first : first + half, :]
    solves[1] = rec[jnp.maximum(row_at - 1, 0), first : first + half, :]
    for k in range(pairs):
        solves[2 + k] = rec[ids[k], first : first + half, :]


def chosen(grid, pairs, ids, mine, others, k, at):
    panel = grid.width * grid.depth
    same = lax.bitwise_and(lax.bitwise_xor(ids[k], ids[pairs]), 1) == 0
    there = slice(k * panel + at.start, k * panel + at.stop)
    return jnp.where(same, mine[k, :, at].astype(F32), others[:, there].astype(F32))


def x_faces(grid, pairs, ids, others, far):
    near = others[:, pairs * grid.width * grid.depth :].astype(F32)
    across = far[...].astype(F32)
    upward = lax.bitwise_and(ids[pairs], 1) == 0
    return jnp.where(upward, near, across), jnp.where(upward, across, near)


def k_partials(
    grid, pairs, base, ids, coef, vent, field, rec, low, high, vents, zm, low2, high2, mine, others,
    far, *rest,
):
    n, d, w, layers = grid.rows, grid.depth, grid.width, grid.layers
    size = zm.shape[0]
    base_ref = rest[0] if base else None
    out, pay = rest[-2:]
    next_first, prev_last = x_faces(grid, pairs, ids, others, far)
    v = operate(grid, coef, vent[...], field[...], incoming(grid, pairs, ids, rec, low, high))
    if base:
        v = base_ref[...] - v
    out[...] = v
    face, zero = jnp.zeros((layers, d), F32), jnp.zeros((n, d), F32)
    own = operate(grid, coef, vent[...], v, (jnp.zeros((w, d), F32), face, face, zero, zero))

    def along(basis, weights):
        total = None
        for i, weight in enumerate(weights):
            term = basis[:, i * d : (i + 1) * d].astype(F32) * weight
            total = term if total is None else total + term
        return total

    even = along(zm, [own[i : i + 1] for i in range(n)])
    ux, lx, uy, ly = [coef[i] * v for i in (3, 4, 5, 6)]
    sums = [
        even,
        -along(next_first, [ux[z * w + w - 1 : z * w + w] for z in range(layers)]),
        -along(prev_last, [lx[z * w : z * w + 1] for z in range(layers)]),
    ]
    toward = pltpu.roll(y_weights(grid, ly, uy), n, 1)
    lane = lax.broadcasted_iota(jnp.int32, (1, d), 1)
    sums.append(-(high2[n : n + size, :] * jnp.where(lane < n, toward, 0.0)))
    sums.append(-(low2[n : n + size, :] * jnp.where(lane < n, 0.0, toward)))
    top = v[-w:]
    for k in range(pairs):
        weight = vents[k] * top
        total = None
        for x in range(w):
            part = chosen(grid, pairs, ids, mine, others, k, slice(x * d, (x + 1) * d))
            term = part * weight[x : x + 1]
            total = term if total is None else total + term
        sums.append(-total)
    ones = jnp.ones((8, d), F32)
    rows = [
        lax.dot_general(
            ones, q, (((1,), (1,)), ((), ())),
            precision=lax.Precision.HIGHEST, preferred_element_type=F32,
        )[0:1]
        for q in sums
    ]
    if len(rows) % 2:
        rows.append(jnp.zeros((1, size), F32))
    block = jnp.concatenate(
        [jnp.concatenate(rows[i : i + 2], axis=1) for i in range(0, len(rows), 2)], axis=0
    )
    for slot in range(pay.shape[0]):
        pay[slot] = block


def k_combine(grid, table, rec, weights, zm, base, vent, out, wide, pay, scratch):
    size = zm.shape[0]
    count = weights.shape[0]
    total = None
    for j in range(count):
        sides = [None, None]
        for i in range(count):
            at = table[j * count + i]
            line, side = divmod(opposite(i), 2)
            term = rec[at, line : line + 1, :]
            sides[side] = term if sides[side] is None else sides[side] + term
        term = weights[j] * (sides[0][:, 0:size] + sides[1][:, size : 2 * size])
        total = term if total is None else total + term
    expand(grid, zm, jnp.sum(total, axis=1, keepdims=True), scratch)
    result = base[...] - scratch[...]
    out[...] = result
    wide[0 : grid.rows, :] = result
    to_all(grid, pay, vent[...] * result[-grid.width :], result)


def k_dots(grid, pairs, ids, coef, vent, field, rec, low, high, r0, p0, i0, out, pay):
    image = operate(grid, coef, vent[...], field[...], incoming(grid, pairs, ids, rec, low, high))
    out[...] = image
    d, r, p, i = field[...], r0[...], p0[...], i0[...]
    products = (r * r, p * i, r * i, i * i, d * i, d * image)
    lane = lax.broadcasted_iota(jnp.int32, pay.shape[1:], 1)
    block = jnp.zeros(pay.shape[1:], F32)
    for k, q in enumerate(products):
        total = jnp.sum(jnp.sum(q, axis=0, keepdims=True), axis=1, keepdims=True)
        block = jnp.where(lane == k, total, block)
    for slot in range(pay.shape[0]):
        pay[slot] = block


def k_last(rec, x0, r0, p0, i0, d, image, x2, r2):
    total = rec[0]
    for slot in range(1, rec.shape[0]):
        total = total + rec[slot]
    rr, pi, ri, ii, di, dd = [total[0:1, k : k + 1] for k in range(6)]
    a1 = rr / pi
    new = rr - 2.0 * a1 * ri + a1 * a1 * ii
    grow = 1.0 + new / rr
    a2 = new / (grow * grow * pi - 2.0 * grow * a1 * di + a1 * a1 * dd)
    x2[...] = x0[...] + (a1 + a2 * grow) * p0[...] - (a2 * a1) * d[...]
    r2[...] = r0[...] - (a1 + a2 * grow) * i0[...] + (a2 * a1) * image[...]


def k_blocks(
    grid, pairs, cols, scale, ids, coef, vents, names, zm, mine, others, x_far, own, inverse,
    face_y, low2, high2, solves, _, out, weights, table, w3,
):
    n, d, w, layers = grid.rows, grid.depth, grid.width, grid.layers
    rows, size = out.shape[0], out.shape[1]
    row_at = ids[pairs]
    up, down = jnp.minimum(row_at + 1, rows - 1), jnp.maximum(row_at - 1, 0)

    col_at = ids[pairs + 1]
    lane = lax.broadcasted_iota(jnp.int32, (1, d), 1)
    near = [(row_at, col_at), (row_at + 1, col_at), (row_at - 1, col_at)]
    near += [(row_at, col_at + 1), (row_at, col_at - 1)]
    near += [(ids[k], col_at) for k in range(pairs)]
    count = len(near)
    for j, (r, c) in enumerate(near):
        places = [(r, c), (r + 1, c), (r - 1, c), (r, c + 1), (r, c - 1)]
        for k in range(pairs):
            met = ids[k]
            if j > 0:
                met = jnp.sum(jnp.where(lane == k, names[j - 1 : j, :], 0.0)).astype(jnp.int32)
            places.append((met, c))
        for i, (pr, pc) in enumerate(places):
            table[j * count + i] = lax.rem(pr + 2 * rows, rows) * cols + lax.rem(pc + 2 * cols, cols)

    def dot(a, b):
        return lax.dot_general(
            a, b, (((1,), (0,)), ((), ())),
            precision=lax.Precision.HIGHEST, preferred_element_type=F32,
        )

    ux, lx, uy, ly = coef[3], coef[4], coef[5], coef[6]
    last = [z * w + w - 1 for z in range(layers)]
    first = [z * w for z in range(layers)]

    def basis_rows(at):
        return [zm[:, i * d : (i + 1) * d] for i in at]

    next_first, prev_last = [f.astype(BF16) for f in x_faces(grid, pairs, ids, others, x_far)]
    found = [
        weighted_gram(w3, basis_rows(last), [-ux[i : i + 1] for i in last], next_first),
        weighted_gram(w3, basis_rows(first), [-lx[i : i + 1] for i in first], prev_last),
    ]
    toward = -pltpu.roll(y_weights(grid, ly, uy), n, 1)
    swapped = pltpu.roll(face_y[...], n, 1)
    for theirs, there in ((high2, lane < n), (low2, lane >= n)):
        weight = jnp.where(there, toward, 0.0)
        found.append(weighted_gram(w3, [swapped], [weight], theirs[n : n + size, :].astype(BF16)))
    top = basis_rows(range(n - w, n))
    for k in range(pairs):
        panel = chosen(grid, pairs, ids, mine, others, k, slice(0, w * d)).astype(BF16)
        found.append(weighted_gram(w3, top, [-vents[k, i : i + 1, :] for i in range(w)], panel))

    for slot in range(rows):
        out[slot] = jnp.zeros((size, size), F32)
    out[row_at] = own[...] * scale
    out[up] = out[up] + jnp.where(row_at < rows - 1, found[0] * scale, 0.0)
    out[down] = out[down] + jnp.where(row_at > 0, found[1] * scale, 0.0)
    for k in range(pairs):
        out[ids[k]] = out[ids[k]] + found[4 + k] * scale

    weights[0] = inverse[...]
    start, stop = n + size, n + size + size // 2
    folded = [solves[0], solves[1], high2[start:stop, :], low2[start:stop, :]]
    folded += [solves[2 + k] for k in range(pairs)]
    for j, (block, theirs) in enumerate(zip(found, folded)):
        weights[j + 1] = -dot(inverse[...], dot(block, unfold(theirs)))


def call(kernel, outs, operands, scratch=(), smem=0, free=(), smem_outs=(), cost=None):
    specs = [
        SMEM if i < smem else ANY if i in free else VMEM for i in range(len(operands))
    ]
    return pl.pallas_call(
        kernel,
        out_shape=tuple(jax.ShapeDtypeStruct(s, t) for s, t in outs),
        in_specs=specs,
        out_specs=tuple(SMEM if i in smem_outs else VMEM for i in range(len(outs))),
        scratch_shapes=list(scratch),
        compiler_params=pltpu.CompilerParams(vmem_limit_bytes=VMEM_LIMIT),
        cost_estimate=cost,
    )(*operands)


def body(forcing_right_hand, material, capacity, conductivity, vent_open, partners, subspace_basis):
    layers, width, depth = forcing_right_hand.shape
    size = subspace_basis.shape[0]
    grid = Grid(layers, width, depth)
    n, cells = grid.rows, forcing_right_hand.size
    row_count, col_count = lax.axis_size("row"), lax.axis_size("col")
    pairs = partners.shape[-1]
    ids = jnp.concatenate(
        [
            partners.reshape(-1),
            jnp.stack([lax.axis_index("row"), lax.axis_index("col")]).astype(jnp.int32),
        ]
    )
    rhs = forcing_right_hand.reshape(n, depth)
    classes = material.reshape(n, depth)
    basis = subspace_basis.reshape(size, n, depth)
    field = ((n, depth), F32)
    pay = ((row_count, width + 2 * layers, depth), F32)
    small = ((size, size), F32)
    wide = ((max(n + size + size // 2, row_count * (width + 2 * layers) + 8), depth), F32)

    def cyclic(value, axis, step):
        count = lax.axis_size(axis)
        return lax.ppermute(value, axis, [(i, (i + step) % count) for i in range(count)])

    def xor_step(value, axis, k):
        count = lax.axis_size(axis)
        return lax.ppermute(value, axis, [(i, i ^ k) for i in range(count)])

    def exchange(value, payload):
        low = cyclic(value, "col", 1)
        high = cyclic(value, "col", -1)
        rec = lax.all_to_all(payload, "row", 0, 0)
        return rec, low, high

    def rows_of(count):
        return ((row_count, width + 2 * layers + count, depth), F32)

    zm, panel, face = call(
        functools.partial(k_order, grid),
        (
            ((size, n * depth), BF16),
            ((size, width * depth), BF16),
            ((size, layers * depth), BF16),
        ),
        (basis,),
        scratch=(pltpu.VMEM((size * n, depth), F32),),
        cost=pl.CostEstimate(flops=1000, bytes_accessed=1000, transcendentals=0),
    )
    held = [xor_step(panel, "row", k) for k in range(2, row_count, 2)]
    x_far = lax.ppermute(
        face,
        "row",
        [(i, (i + 1 if i % 2 else i - 1) % row_count) for i in range(row_count)],
    )
    cond, cap, vent, pay0 = call(
        functools.partial(k_first, grid),
        (((n + 8, depth), F32), field, ((width, depth), F32), rows_of(8)),
        (classes, conductivity, capacity, vent_open, partners.reshape(-1)),
        scratch=(
            pltpu.VMEM((n, depth), jnp.int32),
            pltpu.SMEM(conductivity.shape, F32),
            pltpu.SMEM(capacity.shape, F32),
            pltpu.SMEM((pairs,), jnp.int32),
            pltpu.SemaphoreType.DMA((5,)),
        ),
        free=(0, 1, 2, 3, 4),
    )
    rec0, cond_low, cond_high = exchange(cond, pay0)

    own_inner, projected, face_y = call(
        functools.partial(k_basis, grid),
        (small, ((size, depth), F32), ((size, depth), F32)),
        (zm, rhs, cond, cap),
        scratch=(
            pltpu.VMEM((n, size, depth), F32),
            pltpu.VMEM((3 * size, n * depth), BF16),
            pltpu.VMEM((7, n, depth), F32),
        ),
        cost=pl.CostEstimate(flops=1000, bytes_accessed=1000, transcendentals=0),
    )

    panels = ((pairs, size, width * depth), BF16)
    coef, own, inverse, sent, pay1, mine, wanted, vents, names = call(
        functools.partial(k_setup, grid, pairs, col_count),
        (
            ((7, n, depth), F32),
            small,
            small,
            field,
            rows_of(size // 2),
            panels,
            ((size, (pairs * width + layers) * depth), BF16),
            ((pairs, width, depth), F32),
            ((4 + pairs, depth), F32),
        ),
        (
            ids, cap, vent, cond, cond_low, cond_high, rec0, zm, own_inner, projected, face_y,
            *held,
        ),
        scratch=(
            pltpu.VMEM((3 * size, n * depth), BF16),
            pltpu.VMEM((n, depth), F32),
            pltpu.SemaphoreType.DMA((2 * pairs,)),
        ),
        smem=1,
        free=range(11, 11 + len(held)),
    )
    others = xor_step(wanted, "row", 1)
    rec1, low1, high1 = exchange(sent, pay1)
    places = 5 + pairs
    x0, wide2, pay2, solves = call(
        functools.partial(k_coarse, grid, pairs),
        (field, wide, pay, ((2 + pairs, size // 2, depth), F32)),
        (ids, coef, vent, zm, inverse, sent, rec1, low1, high1, face_y, others, x_far),
        scratch=(pltpu.VMEM((n, depth), F32),),
        smem=1,
        free=(10, 11),
    )
    rec, low2, high2 = exchange(wide2, pay2)

    def everyone(lines):
        return ((row_count * col_count, lines, depth), F32)

    r0, pay3 = call(
        functools.partial(k_partials, grid, pairs, True),
        (field, everyone((places + 1) // 2)),
        (
            ids, coef, vent, x0, rec, low2, high2, vents, zm, low2, high2, mine, others, x_far, rhs,
        ),
        smem=1,
    )
    blocks, weights, table = call(
        functools.partial(k_blocks, grid, pairs, col_count, 1.0 / cells),
        (
            ((row_count, size, size), F32),
            ((places, size, size), F32),
            ((places * places,), jnp.int32),
        ),
        (
            ids, coef, vents, names, zm, mine, others, x_far, own, inverse, face_y, low2,
            high2, solves, pay3,
        ),
        scratch=(pltpu.VMEM((3 * size, width * depth), BF16),),
        smem=1,
        free=(14,),
        smem_outs=(2,),
        cost=pl.CostEstimate(flops=100_000_000, bytes_accessed=4_000_000, transcendentals=0),
    )
    sums = lax.all_to_all(pay3, ("row", "col"), 0, 0)
    p0, wide4, pay4 = call(
        functools.partial(k_combine, grid),
        (field, wide, pay),
        (table, sums, weights, zm, r0, vent),
        scratch=(pltpu.VMEM((n, depth), F32),),
        smem=1,
    )
    rec, low, high = exchange(wide4, pay4)
    i0, pay5 = call(
        functools.partial(k_partials, grid, pairs, False),
        (field, everyone((places + 1) // 2)),
        (
            ids, coef, vent, p0, rec, low, high, vents, zm, low2, high2, mine, others, x_far,
        ),
        smem=1,
    )
    sums = lax.all_to_all(pay5, ("row", "col"), 0, 0)
    d0, wide6, pay6 = call(
        functools.partial(k_combine, grid),
        (field, wide, pay),
        (table, sums, weights, zm, i0, vent),
        scratch=(pltpu.VMEM((n, depth), F32),),
        smem=1,
    )
    rec, low, high = exchange(wide6, pay6)
    image, pay7 = call(
        functools.partial(k_dots, grid, pairs),
        (field, everyone(2)),
        (ids, coef, vent, d0, rec, low, high, r0, p0, i0),
        smem=1,
    )
    total = lax.all_to_all(pay7, ("row", "col"), 0, 0)
    x2, r2 = call(k_last, (field, field), (total, x0, r0, p0, i0, d0, image))
    shape = forcing_right_hand.shape
    return x2.reshape(shape), r2.reshape(shape), blocks[None, None]


def solution(mesh):
    return jax.shard_map(
        body,
        mesh=mesh,
        in_specs=(
            P(None, "row", "col"),
            P(None, "row", "col"),
            P(),
            P(),
            P("row", "col"),
            P("row", "col", None),
            P(None, None, "row", "col"),
        ),
        out_specs=(P(None, "row", "col"), P(None, "row", "col"), P("row", "col", None, None, None)),
        check_vma=False,
    )
```

```python
import functools

import jax
import jax.numpy as jnp
from jax import lax
from jax.experimental import pallas as pl
from jax.experimental.pallas import tpu as pltpu
from jax.sharding import PartitionSpec as P

F32 = jnp.float32
BF16 = jnp.bfloat16
VMEM = pl.BlockSpec(memory_space=pltpu.VMEM)
SMEM = pl.BlockSpec(memory_space=pltpu.SMEM)
ANY = pl.BlockSpec(memory_space=pl.ANY)
VMEM_LIMIT = 16 * 1024 * 1024


def harmonic(a, b):
    return 2.0 * a * b / (a + b)


def lookup(material, table):
    result = jnp.zeros(material.shape, F32)
    for class_id in range(table.shape[0]):
        result = jnp.where(material == class_id, table[class_id], result)
    return result


class Grid:
    def __init__(self, layers, width, depth):
        self.layers, self.width, self.depth = layers, width, depth
        self.rows = layers * width

    def masks(self):
        shape = (self.rows, self.depth)
        row = lax.broadcasted_iota(jnp.int32, shape, 0)
        lane = lax.broadcasted_iota(jnp.int32, shape, 1)
        return lax.rem(row, self.width), lane, row

    def spread(self, face):
        parts = [
            jnp.broadcast_to(face[z : z + 1], (self.width, self.depth)) for z in range(self.layers)
        ]
        return jnp.concatenate(parts, axis=0)

    def faces(self, v):
        w = self.width
        last = [v[z * w + w - 1 : z * w + w] for z in range(self.layers)]
        first = [v[z * w : z * w + 1] for z in range(self.layers)]
        return last + first

    def payload(self, top, v):
        return jnp.concatenate([top] + self.faces(v), axis=0)

    def around(self, v, low_x, high_x, low_y, high_y):
        xi, lane, _ = self.masks()
        n, d = self.rows, self.depth
        zero = jnp.zeros((n, d), F32)
        own = zero if v is None else v
        plus = zero if v is None else pltpu.roll(v, n - 1, 0)
        minus = zero if v is None else pltpu.roll(v, 1, 0)
        up_x = jnp.where(xi == self.width - 1, self.spread(high_x), plus)
        down_x = jnp.where(xi == 0, self.spread(low_x), minus)
        up_y = pltpu.roll(jnp.where(lane == 0, high_y, own), d - 1, 1)
        down_y = pltpu.roll(jnp.where(lane == d - 1, low_y, own), 1, 1)
        return up_x, down_x, up_y, down_y

    def shifted_z(self, v):
        w = self.width
        return jnp.concatenate([v[w:], v[:w]], axis=0), jnp.concatenate([v[-w:], v[:-w]], axis=0)


def received(grid, ids, pairs, rec):
    count = rec.shape[0]
    w, layers = grid.width, grid.layers
    coupled = rec[ids[0], 0:w, :]
    for k in range(1, pairs):
        coupled = coupled + rec[ids[k], 0:w, :]
    row_at = ids[pairs]
    low = rec[jnp.maximum(row_at - 1, 0), w : w + layers, :]
    high = rec[jnp.minimum(row_at + 1, count - 1), w + layers : w + 2 * layers, :]
    return coupled, low, high


def operate(grid, coef, vent, v, rest):
    coupled, low_x, high_x, low_y, high_y = rest
    up_x, down_x, up_y, down_y = grid.around(v, low_x, high_x, low_y, high_y)
    beside = coef[3] * up_x + coef[4] * down_x + coef[5] * up_y + coef[6] * down_y
    if v is None:
        xi, lane, _ = grid.masks()
        result = -beside
    else:
        up_z, down_z = grid.shifted_z(v)
        result = coef[0] * v - (beside + coef[1] * up_z + coef[2] * down_z)
    w = grid.width
    return jnp.concatenate([result[:-w], result[-w:] - vent * coupled], axis=0)


def project(grid, zm, v):
    d = grid.depth
    parts = [None, None]
    for row in range(grid.rows):
        term = zm[:, row * d : (row + 1) * d].astype(F32) * v[row : row + 1, :]
        k = row % 2
        parts[k] = term if parts[k] is None else parts[k] + term
    return jnp.sum(parts[0] + parts[1], axis=1, keepdims=True)


def solve_own(inverse, column):
    size = inverse.shape[0]
    along = jnp.sum(inverse[...] * column, axis=0, keepdims=True)
    eye = lax.broadcasted_iota(jnp.int32, (size, size), 0) == lax.broadcasted_iota(
        jnp.int32, (size, size), 1
    )
    return jnp.sum(jnp.where(eye, along, 0.0), axis=1, keepdims=True)


def expand(grid, zm, column, out):
    d = grid.depth
    wide = jnp.broadcast_to(column, (column.shape[0], d))
    for row in range(grid.rows):
        out[row : row + 1, :] = jnp.sum(
            zm[:, row * d : (row + 1) * d].astype(F32) * wide, axis=0, keepdims=True
        )


def to_all(grid, pay, top, v, *more):
    block = jnp.concatenate([grid.payload(top, v), *more], axis=0)
    for slot in range(pay.shape[0]):
        pay[slot] = block


def split3(w):
    hi = w.astype(BF16)
    rest = w - hi.astype(F32)
    mid = rest.astype(BF16)
    lo = (rest - mid.astype(F32)).astype(BF16)
    return hi, mid, lo


def dot_nt(a, b):
    return lax.dot_general(a, b, (((1,), (1,)), ((), ())), preferred_element_type=F32)


def fold3(stacked):
    size = stacked.shape[0] // 3
    return stacked[:size] + (stacked[size : 2 * size] + stacked[2 * size :])


def weighted_gram(w3, parts, weights, other):
    size = other.shape[0]
    k = other.shape[1] // len(weights)
    for i, (part, weight) in enumerate(zip(parts, weights)):
        at = slice(i * k, (i + 1) * k)
        hi, mid, lo = split3(part.astype(F32) * weight)
        w3[0:size, at] = hi
        w3[size : 2 * size, at] = mid
        w3[2 * size : 3 * size, at] = lo
    return fold3(dot_nt(w3[:, : len(weights) * k], other))


def y_weights(grid, first, last):
    n, d = grid.rows, grid.depth
    row = lax.broadcasted_iota(jnp.int32, (n, d), 0)
    lane = lax.broadcasted_iota(jnp.int32, (n, d), 1)
    wide = jnp.where(lane == row, first[:, 0:1], 0.0)
    wide = wide + jnp.where(lane == n + row, last[:, d - 1 : d], 0.0)
    return jnp.sum(wide, axis=0, keepdims=True)


def invert_spd(m, ahead=5):
    size = m.shape[0]
    row_id = lax.broadcasted_iota(jnp.int32, (size, size), 0)
    col_id = lax.broadcasted_iota(jnp.int32, (size, size), 1)

    def column(k):
        return jnp.broadcast_to(m[:, k : k + 1], (size, size))

    waiting = {k: column(k) for k in range(min(ahead + 1, size))}
    for k in range(size):
        col = waiting.pop(k)
        inv = 1.0 / col[k : k + 1, :]
        for j in list(waiting):
            at_row = col[j : j + 1, :] * inv
            waiting[j] = jnp.where(row_id == k, at_row, waiting[j] - col * at_row)
        scaled_row = jnp.where(col_id[:1] == k, -inv, m[k : k + 1, :] * inv)
        m = jnp.where(row_id == k, scaled_row, jnp.where(col_id == k, 0.0, m) - col * scaled_row)
        if k + ahead + 1 < size:
            waiting[k + ahead + 1] = column(k + ahead + 1)
    return -m


def opposite(place):
    return {1: 2, 2: 1, 3: 4, 4: 3}.get(place, place)


def k_first(
    grid, conductivity, capacity, partners, material, vent, cond_out, cap_out, vent_out, pay
):
    cond = lookup(material[...], conductivity)
    lane = lax.broadcasted_iota(jnp.int32, (8, grid.depth), 1)
    names = jnp.zeros((8, grid.depth), F32)
    for k in range(partners.shape[0]):
        names = jnp.where(lane == k, partners[k].astype(F32), names)
    cond_out[0 : grid.rows, :] = cond
    cond_out[grid.rows :, :] = names
    cap_out[...] = lookup(material[...], capacity)
    vent_out[...] = vent[...]
    to_all(grid, pay, vent[...], cond, names)


def conductances(grid, cond, low_x, high_x, low_y, high_y):
    _, _, row = grid.masks()
    up_z, down_z = grid.shifted_z(cond)
    uz = jnp.where(row < grid.rows - grid.width, harmonic(cond, up_z), 0.0)
    lz = jnp.where(row >= grid.width, harmonic(cond, down_z), 0.0)
    ux, lx, uy, ly = [harmonic(cond, c) for c in grid.around(cond, low_x, high_x, low_y, high_y)]
    return uz, lz, ux, lx, uy, ly


def k_order(grid, basis, zm, panel, face):
    n, d, w, layers = grid.rows, grid.depth, grid.width, grid.layers
    size = basis.shape[0]
    odd = lax.bitwise_and(lax.axis_index("row"), 1) == 1

    for row in range(0, n, w):
        for a in range(0, size, w):
            turned = jnp.swapaxes(basis[a : a + w, row : row + w, :], 0, 1)
            for i in range(w):
                zm[a : a + w, (row + i) * d : (row + i + 1) * d] = turned[i]
    panel[...] = zm[:, (n - w) * d :]
    for z in range(layers):
        start = z * w * d
        first = zm[:, start : start + d].astype(F32)
        last = zm[:, start + (w - 1) * d : start + w * d].astype(F32)
        face[:, z * d : (z + 1) * d] = jnp.where(odd, last, first).astype(BF16)


def k_basis(grid, zm, rhs, cond_ref, cap_ref, own, projected, face_y, zr, w3, coef):
    n, d, w = grid.rows, grid.depth, grid.width
    size = zm.shape[0]
    cond = cond_ref[0:n, :]
    zero_face = jnp.zeros((grid.layers, d), F32)
    zero = jnp.zeros((n, d), F32)
    uz, lz, ux, lx, uy, ly = conductances(grid, cond, zero_face, zero_face, zero, zero)
    coef[0] = cap_ref[...] + uz + lz + ux + lx + uy + ly
    for i, c in enumerate((uz, lz, ux, lx, uy, ly)):
        coef[i + 1] = c

    parts = [None, None]
    lane = lax.broadcasted_iota(jnp.int32, (size, d), 1)
    sides = jnp.zeros((size, d), F32)
    for row in range(n):
        z = zm[:, row * d : (row + 1) * d].astype(F32)
        zr[row] = z
        sides = jnp.where(lane == row, z[:, 0:1], sides)
        sides = jnp.where(lane == n + row, z[:, d - 1 : d], sides)
        term = z * rhs[row : row + 1, :]
        parts[row % 2] = term if parts[row % 2] is None else parts[row % 2] + term
    projected[...] = parts[0] + parts[1]
    face_y[...] = sides
    total = None
    for start in range(0, n, 8):
        for row in range(start, start + 8):
            z = zr[row]

            def c(i):
                return coef[i, row : row + 1, :]

            acc = c(0) * z
            if row + w < n:
                acc = acc - c(1) * zr[row + w]
            if row >= w:
                acc = acc - c(2) * zr[row - w]
            if row % w < w - 1:
                acc = acc - c(3) * zr[row + 1]
            if row % w > 0:
                acc = acc - c(4) * zr[row - 1]
            acc = acc - c(5) * pltpu.roll(z, d - 1, 1) - c(6) * pltpu.roll(z, 1, 1)
            at = slice(row * d, (row + 1) * d)
            hi, mid, lo = split3(acc)
            w3[0:size, at] = hi
            w3[size : 2 * size, at] = mid
            w3[2 * size : 3 * size, at] = lo
        part = dot_nt(w3[:, start * d : (start + 8) * d], zm[:, start * d : (start + 8) * d])
        total = part if total is None else total + part
    own[...] = fold3(total)


def pick(sources, targets, sems):
    for i, (index, target) in enumerate(targets):
        for j, source in enumerate(sources):

            @pl.when(index == j)
            def _(source=source, target=target, i=i):
                pltpu.make_async_copy(source, target, sems.at[i]).start()


def await_picks(sources, targets, sems):
    for i, (_, target) in enumerate(targets):
        pltpu.make_async_copy(sources[0], target, sems.at[i]).wait()


def fold(inverse):
    half = inverse.shape[0] // 2
    return jnp.concatenate([inverse[0:half, :], inverse[half:, :]], axis=1)


def unfold(folded):
    size = folded.shape[1] // 2
    return jnp.concatenate([folded[:, :size], folded[:, size:]], axis=0)


def k_setup(
    grid, pairs, cols, ids, cap, vent, cond, cond_low, cond_high, rec,
    zm, own_inner, projected, face_y, *rest,
):
    n, d, w, layers = grid.rows, grid.depth, grid.width, grid.layers
    held = [zm.at[:, pl.ds((n - w) * d, w * d)], *rest[:-12]]
    coef, own, inverse, sent, pay, mine, wanted, vents, names, w3, v0, sems = rest[-12:]
    count = rec.shape[0]
    panel = w * d
    line = w + 2 * layers
    sibling = lax.bitwise_xor(ids[pairs], 1)
    names_lane = lax.broadcasted_iota(jnp.int32, (1, d), 1)
    targets = []
    for k in range(pairs):
        theirs = jnp.where(names_lane == k, rec[sibling, line : line + 1, :], 0.0)
        for partner, target in (
            (ids[k], mine.at[k]),
            (jnp.sum(theirs).astype(jnp.int32), wanted.at[:, pl.ds(k * panel, panel)]),
        ):
            index = lax.shift_right_logical(lax.bitwise_xor(partner, ids[pairs]), 1)
            targets.append((index, target))
    pick(held, targets, sems)

    upward = lax.bitwise_and(ids[pairs], 1) == 0
    for z in range(layers):
        low_face = zm[:, z * panel : z * panel + d]
        high_face = zm[:, (z + 1) * panel - d : (z + 1) * panel]
        at = slice(pairs * panel + z * d, pairs * panel + (z + 1) * d)
        wanted[:, at] = jnp.where(upward, high_face.astype(F32), low_face.astype(F32)).astype(BF16)
    for k in range(pairs):
        vents[k] = vent[...] * rec[ids[k], 0:w, :]
    up, down = jnp.minimum(ids[pairs] + 1, count - 1), jnp.maximum(ids[pairs] - 1, 0)
    lines = [rec[r, line : line + 1, :] for r in (up, down)]
    lines += [cond_high[n : n + 1, :], cond_low[n : n + 1, :]]
    lines += [rec[ids[k], line : line + 1, :] for k in range(pairs)]
    names[...] = jnp.concatenate(lines, axis=0)
    vent_sum, low_x, high_x = received(grid, ids, pairs, rec)
    row_at, col_at = ids[pairs], ids[pairs + 1]
    low_x = jnp.where(row_at > 0, low_x, 0.0)
    high_x = jnp.where(row_at < count - 1, high_x, 0.0)
    low_y = jnp.where(col_at > 0, cond_low[0:n, :], 0.0)
    high_y = jnp.where(col_at < cols - 1, cond_high[0:n, :], 0.0)
    uz, lz, ux, lx, uy, ly = conductances(grid, cond[0:n, :], low_x, high_x, low_y, high_y)
    plenum = vent[...] * vent_sum
    diagonal = cap[...] + uz + lz + ux + lx + uy + ly
    coef[0] = jnp.concatenate([diagonal[:-w], diagonal[-w:] + plenum], axis=0)
    for i, c in enumerate((uz, lz, ux, lx, uy, ly)):
        coef[i + 1] = c
    last, first = [ux[z * w + w - 1 :][:1] for z in range(layers)], [lx[z * w :][:1] for z in range(layers)]
    top = [plenum[x : x + 1] for x in range(w)]
    top[0] = top[0] + first[-1]
    top[-1] = top[-1] + last[-1]
    row = n - w
    tops = zm[:, row * d :]
    block = own_inner[...] + weighted_gram(
        w3, [tops[:, x * d : (x + 1) * d] for x in range(w)], top, tops
    )
    for at, weights in ((0, first[:-1]), (panel - d, last[:-1])):
        parts = [zm[:, z * panel + at : z * panel + at + d] for z in range(layers - 1)]
        block = block + weighted_gram(w3, parts, weights, jnp.concatenate(parts, axis=1))
    sides = face_y[...].astype(BF16)
    block = block + weighted_gram(w3, [sides], [y_weights(grid, ly, uy)], sides)
    own[...] = block
    inverse[...] = invert_spd(block)
    y0 = solve_own(inverse, jnp.sum(projected[...], axis=1, keepdims=True))
    expand(grid, zm, y0, v0)
    field = v0[...]
    sent[...] = field
    to_all(grid, pay, vent[...] * field[-w:], field, fold(inverse))
    await_picks(held, targets, sems)


def incoming(grid, pairs, ids, rec, low, high):
    coupled, low_x, high_x = received(grid, ids, pairs, rec)
    n = grid.rows
    return coupled, low_x, high_x, low[0:n, :], high[0:n, :]


def k_coarse(
    grid, pairs, ids, coef, vent, zm, inverse, field, rec, low, high, face_y, _, __,
    out, wide, pay, solves, scratch,
):
    n, w = grid.rows, grid.width
    beside = operate(grid, coef, vent[...], None, incoming(grid, pairs, ids, rec, low, high))
    expand(grid, zm, solve_own(inverse, project(grid, zm, beside)), scratch)
    result = field[0:n, :] - scratch[...]
    out[...] = result
    size, half = zm.shape[0], solves.shape[1]
    wide[0:n, :] = result
    wide[n : n + size, :] = face_y[...]
    wide[n + size : n + size + half, :] = fold(inverse)
    to_all(grid, pay, vent[...] * result[-w:], result)
    first = w + 2 * grid.layers
    row_at = ids[pairs]
    solves[0] = rec[jnp.minimum(row_at + 1, rec.shape[0] - 1), first : first + half, :]
    solves[1] = rec[jnp.maximum(row_at - 1, 0), first : first + half, :]
    for k in range(pairs):
        solves[2 + k] = rec[ids[k], first : first + half, :]


def chosen(grid, pairs, ids, mine, others, k, at):
    panel = grid.width * grid.depth
    same = lax.bitwise_and(lax.bitwise_xor(ids[k], ids[pairs]), 1) == 0
    there = slice(k * panel + at.start, k * panel + at.stop)
    return jnp.where(same, mine[k, :, at].astype(F32), others[:, there].astype(F32))


def x_faces(grid, pairs, ids, others, far):
    near = others[:, pairs * grid.width * grid.depth :].astype(F32)
    across = far[...].astype(F32)
    upward = lax.bitwise_and(ids[pairs], 1) == 0
    return jnp.where(upward, near, across), jnp.where(upward, across, near)


def k_partials(
    grid, pairs, base, ids, coef, vent, field, rec, low, high, vents, zm, low2, high2, mine, others,
    far, *rest,
):
    n, d, w, layers = grid.rows, grid.depth, grid.width, grid.layers
    size = zm.shape[0]
    base_ref = rest[0] if base else None
    out, pay = rest[-2:]
    next_first, prev_last = x_faces(grid, pairs, ids, others, far)
    v = operate(grid, coef, vent[...], field[...], incoming(grid, pairs, ids, rec, low, high))
    if base:
        v = base_ref[...] - v
    out[...] = v
    face, zero = jnp.zeros((layers, d), F32), jnp.zeros((n, d), F32)
    own = operate(grid, coef, vent[...], v, (jnp.zeros((w, d), F32), face, face, zero, zero))

    def along(basis, weights):
        total = None
        for i, weight in enumerate(weights):
            term = basis[:, i * d : (i + 1) * d].astype(F32) * weight
            total = term if total is None else total + term
        return total

    even = along(zm, [own[i : i + 1] for i in range(n)])
    ux, lx, uy, ly = [coef[i] * v for i in (3, 4, 5, 6)]
    sums = [
        even,
        -along(next_first, [ux[z * w + w - 1 : z * w + w] for z in range(layers)]),
        -along(prev_last, [lx[z * w : z * w + 1] for z in range(layers)]),
    ]
    toward = pltpu.roll(y_weights(grid, ly, uy), n, 1)
    lane = lax.broadcasted_iota(jnp.int32, (1, d), 1)
    sums.append(-(high2[n : n + size, :] * jnp.where(lane < n, toward, 0.0)))
    sums.append(-(low2[n : n + size, :] * jnp.where(lane < n, 0.0, toward)))
    top = v[-w:]
    for k in range(pairs):
        weight = vents[k] * top
        total = None
        for x in range(w):
            part = chosen(grid, pairs, ids, mine, others, k, slice(x * d, (x + 1) * d))
            term = part * weight[x : x + 1]
            total = term if total is None else total + term
        sums.append(-total)
    eye = lax.broadcasted_iota(jnp.int32, (size, size), 0) == lax.broadcasted_iota(
        jnp.int32, (size, size), 1
    )
    rows = [
        jnp.sum(
            jnp.where(eye, jnp.sum(q, axis=1, keepdims=True), 0.0), axis=0, keepdims=True
        )
        for q in sums
    ]
    if len(rows) % 2:
        rows.append(jnp.zeros((1, size), F32))
    block = jnp.concatenate(
        [jnp.concatenate(rows[i : i + 2], axis=1) for i in range(0, len(rows), 2)], axis=0
    )
    for slot in range(pay.shape[0]):
        pay[slot] = block


def k_combine(grid, table, rec, weights, zm, base, vent, out, wide, pay, scratch):
    size = zm.shape[0]
    count = weights.shape[0]
    total = None
    for j in range(count):
        sides = [None, None]
        for i in range(count):
            at = table[j * count + i]
            line, side = divmod(opposite(i), 2)
            term = rec[at, line : line + 1, :]
            sides[side] = term if sides[side] is None else sides[side] + term
        term = weights[j] * (sides[0][:, 0:size] + sides[1][:, size : 2 * size])
        total = term if total is None else total + term
    expand(grid, zm, jnp.sum(total, axis=1, keepdims=True), scratch)
    result = base[...] - scratch[...]
    out[...] = result
    wide[0 : grid.rows, :] = result
    to_all(grid, pay, vent[...] * result[-grid.width :], result)


def k_dots(grid, pairs, ids, coef, vent, field, rec, low, high, r0, p0, i0, out, pay):
    image = operate(grid, coef, vent[...], field[...], incoming(grid, pairs, ids, rec, low, high))
    out[...] = image
    d, r, p, i = field[...], r0[...], p0[...], i0[...]
    products = (r * r, p * i, r * i, i * i, d * i, d * image)
    lane = lax.broadcasted_iota(jnp.int32, pay.shape[1:], 1)
    block = jnp.zeros(pay.shape[1:], F32)
    for k, q in enumerate(products):
        total = jnp.sum(jnp.sum(q, axis=0, keepdims=True), axis=1, keepdims=True)
        block = jnp.where(lane == k, total, block)
    for slot in range(pay.shape[0]):
        pay[slot] = block


def k_last(rec, x0, r0, p0, i0, d, image, x2, r2):
    total = rec[0]
    for slot in range(1, rec.shape[0]):
        total = total + rec[slot]
    rr, pi, ri, ii, di, dd = [total[0:1, k : k + 1] for k in range(6)]
    a1 = rr / pi
    new = rr - 2.0 * a1 * ri + a1 * a1 * ii
    grow = 1.0 + new / rr
    a2 = new / (grow * grow * pi - 2.0 * grow * a1 * di + a1 * a1 * dd)
    x2[...] = x0[...] + (a1 + a2 * grow) * p0[...] - (a2 * a1) * d[...]
    r2[...] = r0[...] - (a1 + a2 * grow) * i0[...] + (a2 * a1) * image[...]


def k_blocks(
    grid, pairs, cols, scale, ids, coef, vents, names, zm, mine, others, x_far, own, inverse,
    face_y, low2, high2, solves, _, out, weights, table, w3,
):
    n, d, w, layers = grid.rows, grid.depth, grid.width, grid.layers
    rows, size = out.shape[0], out.shape[1]
    row_at = ids[pairs]
    up, down = jnp.minimum(row_at + 1, rows - 1), jnp.maximum(row_at - 1, 0)

    col_at = ids[pairs + 1]
    lane = lax.broadcasted_iota(jnp.int32, (1, d), 1)
    near = [(row_at, col_at), (row_at + 1, col_at), (row_at - 1, col_at)]
    near += [(row_at, col_at + 1), (row_at, col_at - 1)]
    near += [(ids[k], col_at) for k in range(pairs)]
    count = len(near)
    for j, (r, c) in enumerate(near):
        places = [(r, c), (r + 1, c), (r - 1, c), (r, c + 1), (r, c - 1)]
        for k in range(pairs):
            met = ids[k]
            if j > 0:
                met = jnp.sum(jnp.where(lane == k, names[j - 1 : j, :], 0.0)).astype(jnp.int32)
            places.append((met, c))
        for i, (pr, pc) in enumerate(places):
            table[j * count + i] = lax.rem(pr + 2 * rows, rows) * cols + lax.rem(pc + 2 * cols, cols)

    def dot(a, b):
        return lax.dot_general(
            a, b, (((1,), (0,)), ((), ())),
            precision=lax.Precision.HIGHEST, preferred_element_type=F32,
        )

    ux, lx, uy, ly = coef[3], coef[4], coef[5], coef[6]
    last = [z * w + w - 1 for z in range(layers)]
    first = [z * w for z in range(layers)]

    def basis_rows(at):
        return [zm[:, i * d : (i + 1) * d] for i in at]

    next_first, prev_last = [f.astype(BF16) for f in x_faces(grid, pairs, ids, others, x_far)]
    found = [
        weighted_gram(w3, basis_rows(last), [-ux[i : i + 1] for i in last], next_first),
        weighted_gram(w3, basis_rows(first), [-lx[i : i + 1] for i in first], prev_last),
    ]
    toward = -pltpu.roll(y_weights(grid, ly, uy), n, 1)
    swapped = pltpu.roll(face_y[...], n, 1)
    for theirs, there in ((high2, lane < n), (low2, lane >= n)):
        weight = jnp.where(there, toward, 0.0)
        found.append(weighted_gram(w3, [swapped], [weight], theirs[n : n + size, :].astype(BF16)))
    top = basis_rows(range(n - w, n))
    for k in range(pairs):
        panel = chosen(grid, pairs, ids, mine, others, k, slice(0, w * d)).astype(BF16)
        found.append(weighted_gram(w3, top, [-vents[k, i : i + 1, :] for i in range(w)], panel))

    for slot in range(rows):
        out[slot] = jnp.zeros((size, size), F32)
    out[row_at] = own[...] * scale
    out[up] = out[up] + jnp.where(row_at < rows - 1, found[0] * scale, 0.0)
    out[down] = out[down] + jnp.where(row_at > 0, found[1] * scale, 0.0)
    for k in range(pairs):
        out[ids[k]] = out[ids[k]] + found[4 + k] * scale

    weights[0] = inverse[...]
    start, stop = n + size, n + size + size // 2
    folded = [solves[0], solves[1], high2[start:stop, :], low2[start:stop, :]]
    folded += [solves[2 + k] for k in range(pairs)]
    for j, (block, theirs) in enumerate(zip(found, folded)):
        weights[j + 1] = -dot(inverse[...], dot(block, unfold(theirs)))


def call(kernel, outs, operands, scratch=(), smem=0, free=(), smem_outs=(), cost=None):
    specs = [
        SMEM if i < smem else ANY if i in free else VMEM for i in range(len(operands))
    ]
    return pl.pallas_call(
        kernel,
        out_shape=tuple(jax.ShapeDtypeStruct(s, t) for s, t in outs),
        in_specs=specs,
        out_specs=tuple(SMEM if i in smem_outs else VMEM for i in range(len(outs))),
        scratch_shapes=list(scratch),
        compiler_params=pltpu.CompilerParams(vmem_limit_bytes=VMEM_LIMIT),
        cost_estimate=cost,
    )(*operands)


def body(forcing_right_hand, material, capacity, conductivity, vent_open, partners, subspace_basis):
    layers, width, depth = forcing_right_hand.shape
    size = subspace_basis.shape[0]
    grid = Grid(layers, width, depth)
    n, cells = grid.rows, forcing_right_hand.size
    row_count, col_count = lax.axis_size("row"), lax.axis_size("col")
    pairs = partners.shape[-1]
    ids = jnp.concatenate(
        [
            partners.reshape(-1),
            jnp.stack([lax.axis_index("row"), lax.axis_index("col")]).astype(jnp.int32),
        ]
    )
    rhs = forcing_right_hand.reshape(n, depth)
    classes = material.reshape(n, depth)
    basis = subspace_basis.reshape(size, n, depth)
    field = ((n, depth), F32)
    pay = ((row_count, width + 2 * layers, depth), F32)
    small = ((size, size), F32)
    wide = ((max(n + size + size // 2, row_count * (width + 2 * layers) + 8), depth), F32)

    def cyclic(value, axis, step):
        count = lax.axis_size(axis)
        return lax.ppermute(value, axis, [(i, (i + step) % count) for i in range(count)])

    def xor_step(value, axis, k):
        count = lax.axis_size(axis)
        return lax.ppermute(value, axis, [(i, i ^ k) for i in range(count)])

    def exchange(value, payload):
        low = cyclic(value, "col", 1)
        high = cyclic(value, "col", -1)
        rec = lax.all_to_all(payload, "row", 0, 0)
        return rec, low, high

    def rows_of(count):
        return ((row_count, width + 2 * layers + count, depth), F32)

    zm, panel, face = call(
        functools.partial(k_order, grid),
        (
            ((size, n * depth), BF16),
            ((size, width * depth), BF16),
            ((size, layers * depth), BF16),
        ),
        (basis,),
        cost=pl.CostEstimate(flops=1000, bytes_accessed=1000, transcendentals=0),
    )
    held = [xor_step(panel, "row", k) for k in range(2, row_count, 2)]
    x_far = lax.ppermute(
        face,
        "row",
        [(i, (i + 1 if i % 2 else i - 1) % row_count) for i in range(row_count)],
    )
    cond, cap, vent, pay0 = call(
        functools.partial(k_first, grid),
        (((n + 8, depth), F32), field, ((width, depth), F32), rows_of(8)),
        (conductivity, capacity, partners.reshape(-1), classes, vent_open),
        smem=3,
    )
    rec0, cond_low, cond_high = exchange(cond, pay0)

    own_inner, projected, face_y = call(
        functools.partial(k_basis, grid),
        (small, ((size, depth), F32), ((size, depth), F32)),
        (zm, rhs, cond, cap),
        scratch=(
            pltpu.VMEM((n, size, depth), F32),
            pltpu.VMEM((3 * size, n * depth), BF16),
            pltpu.VMEM((7, n, depth), F32),
        ),
        cost=pl.CostEstimate(flops=1000, bytes_accessed=1000, transcendentals=0),
    )

    panels = ((pairs, size, width * depth), BF16)
    coef, own, inverse, sent, pay1, mine, wanted, vents, names = call(
        functools.partial(k_setup, grid, pairs, col_count),
        (
            ((7, n, depth), F32),
            small,
            small,
            field,
            rows_of(size // 2),
            panels,
            ((size, (pairs * width + layers) * depth), BF16),
            ((pairs, width, depth), F32),
            ((4 + pairs, depth), F32),
        ),
        (
            ids, cap, vent, cond, cond_low, cond_high, rec0, zm, own_inner, projected, face_y,
            *held,
        ),
        scratch=(
            pltpu.VMEM((3 * size, n * depth), BF16),
            pltpu.VMEM((n, depth), F32),
            pltpu.SemaphoreType.DMA((2 * pairs,)),
        ),
        smem=1,
        free=range(11, 11 + len(held)),
    )
    others = xor_step(wanted, "row", 1)
    rec1, low1, high1 = exchange(sent, pay1)
    places = 5 + pairs
    x0, wide2, pay2, solves = call(
        functools.partial(k_coarse, grid, pairs),
        (field, wide, pay, ((2 + pairs, size // 2, depth), F32)),
        (ids, coef, vent, zm, inverse, sent, rec1, low1, high1, face_y, others, x_far),
        scratch=(pltpu.VMEM((n, depth), F32),),
        smem=1,
        free=(10, 11),
    )
    rec, low2, high2 = exchange(wide2, pay2)

    def everyone(lines):
        return ((row_count * col_count, lines, depth), F32)

    r0, pay3 = call(
        functools.partial(k_partials, grid, pairs, True),
        (field, everyone((places + 1) // 2)),
        (
            ids, coef, vent, x0, rec, low2, high2, vents, zm, low2, high2, mine, others, x_far, rhs,
        ),
        smem=1,
    )
    blocks, weights, table = call(
        functools.partial(k_blocks, grid, pairs, col_count, 1.0 / cells),
        (
            ((row_count, size, size), F32),
            ((places, size, size), F32),
            ((places * places,), jnp.int32),
        ),
        (
            ids, coef, vents, names, zm, mine, others, x_far, own, inverse, face_y, low2,
            high2, solves, pay3,
        ),
        scratch=(pltpu.VMEM((3 * size, width * depth), BF16),),
        smem=1,
        free=(14,),
        smem_outs=(2,),
        cost=pl.CostEstimate(flops=100_000_000, bytes_accessed=4_000_000, transcendentals=0),
    )
    sums = lax.all_to_all(pay3, ("row", "col"), 0, 0)
    p0, wide4, pay4 = call(
        functools.partial(k_combine, grid),
        (field, wide, pay),
        (table, sums, weights, zm, r0, vent),
        scratch=(pltpu.VMEM((n, depth), F32),),
        smem=1,
    )
    rec, low, high = exchange(wide4, pay4)
    i0, pay5 = call(
        functools.partial(k_partials, grid, pairs, False),
        (field, everyone((places + 1) // 2)),
        (
            ids, coef, vent, p0, rec, low, high, vents, zm, low2, high2, mine, others, x_far,
        ),
        smem=1,
    )
    sums = lax.all_to_all(pay5, ("row", "col"), 0, 0)
    d0, wide6, pay6 = call(
        functools.partial(k_combine, grid),
        (field, wide, pay),
        (table, sums, weights, zm, i0, vent),
        scratch=(pltpu.VMEM((n, depth), F32),),
        smem=1,
    )
    rec, low, high = exchange(wide6, pay6)
    image, pay7 = call(
        functools.partial(k_dots, grid, pairs),
        (field, everyone(2)),
        (ids, coef, vent, d0, rec, low, high, r0, p0, i0),
        smem=1,
    )
    total = lax.all_to_all(pay7, ("row", "col"), 0, 0)
    x2, r2 = call(k_last, (field, field), (total, x0, r0, p0, i0, d0, image))
    shape = forcing_right_hand.shape
    return x2.reshape(shape), r2.reshape(shape), blocks[None, None]


def solution(mesh):
    return jax.shard_map(
        body,
        mesh=mesh,
        in_specs=(
            P(None, "row", "col"),
            P(None, "row", "col"),
            P(),
            P(),
            P("row", "col"),
            P("row", "col", None),
            P(None, None, "row", "col"),
        ),
        out_specs=(P(None, "row", "col"), P(None, "row", "col"), P("row", "col", None, None, None)),
        check_vma=False,
    )
```

```python
import functools

import jax
import jax.numpy as jnp
from jax import lax
from jax.experimental import pallas as pl
from jax.experimental.pallas import tpu as pltpu
from jax.sharding import PartitionSpec as P

F32 = jnp.float32
BF16 = jnp.bfloat16
VMEM = pl.BlockSpec(memory_space=pltpu.VMEM)
SMEM = pl.BlockSpec(memory_space=pltpu.SMEM)
ANY = pl.BlockSpec(memory_space=pl.ANY)
VMEM_LIMIT = 16 * 1024 * 1024


def harmonic(a, b):
    return 2.0 * a * b / (a + b)


def lookup(material, table):
    result = jnp.zeros(material.shape, F32)
    for class_id in range(len(table)):
        result = jnp.where(material == class_id, table[class_id], result)
    return result


class Grid:
    def __init__(self, layers, width, depth):
        self.layers, self.width, self.depth = layers, width, depth
        self.rows = layers * width

    def masks(self):
        shape = (self.rows, self.depth)
        row = lax.broadcasted_iota(jnp.int32, shape, 0)
        lane = lax.broadcasted_iota(jnp.int32, shape, 1)
        return lax.rem(row, self.width), lane, row

    def spread(self, face):
        parts = [
            jnp.broadcast_to(face[z : z + 1], (self.width, self.depth)) for z in range(self.layers)
        ]
        return jnp.concatenate(parts, axis=0)

    def faces(self, v):
        w = self.width
        last = [v[z * w + w - 1 : z * w + w] for z in range(self.layers)]
        first = [v[z * w : z * w + 1] for z in range(self.layers)]
        return last + first

    def payload(self, top, v):
        return jnp.concatenate([top] + self.faces(v), axis=0)

    def around(self, v, low_x, high_x, low_y, high_y):
        xi, lane, _ = self.masks()
        n, d = self.rows, self.depth
        zero = jnp.zeros((n, d), F32)
        own = zero if v is None else v
        plus = zero if v is None else pltpu.roll(v, n - 1, 0)
        minus = zero if v is None else pltpu.roll(v, 1, 0)
        up_x = jnp.where(xi == self.width - 1, self.spread(high_x), plus)
        down_x = jnp.where(xi == 0, self.spread(low_x), minus)
        up_y = pltpu.roll(jnp.where(lane == 0, high_y, own), d - 1, 1)
        down_y = pltpu.roll(jnp.where(lane == d - 1, low_y, own), 1, 1)
        return up_x, down_x, up_y, down_y

    def shifted_z(self, v):
        w = self.width
        return jnp.concatenate([v[w:], v[:w]], axis=0), jnp.concatenate([v[-w:], v[:-w]], axis=0)


def received(grid, ids, pairs, rec):
    count = rec.shape[0]
    w, layers = grid.width, grid.layers
    coupled = rec[ids[0], 0:w, :]
    for k in range(1, pairs):
        coupled = coupled + rec[ids[k], 0:w, :]
    row_at = ids[pairs]
    low = rec[jnp.maximum(row_at - 1, 0), w : w + layers, :]
    high = rec[jnp.minimum(row_at + 1, count - 1), w + layers : w + 2 * layers, :]
    return coupled, low, high


def operate(grid, coef, vent, v, rest):
    coupled, low_x, high_x, low_y, high_y = rest
    up_x, down_x, up_y, down_y = grid.around(v, low_x, high_x, low_y, high_y)
    beside = coef[3] * up_x + coef[4] * down_x + coef[5] * up_y + coef[6] * down_y
    if v is None:
        xi, lane, _ = grid.masks()
        result = -beside
    else:
        up_z, down_z = grid.shifted_z(v)
        result = coef[0] * v - (beside + coef[1] * up_z + coef[2] * down_z)
    w = grid.width
    return jnp.concatenate([result[:-w], result[-w:] - vent * coupled], axis=0)


def project(grid, zm, v):
    d = grid.depth
    parts = [None, None]
    for row in range(grid.rows):
        term = zm[:, row * d : (row + 1) * d].astype(F32) * v[row : row + 1, :]
        k = row % 2
        parts[k] = term if parts[k] is None else parts[k] + term
    return jnp.sum(parts[0] + parts[1], axis=1, keepdims=True)


def solve_own(inverse, column):
    size = inverse.shape[0]
    along = jnp.sum(inverse[...] * column, axis=0, keepdims=True)
    eye = lax.broadcasted_iota(jnp.int32, (size, size), 0) == lax.broadcasted_iota(
        jnp.int32, (size, size), 1
    )
    return jnp.sum(jnp.where(eye, along, 0.0), axis=1, keepdims=True)


def expand(grid, zm, column, out):
    d = grid.depth
    wide = jnp.broadcast_to(column, (column.shape[0], d))
    for row in range(grid.rows):
        out[row : row + 1, :] = jnp.sum(
            zm[:, row * d : (row + 1) * d].astype(F32) * wide, axis=0, keepdims=True
        )


def to_all(grid, pay, top, v, *more):
    block = jnp.concatenate([grid.payload(top, v), *more], axis=0)
    for slot in range(pay.shape[0]):
        pay[slot] = block


def split3(w):
    hi = w.astype(BF16)
    rest = w - hi.astype(F32)
    mid = rest.astype(BF16)
    lo = (rest - mid.astype(F32)).astype(BF16)
    return hi, mid, lo


def dot_nt(a, b):
    return lax.dot_general(a, b, (((1,), (1,)), ((), ())), preferred_element_type=F32)


def fold3(stacked):
    size = stacked.shape[0] // 3
    return stacked[:size] + (stacked[size : 2 * size] + stacked[2 * size :])


def weighted_gram(w3, parts, weights, other):
    size = other.shape[0]
    k = other.shape[1] // len(weights)
    for i, (part, weight) in enumerate(zip(parts, weights)):
        at = slice(i * k, (i + 1) * k)
        hi, mid, lo = split3(part.astype(F32) * weight)
        w3[0:size, at] = hi
        w3[size : 2 * size, at] = mid
        w3[2 * size : 3 * size, at] = lo
    return fold3(dot_nt(w3[:, : len(weights) * k], other))


def y_weights(grid, first, last):
    n, d = grid.rows, grid.depth
    row = lax.broadcasted_iota(jnp.int32, (n, d), 0)
    lane = lax.broadcasted_iota(jnp.int32, (n, d), 1)
    wide = jnp.where(lane == row, first[:, 0:1], 0.0)
    wide = wide + jnp.where(lane == n + row, last[:, d - 1 : d], 0.0)
    return jnp.sum(wide, axis=0, keepdims=True)


def invert_spd(m, ahead=5):
    size = m.shape[0]
    row_id = lax.broadcasted_iota(jnp.int32, (size, size), 0)
    col_id = lax.broadcasted_iota(jnp.int32, (size, size), 1)

    def column(k):
        return jnp.broadcast_to(m[:, k : k + 1], (size, size))

    waiting = {k: column(k) for k in range(min(ahead + 1, size))}
    for k in range(size):
        col = waiting.pop(k)
        inv = 1.0 / col[k : k + 1, :]
        for j in list(waiting):
            at_row = col[j : j + 1, :] * inv
            waiting[j] = jnp.where(row_id == k, at_row, waiting[j] - col * at_row)
        scaled_row = jnp.where(col_id[:1] == k, -inv, m[k : k + 1, :] * inv)
        m = jnp.where(row_id == k, scaled_row, jnp.where(col_id == k, 0.0, m) - col * scaled_row)
        if k + ahead + 1 < size:
            waiting[k + ahead + 1] = column(k + ahead + 1)
    return -m


def opposite(place):
    return {1: 2, 2: 1, 3: 4, 4: 3}.get(place, place)


def k_first(
    grid, pairs, tables, material, vent, cond_out, cap_out, vent_out, pay
):
    classes = (tables.shape[0] - pairs) // 2
    conductivity = [tables[i] for i in range(classes)]
    capacity = [tables[classes + i] for i in range(classes)]
    cond = lookup(material[...], conductivity)
    lane = lax.broadcasted_iota(jnp.int32, (8, grid.depth), 1)
    names = jnp.zeros((8, grid.depth), F32)
    for k in range(pairs):
        names = jnp.where(lane == k, tables[2 * classes + k], names)
    cond_out[0 : grid.rows, :] = cond
    cond_out[grid.rows :, :] = names
    cap_out[...] = lookup(material[...], capacity)
    vent_out[...] = vent[...]
    to_all(grid, pay, vent[...], cond, names)


def conductances(grid, cond, low_x, high_x, low_y, high_y):
    _, _, row = grid.masks()
    up_z, down_z = grid.shifted_z(cond)
    uz = jnp.where(row < grid.rows - grid.width, harmonic(cond, up_z), 0.0)
    lz = jnp.where(row >= grid.width, harmonic(cond, down_z), 0.0)
    ux, lx, uy, ly = [harmonic(cond, c) for c in grid.around(cond, low_x, high_x, low_y, high_y)]
    return uz, lz, ux, lx, uy, ly


def k_order(grid, basis, zm, panel, face):
    n, d, w, layers = grid.rows, grid.depth, grid.width, grid.layers
    size = basis.shape[0]
    odd = lax.bitwise_and(lax.axis_index("row"), 1) == 1

    for row in range(0, n, w):
        for a in range(0, size, w):
            turned = jnp.swapaxes(basis[a : a + w, row : row + w, :], 0, 1)
            for i in range(w):
                zm[a : a + w, (row + i) * d : (row + i + 1) * d] = turned[i]
    panel[...] = zm[:, (n - w) * d :]
    for z in range(layers):
        start = z * w * d
        first = zm[:, start : start + d].astype(F32)
        last = zm[:, start + (w - 1) * d : start + w * d].astype(F32)
        face[:, z * d : (z + 1) * d] = jnp.where(odd, last, first).astype(BF16)


def k_basis(grid, zm, rhs, cond_ref, cap_ref, own, projected, face_y, zr, w3, coef):
    n, d, w = grid.rows, grid.depth, grid.width
    size = zm.shape[0]
    cond = cond_ref[0:n, :]
    zero_face = jnp.zeros((grid.layers, d), F32)
    zero = jnp.zeros((n, d), F32)
    uz, lz, ux, lx, uy, ly = conductances(grid, cond, zero_face, zero_face, zero, zero)
    coef[0] = cap_ref[...] + uz + lz + ux + lx + uy + ly
    for i, c in enumerate((uz, lz, ux, lx, uy, ly)):
        coef[i + 1] = c

    parts = [None, None]
    lane = lax.broadcasted_iota(jnp.int32, (size, d), 1)
    sides = jnp.zeros((size, d), F32)
    for row in range(n):
        z = zm[:, row * d : (row + 1) * d].astype(F32)
        zr[row] = z
        sides = jnp.where(lane == row, z[:, 0:1], sides)
        sides = jnp.where(lane == n + row, z[:, d - 1 : d], sides)
        term = z * rhs[row : row + 1, :]
        parts[row % 2] = term if parts[row % 2] is None else parts[row % 2] + term
    projected[...] = parts[0] + parts[1]
    face_y[...] = sides
    total = None
    for start in range(0, n, 8):
        for row in range(start, start + 8):
            z = zr[row]

            def c(i):
                return coef[i, row : row + 1, :]

            acc = c(0) * z
            if row + w < n:
                acc = acc - c(1) * zr[row + w]
            if row >= w:
                acc = acc - c(2) * zr[row - w]
            if row % w < w - 1:
                acc = acc - c(3) * zr[row + 1]
            if row % w > 0:
                acc = acc - c(4) * zr[row - 1]
            acc = acc - c(5) * pltpu.roll(z, d - 1, 1) - c(6) * pltpu.roll(z, 1, 1)
            at = slice(row * d, (row + 1) * d)
            hi, mid, lo = split3(acc)
            w3[0:size, at] = hi
            w3[size : 2 * size, at] = mid
            w3[2 * size : 3 * size, at] = lo
        part = dot_nt(w3[:, start * d : (start + 8) * d], zm[:, start * d : (start + 8) * d])
        total = part if total is None else total + part
    own[...] = fold3(total)


def pick(sources, targets, sems):
    for i, (index, target) in enumerate(targets):
        for j, source in enumerate(sources):

            @pl.when(index == j)
            def _(source=source, target=target, i=i):
                pltpu.make_async_copy(source, target, sems.at[i]).start()


def await_picks(sources, targets, sems):
    for i, (_, target) in enumerate(targets):
        pltpu.make_async_copy(sources[0], target, sems.at[i]).wait()


def fold(inverse):
    half = inverse.shape[0] // 2
    return jnp.concatenate([inverse[0:half, :], inverse[half:, :]], axis=1)


def unfold(folded):
    size = folded.shape[1] // 2
    return jnp.concatenate([folded[:, :size], folded[:, size:]], axis=0)


def k_setup(
    grid, pairs, cols, ids, cap, vent, cond, cond_low, cond_high, rec,
    zm, own_inner, projected, face_y, *rest,
):
    n, d, w, layers = grid.rows, grid.depth, grid.width, grid.layers
    held = [zm.at[:, pl.ds((n - w) * d, w * d)], *rest[:-12]]
    coef, own, inverse, sent, pay, mine, wanted, vents, names, w3, v0, sems = rest[-12:]
    count = rec.shape[0]
    panel = w * d
    line = w + 2 * layers
    sibling = lax.bitwise_xor(ids[pairs], 1)
    names_lane = lax.broadcasted_iota(jnp.int32, (1, d), 1)
    targets = []
    for k in range(pairs):
        theirs = jnp.where(names_lane == k, rec[sibling, line : line + 1, :], 0.0)
        for partner, target in (
            (ids[k], mine.at[k]),
            (jnp.sum(theirs).astype(jnp.int32), wanted.at[:, pl.ds(k * panel, panel)]),
        ):
            index = lax.shift_right_logical(lax.bitwise_xor(partner, ids[pairs]), 1)
            targets.append((index, target))
    pick(held, targets, sems)

    upward = lax.bitwise_and(ids[pairs], 1) == 0
    for z in range(layers):
        low_face = zm[:, z * panel : z * panel + d]
        high_face = zm[:, (z + 1) * panel - d : (z + 1) * panel]
        at = slice(pairs * panel + z * d, pairs * panel + (z + 1) * d)
        wanted[:, at] = jnp.where(upward, high_face.astype(F32), low_face.astype(F32)).astype(BF16)
    for k in range(pairs):
        vents[k] = vent[...] * rec[ids[k], 0:w, :]
    up, down = jnp.minimum(ids[pairs] + 1, count - 1), jnp.maximum(ids[pairs] - 1, 0)
    lines = [rec[r, line : line + 1, :] for r in (up, down)]
    lines += [cond_high[n : n + 1, :], cond_low[n : n + 1, :]]
    lines += [rec[ids[k], line : line + 1, :] for k in range(pairs)]
    names[...] = jnp.concatenate(lines, axis=0)
    vent_sum, low_x, high_x = received(grid, ids, pairs, rec)
    row_at, col_at = ids[pairs], ids[pairs + 1]
    low_x = jnp.where(row_at > 0, low_x, 0.0)
    high_x = jnp.where(row_at < count - 1, high_x, 0.0)
    low_y = jnp.where(col_at > 0, cond_low[0:n, :], 0.0)
    high_y = jnp.where(col_at < cols - 1, cond_high[0:n, :], 0.0)
    uz, lz, ux, lx, uy, ly = conductances(grid, cond[0:n, :], low_x, high_x, low_y, high_y)
    plenum = vent[...] * vent_sum
    diagonal = cap[...] + uz + lz + ux + lx + uy + ly
    coef[0] = jnp.concatenate([diagonal[:-w], diagonal[-w:] + plenum], axis=0)
    for i, c in enumerate((uz, lz, ux, lx, uy, ly)):
        coef[i + 1] = c
    last, first = [ux[z * w + w - 1 :][:1] for z in range(layers)], [lx[z * w :][:1] for z in range(layers)]
    top = [plenum[x : x + 1] for x in range(w)]
    top[0] = top[0] + first[-1]
    top[-1] = top[-1] + last[-1]
    row = n - w
    tops = zm[:, row * d :]
    block = own_inner[...] + weighted_gram(
        w3, [tops[:, x * d : (x + 1) * d] for x in range(w)], top, tops
    )
    for at, weights in ((0, first[:-1]), (panel - d, last[:-1])):
        parts = [zm[:, z * panel + at : z * panel + at + d] for z in range(layers - 1)]
        block = block + weighted_gram(w3, parts, weights, jnp.concatenate(parts, axis=1))
    sides = face_y[...].astype(BF16)
    block = block + weighted_gram(w3, [sides], [y_weights(grid, ly, uy)], sides)
    own[...] = block
    inverse[...] = invert_spd(block)
    y0 = solve_own(inverse, jnp.sum(projected[...], axis=1, keepdims=True))
    expand(grid, zm, y0, v0)
    field = v0[...]
    sent[...] = field
    to_all(grid, pay, vent[...] * field[-w:], field, fold(inverse))
    await_picks(held, targets, sems)


def incoming(grid, pairs, ids, rec, low, high):
    coupled, low_x, high_x = received(grid, ids, pairs, rec)
    n = grid.rows
    return coupled, low_x, high_x, low[0:n, :], high[0:n, :]


def k_coarse(
    grid, pairs, ids, coef, vent, zm, inverse, field, rec, low, high, face_y, _, __,
    out, wide, pay, solves, scratch,
):
    n, w = grid.rows, grid.width
    beside = operate(grid, coef, vent[...], None, incoming(grid, pairs, ids, rec, low, high))
    expand(grid, zm, solve_own(inverse, project(grid, zm, beside)), scratch)
    result = field[0:n, :] - scratch[...]
    out[...] = result
    size, half = zm.shape[0], solves.shape[1]
    wide[0:n, :] = result
    wide[n : n + size, :] = face_y[...]
    wide[n + size : n + size + half, :] = fold(inverse)
    to_all(grid, pay, vent[...] * result[-w:], result)
    first = w + 2 * grid.layers
    row_at = ids[pairs]
    solves[0] = rec[jnp.minimum(row_at + 1, rec.shape[0] - 1), first : first + half, :]
    solves[1] = rec[jnp.maximum(row_at - 1, 0), first : first + half, :]
    for k in range(pairs):
        solves[2 + k] = rec[ids[k], first : first + half, :]


def chosen(grid, pairs, ids, mine, others, k, at):
    panel = grid.width * grid.depth
    same = lax.bitwise_and(lax.bitwise_xor(ids[k], ids[pairs]), 1) == 0
    there = slice(k * panel + at.start, k * panel + at.stop)
    return jnp.where(same, mine[k, :, at].astype(F32), others[:, there].astype(F32))


def x_faces(grid, pairs, ids, others, far):
    near = others[:, pairs * grid.width * grid.depth :].astype(F32)
    across = far[...].astype(F32)
    upward = lax.bitwise_and(ids[pairs], 1) == 0
    return jnp.where(upward, near, across), jnp.where(upward, across, near)


def k_partials(
    grid, pairs, base, ids, coef, vent, field, rec, low, high, vents, zm, low2, high2, mine, others,
    far, *rest,
):
    n, d, w, layers = grid.rows, grid.depth, grid.width, grid.layers
    size = zm.shape[0]
    base_ref = rest[0] if base else None
    out, pay = rest[-2:]
    next_first, prev_last = x_faces(grid, pairs, ids, others, far)
    v = operate(grid, coef, vent[...], field[...], incoming(grid, pairs, ids, rec, low, high))
    if base:
        v = base_ref[...] - v
    out[...] = v
    face, zero = jnp.zeros((layers, d), F32), jnp.zeros((n, d), F32)
    own = operate(grid, coef, vent[...], v, (jnp.zeros((w, d), F32), face, face, zero, zero))

    def along(basis, weights):
        total = None
        for i, weight in enumerate(weights):
            term = basis[:, i * d : (i + 1) * d].astype(F32) * weight
            total = term if total is None else total + term
        return total

    even = along(zm, [own[i : i + 1] for i in range(n)])
    ux, lx, uy, ly = [coef[i] * v for i in (3, 4, 5, 6)]
    sums = [
        even,
        -along(next_first, [ux[z * w + w - 1 : z * w + w] for z in range(layers)]),
        -along(prev_last, [lx[z * w : z * w + 1] for z in range(layers)]),
    ]
    toward = pltpu.roll(y_weights(grid, ly, uy), n, 1)
    lane = lax.broadcasted_iota(jnp.int32, (1, d), 1)
    sums.append(-(high2[n : n + size, :] * jnp.where(lane < n, toward, 0.0)))
    sums.append(-(low2[n : n + size, :] * jnp.where(lane < n, 0.0, toward)))
    top = v[-w:]
    for k in range(pairs):
        weight = vents[k] * top
        total = None
        for x in range(w):
            part = chosen(grid, pairs, ids, mine, others, k, slice(x * d, (x + 1) * d))
            term = part * weight[x : x + 1]
            total = term if total is None else total + term
        sums.append(-total)
    eye = lax.broadcasted_iota(jnp.int32, (size, size), 0) == lax.broadcasted_iota(
        jnp.int32, (size, size), 1
    )
    rows = [
        jnp.sum(
            jnp.where(eye, jnp.sum(q, axis=1, keepdims=True), 0.0), axis=0, keepdims=True
        )
        for q in sums
    ]
    if len(rows) % 2:
        rows.append(jnp.zeros((1, size), F32))
    block = jnp.concatenate(
        [jnp.concatenate(rows[i : i + 2], axis=1) for i in range(0, len(rows), 2)], axis=0
    )
    for slot in range(pay.shape[0]):
        pay[slot] = block


def k_combine(grid, table, rec, weights, zm, base, vent, out, wide, pay, scratch):
    size = zm.shape[0]
    count = weights.shape[0]
    total = None
    for j in range(count):
        sides = [None, None]
        for i in range(count):
            at = table[j * count + i]
            line, side = divmod(opposite(i), 2)
            term = rec[at, line : line + 1, :]
            sides[side] = term if sides[side] is None else sides[side] + term
        term = weights[j] * (sides[0][:, 0:size] + sides[1][:, size : 2 * size])
        total = term if total is None else total + term
    expand(grid, zm, jnp.sum(total, axis=1, keepdims=True), scratch)
    result = base[...] - scratch[...]
    out[...] = result
    wide[0 : grid.rows, :] = result
    to_all(grid, pay, vent[...] * result[-grid.width :], result)


def k_dots(grid, pairs, ids, coef, vent, field, rec, low, high, r0, p0, i0, out, pay):
    image = operate(grid, coef, vent[...], field[...], incoming(grid, pairs, ids, rec, low, high))
    out[...] = image
    d, r, p, i = field[...], r0[...], p0[...], i0[...]
    products = (r * r, p * i, r * i, i * i, d * i, d * image)
    lane = lax.broadcasted_iota(jnp.int32, pay.shape[1:], 1)
    block = jnp.zeros(pay.shape[1:], F32)
    for k, q in enumerate(products):
        total = jnp.sum(jnp.sum(q, axis=0, keepdims=True), axis=1, keepdims=True)
        block = jnp.where(lane == k, total, block)
    for slot in range(pay.shape[0]):
        pay[slot] = block


def k_last(rec, x0, r0, p0, i0, d, image, x2, r2):
    total = rec[0]
    for slot in range(1, rec.shape[0]):
        total = total + rec[slot]
    rr, pi, ri, ii, di, dd = [total[0:1, k : k + 1] for k in range(6)]
    a1 = rr / pi
    new = rr - 2.0 * a1 * ri + a1 * a1 * ii
    grow = 1.0 + new / rr
    a2 = new / (grow * grow * pi - 2.0 * grow * a1 * di + a1 * a1 * dd)
    x2[...] = x0[...] + (a1 + a2 * grow) * p0[...] - (a2 * a1) * d[...]
    r2[...] = r0[...] - (a1 + a2 * grow) * i0[...] + (a2 * a1) * image[...]


def k_blocks(
    grid, pairs, cols, scale, ids, coef, vents, names, zm, mine, others, x_far, own, inverse,
    face_y, low2, high2, solves, _, out, weights, table, w3,
):
    n, d, w, layers = grid.rows, grid.depth, grid.width, grid.layers
    rows, size = out.shape[0], out.shape[1]
    row_at = ids[pairs]
    up, down = jnp.minimum(row_at + 1, rows - 1), jnp.maximum(row_at - 1, 0)

    col_at = ids[pairs + 1]
    lane = lax.broadcasted_iota(jnp.int32, (1, d), 1)
    near = [(row_at, col_at), (row_at + 1, col_at), (row_at - 1, col_at)]
    near += [(row_at, col_at + 1), (row_at, col_at - 1)]
    near += [(ids[k], col_at) for k in range(pairs)]
    count = len(near)
    for j, (r, c) in enumerate(near):
        places = [(r, c), (r + 1, c), (r - 1, c), (r, c + 1), (r, c - 1)]
        for k in range(pairs):
            met = ids[k]
            if j > 0:
                met = jnp.sum(jnp.where(lane == k, names[j - 1 : j, :], 0.0)).astype(jnp.int32)
            places.append((met, c))
        for i, (pr, pc) in enumerate(places):
            table[j * count + i] = lax.rem(pr + 2 * rows, rows) * cols + lax.rem(pc + 2 * cols, cols)

    def dot(a, b):
        return lax.dot_general(
            a, b, (((1,), (0,)), ((), ())),
            precision=lax.Precision.HIGHEST, preferred_element_type=F32,
        )

    ux, lx, uy, ly = coef[3], coef[4], coef[5], coef[6]
    last = [z * w + w - 1 for z in range(layers)]
    first = [z * w for z in range(layers)]

    def basis_rows(at):
        return [zm[:, i * d : (i + 1) * d] for i in at]

    next_first, prev_last = [f.astype(BF16) for f in x_faces(grid, pairs, ids, others, x_far)]
    found = [
        weighted_gram(w3, basis_rows(last), [-ux[i : i + 1] for i in last], next_first),
        weighted_gram(w3, basis_rows(first), [-lx[i : i + 1] for i in first], prev_last),
    ]
    toward = -pltpu.roll(y_weights(grid, ly, uy), n, 1)
    swapped = pltpu.roll(face_y[...], n, 1)
    for theirs, there in ((high2, lane < n), (low2, lane >= n)):
        weight = jnp.where(there, toward, 0.0)
        found.append(weighted_gram(w3, [swapped], [weight], theirs[n : n + size, :].astype(BF16)))
    top = basis_rows(range(n - w, n))
    for k in range(pairs):
        panel = chosen(grid, pairs, ids, mine, others, k, slice(0, w * d)).astype(BF16)
        found.append(weighted_gram(w3, top, [-vents[k, i : i + 1, :] for i in range(w)], panel))

    for slot in range(rows):
        out[slot] = jnp.zeros((size, size), F32)
    out[row_at] = own[...] * scale
    out[up] = out[up] + jnp.where(row_at < rows - 1, found[0] * scale, 0.0)
    out[down] = out[down] + jnp.where(row_at > 0, found[1] * scale, 0.0)
    for k in range(pairs):
        out[ids[k]] = out[ids[k]] + found[4 + k] * scale

    weights[0] = inverse[...]
    start, stop = n + size, n + size + size // 2
    folded = [solves[0], solves[1], high2[start:stop, :], low2[start:stop, :]]
    folded += [solves[2 + k] for k in range(pairs)]
    for j, (block, theirs) in enumerate(zip(found, folded)):
        weights[j + 1] = -dot(inverse[...], dot(block, unfold(theirs)))


def call(kernel, outs, operands, scratch=(), smem=0, free=(), smem_outs=(), cost=None):
    specs = [
        SMEM if i < smem else ANY if i in free else VMEM for i in range(len(operands))
    ]
    return pl.pallas_call(
        kernel,
        out_shape=tuple(jax.ShapeDtypeStruct(s, t) for s, t in outs),
        in_specs=specs,
        out_specs=tuple(SMEM if i in smem_outs else VMEM for i in range(len(outs))),
        scratch_shapes=list(scratch),
        compiler_params=pltpu.CompilerParams(vmem_limit_bytes=VMEM_LIMIT),
        cost_estimate=cost,
    )(*operands)


def body(forcing_right_hand, material, capacity, conductivity, vent_open, partners, subspace_basis):
    layers, width, depth = forcing_right_hand.shape
    size = subspace_basis.shape[0]
    grid = Grid(layers, width, depth)
    n, cells = grid.rows, forcing_right_hand.size
    row_count, col_count = lax.axis_size("row"), lax.axis_size("col")
    pairs = partners.shape[-1]
    ids = jnp.concatenate(
        [
            partners.reshape(-1),
            jnp.stack([lax.axis_index("row"), lax.axis_index("col")]).astype(jnp.int32),
        ]
    )
    rhs = forcing_right_hand.reshape(n, depth)
    classes = material.reshape(n, depth)
    basis = subspace_basis.reshape(size, n, depth)
    field = ((n, depth), F32)
    pay = ((row_count, width + 2 * layers, depth), F32)
    small = ((size, size), F32)
    wide = ((max(n + size + size // 2, row_count * (width + 2 * layers) + 8), depth), F32)

    def cyclic(value, axis, step):
        count = lax.axis_size(axis)
        return lax.ppermute(value, axis, [(i, (i + step) % count) for i in range(count)])

    def xor_step(value, axis, k):
        count = lax.axis_size(axis)
        return lax.ppermute(value, axis, [(i, i ^ k) for i in range(count)])

    def exchange(value, payload):
        low = cyclic(value, "col", 1)
        high = cyclic(value, "col", -1)
        rec = lax.all_to_all(payload, "row", 0, 0)
        return rec, low, high

    def rows_of(count):
        return ((row_count, width + 2 * layers + count, depth), F32)

    tables = jnp.concatenate([conductivity, capacity, partners.reshape(-1).astype(F32)])
    zm, panel, face = call(
        functools.partial(k_order, grid),
        (
            ((size, n * depth), BF16),
            ((size, width * depth), BF16),
            ((size, layers * depth), BF16),
        ),
        (basis,),
        cost=pl.CostEstimate(flops=1000, bytes_accessed=1000, transcendentals=0),
    )
    held = [xor_step(panel, "row", k) for k in range(2, row_count, 2)]
    x_far = lax.ppermute(
        face,
        "row",
        [(i, (i + 1 if i % 2 else i - 1) % row_count) for i in range(row_count)],
    )
    cond, cap, vent, pay0 = call(
        functools.partial(k_first, grid, pairs),
        (((n + 8, depth), F32), field, ((width, depth), F32), rows_of(8)),
        (tables, classes, vent_open),
        smem=1,
    )
    rec0, cond_low, cond_high = exchange(cond, pay0)

    own_inner, projected, face_y = call(
        functools.partial(k_basis, grid),
        (small, ((size, depth), F32), ((size, depth), F32)),
        (zm, rhs, cond, cap),
        scratch=(
            pltpu.VMEM((n, size, depth), F32),
            pltpu.VMEM((3 * size, n * depth), BF16),
            pltpu.VMEM((7, n, depth), F32),
        ),
        cost=pl.CostEstimate(flops=1000, bytes_accessed=1000, transcendentals=0),
    )

    panels = ((pairs, size, width * depth), BF16)
    coef, own, inverse, sent, pay1, mine, wanted, vents, names = call(
        functools.partial(k_setup, grid, pairs, col_count),
        (
            ((7, n, depth), F32),
            small,
            small,
            field,
            rows_of(size // 2),
            panels,
            ((size, (pairs * width + layers) * depth), BF16),
            ((pairs, width, depth), F32),
            ((4 + pairs, depth), F32),
        ),
        (
            ids, cap, vent, cond, cond_low, cond_high, rec0, zm, own_inner, projected, face_y,
            *held,
        ),
        scratch=(
            pltpu.VMEM((3 * size, n * depth), BF16),
            pltpu.VMEM((n, depth), F32),
            pltpu.SemaphoreType.DMA((2 * pairs,)),
        ),
        smem=1,
        free=range(11, 11 + len(held)),
    )
    others = xor_step(wanted, "row", 1)
    rec1, low1, high1 = exchange(sent, pay1)
    places = 5 + pairs
    x0, wide2, pay2, solves = call(
        functools.partial(k_coarse, grid, pairs),
        (field, wide, pay, ((2 + pairs, size // 2, depth), F32)),
        (ids, coef, vent, zm, inverse, sent, rec1, low1, high1, face_y, others, x_far),
        scratch=(pltpu.VMEM((n, depth), F32),),
        smem=1,
        free=(10, 11),
    )
    rec, low2, high2 = exchange(wide2, pay2)

    def everyone(lines):
        return ((row_count * col_count, lines, depth), F32)

    r0, pay3 = call(
        functools.partial(k_partials, grid, pairs, True),
        (field, everyone((places + 1) // 2)),
        (
            ids, coef, vent, x0, rec, low2, high2, vents, zm, low2, high2, mine, others, x_far, rhs,
        ),
        smem=1,
    )
    blocks, weights, table = call(
        functools.partial(k_blocks, grid, pairs, col_count, 1.0 / cells),
        (
            ((row_count, size, size), F32),
            ((places, size, size), F32),
            ((places * places,), jnp.int32),
        ),
        (
            ids, coef, vents, names, zm, mine, others, x_far, own, inverse, face_y, low2,
            high2, solves, pay3,
        ),
        scratch=(pltpu.VMEM((3 * size, width * depth), BF16),),
        smem=1,
        free=(14,),
        smem_outs=(2,),
        cost=pl.CostEstimate(flops=100_000_000, bytes_accessed=4_000_000, transcendentals=0),
    )
    sums = lax.all_to_all(pay3, ("row", "col"), 0, 0)
    p0, wide4, pay4 = call(
        functools.partial(k_combine, grid),
        (field, wide, pay),
        (table, sums, weights, zm, r0, vent),
        scratch=(pltpu.VMEM((n, depth), F32),),
        smem=1,
    )
    rec, low, high = exchange(wide4, pay4)
    i0, pay5 = call(
        functools.partial(k_partials, grid, pairs, False),
        (field, everyone((places + 1) // 2)),
        (
            ids, coef, vent, p0, rec, low, high, vents, zm, low2, high2, mine, others, x_far,
        ),
        smem=1,
    )
    sums = lax.all_to_all(pay5, ("row", "col"), 0, 0)
    d0, wide6, pay6 = call(
        functools.partial(k_combine, grid),
        (field, wide, pay),
        (table, sums, weights, zm, i0, vent),
        scratch=(pltpu.VMEM((n, depth), F32),),
        smem=1,
    )
    rec, low, high = exchange(wide6, pay6)
    image, pay7 = call(
        functools.partial(k_dots, grid, pairs),
        (field, everyone(2)),
        (ids, coef, vent, d0, rec, low, high, r0, p0, i0),
        smem=1,
    )
    total = lax.all_to_all(pay7, ("row", "col"), 0, 0)
    x2, r2 = call(k_last, (field, field), (total, x0, r0, p0, i0, d0, image))
    shape = forcing_right_hand.shape
    return x2.reshape(shape), r2.reshape(shape), blocks[None, None]


def solution(mesh):
    return jax.shard_map(
        body,
        mesh=mesh,
        in_specs=(
            P(None, "row", "col"),
            P(None, "row", "col"),
            P(),
            P(),
            P("row", "col"),
            P("row", "col", None),
            P(None, None, "row", "col"),
        ),
        out_specs=(P(None, "row", "col"), P(None, "row", "col"), P("row", "col", None, None, None)),
        check_vma=False,
    )
```

```python
import functools

import jax
import jax.numpy as jnp
from jax import lax
from jax.experimental import pallas as pl
from jax.experimental.pallas import tpu as pltpu
from jax.sharding import PartitionSpec as P

F32 = jnp.float32
BF16 = jnp.bfloat16
VMEM = pl.BlockSpec(memory_space=pltpu.VMEM)
SMEM = pl.BlockSpec(memory_space=pltpu.SMEM)
ANY = pl.BlockSpec(memory_space=pl.ANY)
VMEM_LIMIT = 16 * 1024 * 1024


def harmonic(a, b):
    return 2.0 * a * b / (a + b)


def lookup(material, table):
    result = jnp.zeros(material.shape, F32)
    for class_id in range(len(table)):
        result = jnp.where(material == class_id, table[class_id], result)
    return result


class Grid:
    def __init__(self, layers, width, depth):
        self.layers, self.width, self.depth = layers, width, depth
        self.rows = layers * width

    def masks(self):
        shape = (self.rows, self.depth)
        row = lax.broadcasted_iota(jnp.int32, shape, 0)
        lane = lax.broadcasted_iota(jnp.int32, shape, 1)
        return lax.rem(row, self.width), lane, row

    def spread(self, face):
        parts = [
            jnp.broadcast_to(face[z : z + 1], (self.width, self.depth)) for z in range(self.layers)
        ]
        return jnp.concatenate(parts, axis=0)

    def faces(self, v):
        w = self.width
        last = [v[z * w + w - 1 : z * w + w] for z in range(self.layers)]
        first = [v[z * w : z * w + 1] for z in range(self.layers)]
        return last + first

    def payload(self, top, v):
        return jnp.concatenate([top] + self.faces(v), axis=0)

    def around(self, v, low_x, high_x, low_y, high_y):
        xi, lane, _ = self.masks()
        n, d = self.rows, self.depth
        zero = jnp.zeros((n, d), F32)
        own = zero if v is None else v
        plus = zero if v is None else pltpu.roll(v, n - 1, 0)
        minus = zero if v is None else pltpu.roll(v, 1, 0)
        up_x = jnp.where(xi == self.width - 1, self.spread(high_x), plus)
        down_x = jnp.where(xi == 0, self.spread(low_x), minus)
        up_y = pltpu.roll(jnp.where(lane == 0, high_y, own), d - 1, 1)
        down_y = pltpu.roll(jnp.where(lane == d - 1, low_y, own), 1, 1)
        return up_x, down_x, up_y, down_y

    def shifted_z(self, v):
        w = self.width
        return jnp.concatenate([v[w:], v[:w]], axis=0), jnp.concatenate([v[-w:], v[:-w]], axis=0)


def received(grid, ids, pairs, rec):
    count = rec.shape[0]
    w, layers = grid.width, grid.layers
    coupled = rec[ids[0], 0:w, :]
    for k in range(1, pairs):
        coupled = coupled + rec[ids[k], 0:w, :]
    row_at = ids[pairs]
    low = rec[jnp.maximum(row_at - 1, 0), w : w + layers, :]
    high = rec[jnp.minimum(row_at + 1, count - 1), w + layers : w + 2 * layers, :]
    return coupled, low, high


def operate(grid, coef, vent, v, rest):
    coupled, low_x, high_x, low_y, high_y = rest
    up_x, down_x, up_y, down_y = grid.around(v, low_x, high_x, low_y, high_y)
    beside = coef[3] * up_x + coef[4] * down_x + coef[5] * up_y + coef[6] * down_y
    if v is None:
        xi, lane, _ = grid.masks()
        result = -beside
    else:
        up_z, down_z = grid.shifted_z(v)
        result = coef[0] * v - (beside + coef[1] * up_z + coef[2] * down_z)
    w = grid.width
    return jnp.concatenate([result[:-w], result[-w:] - vent * coupled], axis=0)


def project(grid, zm, v):
    d = grid.depth
    parts = [None, None]
    for row in range(grid.rows):
        term = zm[:, row * d : (row + 1) * d].astype(F32) * v[row : row + 1, :]
        k = row % 2
        parts[k] = term if parts[k] is None else parts[k] + term
    return jnp.sum(parts[0] + parts[1], axis=1, keepdims=True)


def solve_own(inverse, column):
    size = inverse.shape[0]
    along = jnp.sum(inverse[...] * column, axis=0, keepdims=True)
    eye = lax.broadcasted_iota(jnp.int32, (size, size), 0) == lax.broadcasted_iota(
        jnp.int32, (size, size), 1
    )
    return jnp.sum(jnp.where(eye, along, 0.0), axis=1, keepdims=True)


def expand(grid, zm, column, out):
    d = grid.depth
    wide = jnp.broadcast_to(column, (column.shape[0], d))
    for row in range(grid.rows):
        out[row : row + 1, :] = jnp.sum(
            zm[:, row * d : (row + 1) * d].astype(F32) * wide, axis=0, keepdims=True
        )


def to_all(grid, pay, top, v, *more):
    block = jnp.concatenate([grid.payload(top, v), *more], axis=0)
    for slot in range(pay.shape[0]):
        pay[slot] = block


def split3(w):
    hi = w.astype(BF16)
    rest = w - hi.astype(F32)
    mid = rest.astype(BF16)
    lo = (rest - mid.astype(F32)).astype(BF16)
    return hi, mid, lo


def dot_nt(a, b):
    return lax.dot_general(a, b, (((1,), (1,)), ((), ())), preferred_element_type=F32)


def fold3(stacked):
    size = stacked.shape[0] // 3
    return stacked[:size] + (stacked[size : 2 * size] + stacked[2 * size :])


def weighted_gram(w3, parts, weights, other):
    size = other.shape[0]
    k = other.shape[1] // len(weights)
    for i, (part, weight) in enumerate(zip(parts, weights)):
        at = slice(i * k, (i + 1) * k)
        hi, mid, lo = split3(part.astype(F32) * weight)
        w3[0:size, at] = hi
        w3[size : 2 * size, at] = mid
        w3[2 * size : 3 * size, at] = lo
    return fold3(dot_nt(w3[:, : len(weights) * k], other))


def y_weights(grid, first, last):
    n, d = grid.rows, grid.depth
    row = lax.broadcasted_iota(jnp.int32, (n, d), 0)
    lane = lax.broadcasted_iota(jnp.int32, (n, d), 1)
    wide = jnp.where(lane == row, first[:, 0:1], 0.0)
    wide = wide + jnp.where(lane == n + row, last[:, d - 1 : d], 0.0)
    return jnp.sum(wide, axis=0, keepdims=True)


def invert_spd(m, ahead=5):
    size = m.shape[0]
    row_id = lax.broadcasted_iota(jnp.int32, (size, size), 0)
    col_id = lax.broadcasted_iota(jnp.int32, (size, size), 1)

    def column(k):
        return jnp.broadcast_to(m[:, k : k + 1], (size, size))

    waiting = {k: column(k) for k in range(min(ahead + 1, size))}
    for k in range(size):
        col = waiting.pop(k)
        inv = 1.0 / col[k : k + 1, :]
        for j in list(waiting):
            at_row = col[j : j + 1, :] * inv
            waiting[j] = jnp.where(row_id == k, at_row, waiting[j] - col * at_row)
        scaled_row = jnp.where(col_id[:1] == k, -inv, m[k : k + 1, :] * inv)
        m = jnp.where(row_id == k, scaled_row, jnp.where(col_id == k, 0.0, m) - col * scaled_row)
        if k + ahead + 1 < size:
            waiting[k + ahead + 1] = column(k + ahead + 1)
    return -m


def opposite(place):
    return {1: 2, 2: 1, 3: 4, 4: 3}.get(place, place)


def k_first(
    grid, pairs, tables, material, vent, cond_out, cap_out, vent_out, pay
):
    classes = (tables.shape[0] - pairs) // 2
    conductivity = [tables[i] for i in range(classes)]
    capacity = [tables[classes + i] for i in range(classes)]
    cond = lookup(material[...], conductivity)
    lane = lax.broadcasted_iota(jnp.int32, (8, grid.depth), 1)
    names = jnp.zeros((8, grid.depth), F32)
    for k in range(pairs):
        names = jnp.where(lane == k, tables[2 * classes + k], names)
    cond_out[0 : grid.rows, :] = cond
    cond_out[grid.rows :, :] = names
    cap_out[...] = lookup(material[...], capacity)
    vent_out[...] = vent[...]
    to_all(grid, pay, vent[...], cond, names)


def conductances(grid, cond, low_x, high_x, low_y, high_y):
    _, _, row = grid.masks()
    up_z, down_z = grid.shifted_z(cond)
    uz = jnp.where(row < grid.rows - grid.width, harmonic(cond, up_z), 0.0)
    lz = jnp.where(row >= grid.width, harmonic(cond, down_z), 0.0)
    ux, lx, uy, ly = [harmonic(cond, c) for c in grid.around(cond, low_x, high_x, low_y, high_y)]
    return uz, lz, ux, lx, uy, ly


def k_order(grid, basis, zm, panel, face):
    n, d, w, layers = grid.rows, grid.depth, grid.width, grid.layers
    size = basis.shape[0]
    odd = lax.bitwise_and(lax.axis_index("row"), 1) == 1

    for row in range(0, n, w):
        for a in range(0, size, w):
            turned = jnp.swapaxes(basis[a : a + w, row : row + w, :], 0, 1)
            for i in range(w):
                zm[a : a + w, (row + i) * d : (row + i + 1) * d] = turned[i]
    panel[...] = zm[:, (n - w) * d :]
    for z in range(layers):
        start = z * w * d
        first = zm[:, start : start + d].astype(F32)
        last = zm[:, start + (w - 1) * d : start + w * d].astype(F32)
        face[:, z * d : (z + 1) * d] = jnp.where(odd, last, first).astype(BF16)


def k_basis(grid, zm, rhs, cond_ref, cap_ref, own, projected, face_y, zr, w3, coef):
    n, d, w = grid.rows, grid.depth, grid.width
    size = zm.shape[0]
    cond = cond_ref[0:n, :]
    zero_face = jnp.zeros((grid.layers, d), F32)
    zero = jnp.zeros((n, d), F32)
    uz, lz, ux, lx, uy, ly = conductances(grid, cond, zero_face, zero_face, zero, zero)
    coef[0] = cap_ref[...] + uz + lz + ux + lx + uy + ly
    for i, c in enumerate((uz, lz, ux, lx, uy, ly)):
        coef[i + 1] = c

    parts = [None, None]
    lane = lax.broadcasted_iota(jnp.int32, (size, d), 1)
    sides = jnp.zeros((size, d), F32)
    for row in range(n):
        z = zm[:, row * d : (row + 1) * d].astype(F32)
        zr[row] = z
        sides = jnp.where(lane == row, z[:, 0:1], sides)
        sides = jnp.where(lane == n + row, z[:, d - 1 : d], sides)
        term = z * rhs[row : row + 1, :]
        parts[row % 2] = term if parts[row % 2] is None else parts[row % 2] + term
    projected[...] = parts[0] + parts[1]
    face_y[...] = sides
    total = None
    for start in range(0, n, 8):
        for row in range(start, start + 8):
            z = zr[row]

            def c(i):
                return coef[i, row : row + 1, :]

            acc = c(0) * z
            if row + w < n:
                acc = acc - c(1) * zr[row + w]
            if row >= w:
                acc = acc - c(2) * zr[row - w]
            if row % w < w - 1:
                acc = acc - c(3) * zr[row + 1]
            if row % w > 0:
                acc = acc - c(4) * zr[row - 1]
            acc = acc - c(5) * pltpu.roll(z, d - 1, 1) - c(6) * pltpu.roll(z, 1, 1)
            at = slice(row * d, (row + 1) * d)
            hi, mid, lo = split3(acc)
            w3[0:size, at] = hi
            w3[size : 2 * size, at] = mid
            w3[2 * size : 3 * size, at] = lo
        part = dot_nt(w3[:, start * d : (start + 8) * d], zm[:, start * d : (start + 8) * d])
        total = part if total is None else total + part
    own[...] = fold3(total)


def pick(sources, targets, sems):
    for i, (index, target) in enumerate(targets):
        for j, source in enumerate(sources):

            @pl.when(index == j)
            def _(source=source, target=target, i=i):
                pltpu.make_async_copy(source, target, sems.at[i]).start()


def await_picks(sources, targets, sems):
    for i, (_, target) in enumerate(targets):
        pltpu.make_async_copy(sources[0], target, sems.at[i]).wait()


def fold(inverse):
    half = inverse.shape[0] // 2
    return jnp.concatenate([inverse[0:half, :], inverse[half:, :]], axis=1)


def unfold(folded):
    size = folded.shape[1] // 2
    return jnp.concatenate([folded[:, :size], folded[:, size:]], axis=0)


def k_setup(
    grid, pairs, cols, ids, cap, vent, cond, cond_low, cond_high, rec,
    zm, own_inner, projected, face_y, *rest,
):
    n, d, w, layers = grid.rows, grid.depth, grid.width, grid.layers
    held = [zm.at[:, pl.ds((n - w) * d, w * d)], *rest[:-12]]
    coef, own, inverse, sent, pay, mine, wanted, vents, names, w3, v0, sems = rest[-12:]
    count = rec.shape[0]
    panel = w * d
    line = w + 2 * layers
    sibling = lax.bitwise_xor(ids[pairs], 1)
    names_lane = lax.broadcasted_iota(jnp.int32, (1, d), 1)
    targets = []
    for k in range(pairs):
        theirs = jnp.where(names_lane == k, rec[sibling, line : line + 1, :], 0.0)
        for partner, target in (
            (ids[k], mine.at[k]),
            (jnp.sum(theirs).astype(jnp.int32), wanted.at[:, pl.ds(k * panel, panel)]),
        ):
            index = lax.shift_right_logical(lax.bitwise_xor(partner, ids[pairs]), 1)
            targets.append((index, target))
    pick(held, targets, sems)

    upward = lax.bitwise_and(ids[pairs], 1) == 0
    for z in range(layers):
        low_face = zm[:, z * panel : z * panel + d]
        high_face = zm[:, (z + 1) * panel - d : (z + 1) * panel]
        at = slice(pairs * panel + z * d, pairs * panel + (z + 1) * d)
        wanted[:, at] = jnp.where(upward, high_face.astype(F32), low_face.astype(F32)).astype(BF16)
    for k in range(pairs):
        vents[k] = vent[...] * rec[ids[k], 0:w, :]
    up, down = jnp.minimum(ids[pairs] + 1, count - 1), jnp.maximum(ids[pairs] - 1, 0)
    lines = [rec[r, line : line + 1, :] for r in (up, down)]
    lines += [cond_high[n : n + 1, :], cond_low[n : n + 1, :]]
    lines += [rec[ids[k], line : line + 1, :] for k in range(pairs)]
    names[...] = jnp.concatenate(lines, axis=0)
    vent_sum, low_x, high_x = received(grid, ids, pairs, rec)
    row_at, col_at = ids[pairs], ids[pairs + 1]
    low_x = jnp.where(row_at > 0, low_x, 0.0)
    high_x = jnp.where(row_at < count - 1, high_x, 0.0)
    low_y = jnp.where(col_at > 0, cond_low[0:n, :], 0.0)
    high_y = jnp.where(col_at < cols - 1, cond_high[0:n, :], 0.0)
    uz, lz, ux, lx, uy, ly = conductances(grid, cond[0:n, :], low_x, high_x, low_y, high_y)
    plenum = vent[...] * vent_sum
    diagonal = cap[...] + uz + lz + ux + lx + uy + ly
    coef[0] = jnp.concatenate([diagonal[:-w], diagonal[-w:] + plenum], axis=0)
    for i, c in enumerate((uz, lz, ux, lx, uy, ly)):
        coef[i + 1] = c
    last, first = [ux[z * w + w - 1 :][:1] for z in range(layers)], [lx[z * w :][:1] for z in range(layers)]
    top = [plenum[x : x + 1] for x in range(w)]
    top[0] = top[0] + first[-1]
    top[-1] = top[-1] + last[-1]
    row = n - w
    tops = zm[:, row * d :]
    block = own_inner[...] + weighted_gram(
        w3, [tops[:, x * d : (x + 1) * d] for x in range(w)], top, tops
    )
    for at, weights in ((0, first[:-1]), (panel - d, last[:-1])):
        parts = [zm[:, z * panel + at : z * panel + at + d] for z in range(layers - 1)]
        block = block + weighted_gram(w3, parts, weights, jnp.concatenate(parts, axis=1))
    sides = face_y[...].astype(BF16)
    block = block + weighted_gram(w3, [sides], [y_weights(grid, ly, uy)], sides)
    own[...] = block
    inverse[...] = invert_spd(block)
    y0 = solve_own(inverse, jnp.sum(projected[...], axis=1, keepdims=True))
    expand(grid, zm, y0, v0)
    field = v0[...]
    sent[0:n, :] = field
    to_all(grid, pay, vent[...] * field[-w:], field, fold(inverse))
    await_picks(held, targets, sems)


def incoming(grid, pairs, ids, rec, low, high):
    coupled, low_x, high_x = received(grid, ids, pairs, rec)
    n = grid.rows
    return coupled, low_x, high_x, low[0:n, :], high[0:n, :]


def k_coarse(
    grid, pairs, ids, coef, vent, zm, inverse, field, rec, low, high, face_y, _,
    out, wide, pay, solves, scratch,
):
    n, w = grid.rows, grid.width
    beside = operate(grid, coef, vent[...], None, incoming(grid, pairs, ids, rec, low, high))
    expand(grid, zm, solve_own(inverse, project(grid, zm, beside)), scratch)
    result = field[0:n, :] - scratch[...]
    out[...] = result
    size, half = zm.shape[0], solves.shape[1]
    wide[0:n, :] = result
    wide[n : n + size, :] = face_y[...]
    wide[n + size : n + size + half, :] = fold(inverse)
    to_all(grid, pay, vent[...] * result[-w:], result)
    first = w + 2 * grid.layers
    row_at = ids[pairs]
    solves[0] = rec[jnp.minimum(row_at + 1, rec.shape[0] - 1), first : first + half, :]
    solves[1] = rec[jnp.maximum(row_at - 1, 0), first : first + half, :]
    for k in range(pairs):
        solves[2 + k] = rec[ids[k], first : first + half, :]


def chosen(grid, pairs, ids, mine, others, k, at):
    panel = grid.width * grid.depth
    same = lax.bitwise_and(lax.bitwise_xor(ids[k], ids[pairs]), 1) == 0
    there = slice(k * panel + at.start, k * panel + at.stop)
    return jnp.where(same, mine[k, :, at].astype(F32), others[:, there].astype(F32))


def x_faces(grid, pairs, ids, others, far):
    near = others[:, pairs * grid.width * grid.depth :].astype(F32)
    across = far[...].astype(F32)
    upward = lax.bitwise_and(ids[pairs], 1) == 0
    return jnp.where(upward, near, across), jnp.where(upward, across, near)


def k_partials(
    grid, pairs, base, ids, coef, vent, field, far, rec, low, high, vents, zm, low2, high2, mine,
    others, *rest,
):
    n, d, w, layers = grid.rows, grid.depth, grid.width, grid.layers
    size = zm.shape[0]
    base_ref = rest[0] if base else None
    out, pay = rest[-2:]
    next_first, prev_last = x_faces(grid, pairs, ids, others, far)
    v = operate(grid, coef, vent[...], field[...], incoming(grid, pairs, ids, rec, low, high))
    if base:
        v = base_ref[...] - v
    out[...] = v
    face, zero = jnp.zeros((layers, d), F32), jnp.zeros((n, d), F32)
    own = operate(grid, coef, vent[...], v, (jnp.zeros((w, d), F32), face, face, zero, zero))

    def along(basis, weights):
        total = None
        for i, weight in enumerate(weights):
            term = basis[:, i * d : (i + 1) * d].astype(F32) * weight
            total = term if total is None else total + term
        return total

    even = along(zm, [own[i : i + 1] for i in range(n)])
    ux, lx, uy, ly = [coef[i] * v for i in (3, 4, 5, 6)]
    sums = [
        even,
        -along(next_first, [ux[z * w + w - 1 : z * w + w] for z in range(layers)]),
        -along(prev_last, [lx[z * w : z * w + 1] for z in range(layers)]),
    ]
    toward = pltpu.roll(y_weights(grid, ly, uy), n, 1)
    lane = lax.broadcasted_iota(jnp.int32, (1, d), 1)
    sums.append(-(high2[n : n + size, :] * jnp.where(lane < n, toward, 0.0)))
    sums.append(-(low2[n : n + size, :] * jnp.where(lane < n, 0.0, toward)))
    top = v[-w:]
    for k in range(pairs):
        weight = vents[k] * top
        total = None
        for x in range(w):
            part = chosen(grid, pairs, ids, mine, others, k, slice(x * d, (x + 1) * d))
            term = part * weight[x : x + 1]
            total = term if total is None else total + term
        sums.append(-total)
    eye = lax.broadcasted_iota(jnp.int32, (size, size), 0) == lax.broadcasted_iota(
        jnp.int32, (size, size), 1
    )
    rows = [
        jnp.sum(
            jnp.where(eye, jnp.sum(q, axis=1, keepdims=True), 0.0), axis=0, keepdims=True
        )
        for q in sums
    ]
    if len(rows) % 2:
        rows.append(jnp.zeros((1, size), F32))
    block = jnp.concatenate(
        [jnp.concatenate(rows[i : i + 2], axis=1) for i in range(0, len(rows), 2)], axis=0
    )
    for slot in range(pay.shape[0]):
        pay[slot] = block


def k_combine(grid, table, rec, weights, zm, base, vent, out, wide, pay, scratch):
    size = zm.shape[0]
    count = weights.shape[0]
    total = None
    for j in range(count):
        sides = [None, None]
        for i in range(count):
            at = table[j * count + i]
            line, side = divmod(opposite(i), 2)
            term = rec[at, line : line + 1, :]
            sides[side] = term if sides[side] is None else sides[side] + term
        term = weights[j] * (sides[0][:, 0:size] + sides[1][:, size : 2 * size])
        total = term if total is None else total + term
    expand(grid, zm, jnp.sum(total, axis=1, keepdims=True), scratch)
    result = base[...] - scratch[...]
    out[...] = result
    wide[0 : grid.rows, :] = result
    to_all(grid, pay, vent[...] * result[-grid.width :], result)


def k_dots(grid, pairs, ids, coef, vent, field, rec, low, high, r0, p0, i0, out, pay):
    image = operate(grid, coef, vent[...], field[...], incoming(grid, pairs, ids, rec, low, high))
    out[...] = image
    d, r, p, i = field[...], r0[...], p0[...], i0[...]
    products = (r * r, p * i, r * i, i * i, d * i, d * image)
    lane = lax.broadcasted_iota(jnp.int32, pay.shape[1:], 1)
    block = jnp.zeros(pay.shape[1:], F32)
    for k, q in enumerate(products):
        total = jnp.sum(jnp.sum(q, axis=0, keepdims=True), axis=1, keepdims=True)
        block = jnp.where(lane == k, total, block)
    for slot in range(pay.shape[0]):
        pay[slot] = block


def k_last(rec, x0, r0, p0, i0, d, image, x2, r2):
    total = rec[0]
    for slot in range(1, rec.shape[0]):
        total = total + rec[slot]
    rr, pi, ri, ii, di, dd = [total[0:1, k : k + 1] for k in range(6)]
    a1 = rr / pi
    new = rr - 2.0 * a1 * ri + a1 * a1 * ii
    grow = 1.0 + new / rr
    a2 = new / (grow * grow * pi - 2.0 * grow * a1 * di + a1 * a1 * dd)
    x2[...] = x0[...] + (a1 + a2 * grow) * p0[...] - (a2 * a1) * d[...]
    r2[...] = r0[...] - (a1 + a2 * grow) * i0[...] + (a2 * a1) * image[...]


def k_blocks(
    grid, pairs, cols, scale, ids, coef, vents, names, zm, mine, others, x_far, own, inverse,
    face_y, low2, high2, solves, _, out, weights, table, w3,
):
    n, d, w, layers = grid.rows, grid.depth, grid.width, grid.layers
    rows, size = out.shape[0], out.shape[1]
    row_at = ids[pairs]
    up, down = jnp.minimum(row_at + 1, rows - 1), jnp.maximum(row_at - 1, 0)

    col_at = ids[pairs + 1]
    lane = lax.broadcasted_iota(jnp.int32, (1, d), 1)
    near = [(row_at, col_at), (row_at + 1, col_at), (row_at - 1, col_at)]
    near += [(row_at, col_at + 1), (row_at, col_at - 1)]
    near += [(ids[k], col_at) for k in range(pairs)]
    count = len(near)
    for j, (r, c) in enumerate(near):
        places = [(r, c), (r + 1, c), (r - 1, c), (r, c + 1), (r, c - 1)]
        for k in range(pairs):
            met = ids[k]
            if j > 0:
                met = jnp.sum(jnp.where(lane == k, names[j - 1 : j, :], 0.0)).astype(jnp.int32)
            places.append((met, c))
        for i, (pr, pc) in enumerate(places):
            table[j * count + i] = lax.rem(pr + 2 * rows, rows) * cols + lax.rem(pc + 2 * cols, cols)

    def dot(a, b):
        return lax.dot_general(
            a, b, (((1,), (0,)), ((), ())),
            precision=lax.Precision.HIGHEST, preferred_element_type=F32,
        )

    ux, lx, uy, ly = coef[3], coef[4], coef[5], coef[6]
    last = [z * w + w - 1 for z in range(layers)]
    first = [z * w for z in range(layers)]

    def basis_rows(at):
        return [zm[:, i * d : (i + 1) * d] for i in at]

    next_first, prev_last = [f.astype(BF16) for f in x_faces(grid, pairs, ids, others, x_far)]
    found = [
        weighted_gram(w3, basis_rows(last), [-ux[i : i + 1] for i in last], next_first),
        weighted_gram(w3, basis_rows(first), [-lx[i : i + 1] for i in first], prev_last),
    ]
    toward = -pltpu.roll(y_weights(grid, ly, uy), n, 1)
    swapped = pltpu.roll(face_y[...], n, 1)
    for theirs, there in ((high2, lane < n), (low2, lane >= n)):
        weight = jnp.where(there, toward, 0.0)
        found.append(weighted_gram(w3, [swapped], [weight], theirs[n : n + size, :].astype(BF16)))
    top = basis_rows(range(n - w, n))
    for k in range(pairs):
        panel = chosen(grid, pairs, ids, mine, others, k, slice(0, w * d)).astype(BF16)
        found.append(weighted_gram(w3, top, [-vents[k, i : i + 1, :] for i in range(w)], panel))

    for slot in range(rows):
        out[slot] = jnp.zeros((size, size), F32)
    out[row_at] = own[...] * scale
    out[up] = out[up] + jnp.where(row_at < rows - 1, found[0] * scale, 0.0)
    out[down] = out[down] + jnp.where(row_at > 0, found[1] * scale, 0.0)
    for k in range(pairs):
        out[ids[k]] = out[ids[k]] + found[4 + k] * scale

    weights[0] = inverse[...]
    start, stop = n + size, n + size + size // 2
    folded = [solves[0], solves[1], high2[start:stop, :], low2[start:stop, :]]
    folded += [solves[2 + k] for k in range(pairs)]
    for j, (block, theirs) in enumerate(zip(found, folded)):
        weights[j + 1] = -dot(inverse[...], dot(block, unfold(theirs)))


def call(kernel, outs, operands, scratch=(), smem=0, free=(), smem_outs=(), cost=None):
    specs = [
        SMEM if i < smem else ANY if i in free else VMEM for i in range(len(operands))
    ]
    return pl.pallas_call(
        kernel,
        out_shape=tuple(jax.ShapeDtypeStruct(s, t) for s, t in outs),
        in_specs=specs,
        out_specs=tuple(SMEM if i in smem_outs else VMEM for i in range(len(outs))),
        scratch_shapes=list(scratch),
        compiler_params=pltpu.CompilerParams(vmem_limit_bytes=VMEM_LIMIT),
        cost_estimate=cost,
    )(*operands)


def body(forcing_right_hand, material, capacity, conductivity, vent_open, partners, subspace_basis):
    layers, width, depth = forcing_right_hand.shape
    size = subspace_basis.shape[0]
    grid = Grid(layers, width, depth)
    n, cells = grid.rows, forcing_right_hand.size
    row_count, col_count = lax.axis_size("row"), lax.axis_size("col")
    pairs = partners.shape[-1]
    ids = jnp.concatenate(
        [
            partners.reshape(-1),
            jnp.stack([lax.axis_index("row"), lax.axis_index("col")]).astype(jnp.int32),
        ]
    )
    rhs = forcing_right_hand.reshape(n, depth)
    classes = material.reshape(n, depth)
    basis = subspace_basis.reshape(size, n, depth)
    field = ((n, depth), F32)
    pay = ((row_count, width + 2 * layers, depth), F32)
    small = ((size, size), F32)
    wide = ((max(n + size + size // 2, row_count * (width + 2 * layers) + 8), depth), F32)

    def cyclic(value, axis, step):
        count = lax.axis_size(axis)
        return lax.ppermute(value, axis, [(i, (i + step) % count) for i in range(count)])

    def xor_step(value, axis, k):
        count = lax.axis_size(axis)
        return lax.ppermute(value, axis, [(i, i ^ k) for i in range(count)])

    def exchange(value, payload):
        low = cyclic(value, "col", 1)
        high = cyclic(value, "col", -1)
        rec = lax.all_to_all(payload, "row", 0, 0)
        return rec, low, high

    def rows_of(count):
        return ((row_count, width + 2 * layers + count, depth), F32)

    tables = jnp.concatenate([conductivity, capacity, partners.reshape(-1).astype(F32)])
    zm, panel, face = call(
        functools.partial(k_order, grid),
        (
            ((size, n * depth), BF16),
            ((size, width * depth), BF16),
            ((size, layers * depth), BF16),
        ),
        (basis,),
        cost=pl.CostEstimate(flops=1000, bytes_accessed=1000, transcendentals=0),
    )
    held = [xor_step(panel, "row", k) for k in range(2, row_count, 2)]
    x_far = lax.ppermute(
        face,
        "row",
        [(i, (i + 1 if i % 2 else i - 1) % row_count) for i in range(row_count)],
    )
    cond, cap, vent, pay0 = call(
        functools.partial(k_first, grid, pairs),
        (((n + 8, depth), F32), field, ((width, depth), F32), rows_of(8)),
        (tables, classes, vent_open),
        smem=1,
    )
    rec0, cond_low, cond_high = exchange(cond, pay0)

    own_inner, projected, face_y = call(
        functools.partial(k_basis, grid),
        (small, ((size, depth), F32), ((size, depth), F32)),
        (zm, rhs, cond, cap),
        scratch=(
            pltpu.VMEM((n, size, depth), F32),
            pltpu.VMEM((3 * size, n * depth), BF16),
            pltpu.VMEM((7, n, depth), F32),
        ),
        cost=pl.CostEstimate(flops=1000, bytes_accessed=1000, transcendentals=0),
    )

    panels = ((pairs, size, width * depth), BF16)
    coef, own, inverse, sent, pay1, mine, wanted, vents, names = call(
        functools.partial(k_setup, grid, pairs, col_count),
        (
            ((7, n, depth), F32),
            small,
            small,
            ((136, depth), F32),
            rows_of(size // 2),
            panels,
            ((size, (pairs * width + layers) * depth), BF16),
            ((pairs, width, depth), F32),
            ((4 + pairs, depth), F32),
        ),
        (
            ids, cap, vent, cond, cond_low, cond_high, rec0, zm, own_inner, projected, face_y,
            *held,
        ),
        scratch=(
            pltpu.VMEM((3 * size, n * depth), BF16),
            pltpu.VMEM((n, depth), F32),
            pltpu.SemaphoreType.DMA((2 * pairs,)),
        ),
        smem=1,
        free=range(11, 11 + len(held)),
    )
    others = xor_step(wanted, "row", 1)
    rec1, low1, high1 = exchange(sent, pay1)
    places = 5 + pairs
    x0, wide2, pay2, solves = call(
        functools.partial(k_coarse, grid, pairs),
        (field, wide, pay, ((2 + pairs, size // 2, depth), F32)),
        (ids, coef, vent, zm, inverse, sent, rec1, low1, high1, face_y, others),
        scratch=(pltpu.VMEM((n, depth), F32),),
        smem=1,
        free=(10,),
    )
    pay2, x_far = lax.optimization_barrier((pay2, x_far))
    rec, low2, high2 = exchange(wide2, pay2)

    def everyone(lines):
        return ((row_count * col_count, lines, depth), F32)

    r0, pay3 = call(
        functools.partial(k_partials, grid, pairs, True),
        (field, everyone((places + 1) // 2)),
        (
            ids, coef, vent, x0, x_far, rec, low2, high2, vents, zm, low2, high2, mine, others, rhs,
        ),
        smem=1,
    )
    blocks, weights, table = call(
        functools.partial(k_blocks, grid, pairs, col_count, 1.0 / cells),
        (
            ((row_count, size, size), F32),
            ((places, size, size), F32),
            ((places * places,), jnp.int32),
        ),
        (
            ids, coef, vents, names, zm, mine, others, x_far, own, inverse, face_y, low2,
            high2, solves, pay3,
        ),
        scratch=(pltpu.VMEM((3 * size, width * depth), BF16),),
        smem=1,
        free=(14,),
        smem_outs=(2,),
        cost=pl.CostEstimate(flops=100_000_000, bytes_accessed=4_000_000, transcendentals=0),
    )
    sums = lax.all_to_all(pay3, ("row", "col"), 0, 0)
    p0, wide4, pay4 = call(
        functools.partial(k_combine, grid),
        (field, wide, pay),
        (table, sums, weights, zm, r0, vent),
        scratch=(pltpu.VMEM((n, depth), F32),),
        smem=1,
    )
    rec, low, high = exchange(wide4, pay4)
    i0, pay5 = call(
        functools.partial(k_partials, grid, pairs, False),
        (field, everyone((places + 1) // 2)),
        (
            ids, coef, vent, p0, x_far, rec, low, high, vents, zm, low2, high2, mine, others,
        ),
        smem=1,
    )
    sums = lax.all_to_all(pay5, ("row", "col"), 0, 0)
    d0, wide6, pay6 = call(
        functools.partial(k_combine, grid),
        (field, wide, pay),
        (table, sums, weights, zm, i0, vent),
        scratch=(pltpu.VMEM((n, depth), F32),),
        smem=1,
    )
    rec, low, high = exchange(wide6, pay6)
    image, pay7 = call(
        functools.partial(k_dots, grid, pairs),
        (field, everyone(2)),
        (ids, coef, vent, d0, rec, low, high, r0, p0, i0),
        smem=1,
    )
    total = lax.all_to_all(pay7, ("row", "col"), 0, 0)
    x2, r2 = call(k_last, (field, field), (total, x0, r0, p0, i0, d0, image))
    shape = forcing_right_hand.shape
    return x2.reshape(shape), r2.reshape(shape), blocks[None, None]


def solution(mesh):
    return jax.shard_map(
        body,
        mesh=mesh,
        in_specs=(
            P(None, "row", "col"),
            P(None, "row", "col"),
            P(),
            P(),
            P("row", "col"),
            P("row", "col", None),
            P(None, None, "row", "col"),
        ),
        out_specs=(P(None, "row", "col"), P(None, "row", "col"), P("row", "col", None, None, None)),
        check_vma=False,
    )
```

```python
import functools

import jax
import jax.numpy as jnp
from jax import lax
from jax.experimental import pallas as pl
from jax.experimental.pallas import tpu as pltpu
from jax.sharding import PartitionSpec as P

F32 = jnp.float32
BF16 = jnp.bfloat16
VMEM = pl.BlockSpec(memory_space=pltpu.VMEM)
SMEM = pl.BlockSpec(memory_space=pltpu.SMEM)
ANY = pl.BlockSpec(memory_space=pl.ANY)
VMEM_LIMIT = 16 * 1024 * 1024


def harmonic(a, b):
    return 2.0 * a * b / (a + b)


def lookup(material, table):
    result = jnp.zeros(material.shape, F32)
    for class_id in range(len(table)):
        result = jnp.where(material == class_id, table[class_id], result)
    return result


class Grid:
    def __init__(self, layers, width, depth):
        self.layers, self.width, self.depth = layers, width, depth
        self.rows = layers * width

    def masks(self):
        shape = (self.rows, self.depth)
        row = lax.broadcasted_iota(jnp.int32, shape, 0)
        lane = lax.broadcasted_iota(jnp.int32, shape, 1)
        return lax.rem(row, self.width), lane, row

    def spread(self, face):
        parts = [
            jnp.broadcast_to(face[z : z + 1], (self.width, self.depth)) for z in range(self.layers)
        ]
        return jnp.concatenate(parts, axis=0)

    def faces(self, v):
        w = self.width
        last = [v[z * w + w - 1 : z * w + w] for z in range(self.layers)]
        first = [v[z * w : z * w + 1] for z in range(self.layers)]
        return last + first

    def payload(self, top, v):
        return jnp.concatenate([top] + self.faces(v), axis=0)

    def around(self, v, low_x, high_x, low_y, high_y):
        xi, lane, _ = self.masks()
        n, d = self.rows, self.depth
        zero = jnp.zeros((n, d), F32)
        own = zero if v is None else v
        plus = zero if v is None else pltpu.roll(v, n - 1, 0)
        minus = zero if v is None else pltpu.roll(v, 1, 0)
        up_x = jnp.where(xi == self.width - 1, self.spread(high_x), plus)
        down_x = jnp.where(xi == 0, self.spread(low_x), minus)
        up_y = pltpu.roll(jnp.where(lane == 0, high_y, own), d - 1, 1)
        down_y = pltpu.roll(jnp.where(lane == d - 1, low_y, own), 1, 1)
        return up_x, down_x, up_y, down_y

    def shifted_z(self, v):
        w = self.width
        return jnp.concatenate([v[w:], v[:w]], axis=0), jnp.concatenate([v[-w:], v[:-w]], axis=0)


def received(grid, ids, pairs, rec):
    count = rec.shape[0]
    w, layers = grid.width, grid.layers
    coupled = rec[ids[0], 0:w, :]
    for k in range(1, pairs):
        coupled = coupled + rec[ids[k], 0:w, :]
    row_at = ids[pairs]
    low = rec[jnp.maximum(row_at - 1, 0), w : w + layers, :]
    high = rec[jnp.minimum(row_at + 1, count - 1), w + layers : w + 2 * layers, :]
    return coupled, low, high


def operate(grid, coef, vent, v, rest):
    coupled, low_x, high_x, low_y, high_y = rest
    up_x, down_x, up_y, down_y = grid.around(v, low_x, high_x, low_y, high_y)
    beside = coef[3] * up_x + coef[4] * down_x + coef[5] * up_y + coef[6] * down_y
    if v is None:
        xi, lane, _ = grid.masks()
        result = -beside
    else:
        up_z, down_z = grid.shifted_z(v)
        result = coef[0] * v - (beside + coef[1] * up_z + coef[2] * down_z)
    w = grid.width
    return jnp.concatenate([result[:-w], result[-w:] - vent * coupled], axis=0)


def project(grid, zm, v):
    d = grid.depth
    parts = [None, None]
    for row in range(grid.rows):
        term = zm[:, row * d : (row + 1) * d].astype(F32) * v[row : row + 1, :]
        k = row % 2
        parts[k] = term if parts[k] is None else parts[k] + term
    return jnp.sum(parts[0] + parts[1], axis=1, keepdims=True)


def solve_own(inverse, column):
    size = inverse.shape[0]
    along = jnp.sum(inverse[...] * column, axis=0, keepdims=True)
    eye = lax.broadcasted_iota(jnp.int32, (size, size), 0) == lax.broadcasted_iota(
        jnp.int32, (size, size), 1
    )
    return jnp.sum(jnp.where(eye, along, 0.0), axis=1, keepdims=True)


def expand(grid, zm, column, out):
    d = grid.depth
    wide = jnp.broadcast_to(column, (column.shape[0], d))
    for row in range(grid.rows):
        out[row : row + 1, :] = jnp.sum(
            zm[:, row * d : (row + 1) * d].astype(F32) * wide, axis=0, keepdims=True
        )


def to_all(grid, pay, top, v, *more):
    block = jnp.concatenate([grid.payload(top, v), *more], axis=0)
    for slot in range(pay.shape[0]):
        pay[slot] = block


def split3(w):
    hi = w.astype(BF16)
    rest = w - hi.astype(F32)
    mid = rest.astype(BF16)
    lo = (rest - mid.astype(F32)).astype(BF16)
    return hi, mid, lo


def dot_nt(a, b):
    return lax.dot_general(a, b, (((1,), (1,)), ((), ())), preferred_element_type=F32)


def fold3(stacked):
    size = stacked.shape[0] // 3
    return stacked[:size] + (stacked[size : 2 * size] + stacked[2 * size :])


def weighted_gram(w3, parts, weights, other):
    size = other.shape[0]
    k = other.shape[1] // len(weights)
    for i, (part, weight) in enumerate(zip(parts, weights)):
        at = slice(i * k, (i + 1) * k)
        hi, mid, lo = split3(part.astype(F32) * weight)
        w3[0:size, at] = hi
        w3[size : 2 * size, at] = mid
        w3[2 * size : 3 * size, at] = lo
    return fold3(dot_nt(w3[:, : len(weights) * k], other))


def y_weights(grid, first, last):
    n, d = grid.rows, grid.depth
    row = lax.broadcasted_iota(jnp.int32, (n, d), 0)
    lane = lax.broadcasted_iota(jnp.int32, (n, d), 1)
    wide = jnp.where(lane == row, first[:, 0:1], 0.0)
    wide = wide + jnp.where(lane == n + row, last[:, d - 1 : d], 0.0)
    return jnp.sum(wide, axis=0, keepdims=True)


def invert_spd(m, ahead=5):
    size = m.shape[0]
    row_id = lax.broadcasted_iota(jnp.int32, (size, size), 0)
    col_id = lax.broadcasted_iota(jnp.int32, (size, size), 1)

    def column(k):
        return jnp.broadcast_to(m[:, k : k + 1], (size, size))

    waiting = {k: column(k) for k in range(min(ahead + 1, size))}
    for k in range(size):
        col = waiting.pop(k)
        inv = 1.0 / col[k : k + 1, :]
        for j in list(waiting):
            at_row = col[j : j + 1, :] * inv
            waiting[j] = jnp.where(row_id == k, at_row, waiting[j] - col * at_row)
        scaled_row = jnp.where(col_id[:1] == k, -inv, m[k : k + 1, :] * inv)
        m = jnp.where(row_id == k, scaled_row, jnp.where(col_id == k, 0.0, m) - col * scaled_row)
        if k + ahead + 1 < size:
            waiting[k + ahead + 1] = column(k + ahead + 1)
    return -m


def opposite(place):
    return {1: 2, 2: 1, 3: 4, 4: 3}.get(place, place)


def k_first(
    grid, pairs, tables, material, vent, cond_out, cap_out, vent_out, pay
):
    classes = (tables.shape[0] - pairs) // 2
    conductivity = [tables[i] for i in range(classes)]
    capacity = [tables[classes + i] for i in range(classes)]
    cond = lookup(material[...], conductivity)
    lane = lax.broadcasted_iota(jnp.int32, (8, grid.depth), 1)
    names = jnp.zeros((8, grid.depth), F32)
    for k in range(pairs):
        names = jnp.where(lane == k, tables[2 * classes + k], names)
    cond_out[0 : grid.rows, :] = cond
    cond_out[grid.rows :, :] = names
    cap_out[...] = lookup(material[...], capacity)
    vent_out[...] = vent[...]
    to_all(grid, pay, vent[...], cond, names)


def conductances(grid, cond, low_x, high_x, low_y, high_y):
    _, _, row = grid.masks()
    up_z, down_z = grid.shifted_z(cond)
    uz = jnp.where(row < grid.rows - grid.width, harmonic(cond, up_z), 0.0)
    lz = jnp.where(row >= grid.width, harmonic(cond, down_z), 0.0)
    ux, lx, uy, ly = [harmonic(cond, c) for c in grid.around(cond, low_x, high_x, low_y, high_y)]
    return uz, lz, ux, lx, uy, ly


def k_order(grid, basis, zm, panel, face_a, face_b):
    n, d, w, layers = grid.rows, grid.depth, grid.width, grid.layers
    size = basis.shape[0]
    odd = lax.bitwise_and(lax.axis_index("row"), 1) == 1

    for row in range(0, n, w):
        for a in range(0, size, w):
            turned = jnp.swapaxes(basis[a : a + w, row : row + w, :], 0, 1)
            for i in range(w):
                zm[a : a + w, (row + i) * d : (row + i + 1) * d] = turned[i]
    panel[...] = zm[:, (n - w) * d :]
    for z in range(layers):
        start = z * w * d
        first = zm[:, start : start + d].astype(F32)
        last = zm[:, start + (w - 1) * d : start + w * d].astype(F32)
        half = layers // 2
        face, at = (face_a, z) if z < half else (face_b, z - half)
        face[:, at * d : (at + 1) * d] = jnp.where(odd, last, first).astype(BF16)


def k_basis(grid, zm, rhs, cond_ref, cap_ref, own, projected, face_y, zr, w3, coef):
    n, d, w = grid.rows, grid.depth, grid.width
    size = zm.shape[0]
    cond = cond_ref[0:n, :]
    zero_face = jnp.zeros((grid.layers, d), F32)
    zero = jnp.zeros((n, d), F32)
    uz, lz, ux, lx, uy, ly = conductances(grid, cond, zero_face, zero_face, zero, zero)
    coef[0] = cap_ref[...] + uz + lz + ux + lx + uy + ly
    for i, c in enumerate((uz, lz, ux, lx, uy, ly)):
        coef[i + 1] = c

    parts = [None, None]
    lane = lax.broadcasted_iota(jnp.int32, (size, d), 1)
    sides = jnp.zeros((size, d), F32)
    for row in range(n):
        z = zm[:, row * d : (row + 1) * d].astype(F32)
        zr[row] = z
        sides = jnp.where(lane == row, z[:, 0:1], sides)
        sides = jnp.where(lane == n + row, z[:, d - 1 : d], sides)
        term = z * rhs[row : row + 1, :]
        parts[row % 2] = term if parts[row % 2] is None else parts[row % 2] + term
    projected[...] = parts[0] + parts[1]
    face_y[...] = sides
    total = None
    for start in range(0, n, 8):
        for row in range(start, start + 8):
            z = zr[row]

            def c(i):
                return coef[i, row : row + 1, :]

            acc = c(0) * z
            if row + w < n:
                acc = acc - c(1) * zr[row + w]
            if row >= w:
                acc = acc - c(2) * zr[row - w]
            if row % w < w - 1:
                acc = acc - c(3) * zr[row + 1]
            if row % w > 0:
                acc = acc - c(4) * zr[row - 1]
            acc = acc - c(5) * pltpu.roll(z, d - 1, 1) - c(6) * pltpu.roll(z, 1, 1)
            at = slice(row * d, (row + 1) * d)
            hi, mid, lo = split3(acc)
            w3[0:size, at] = hi
            w3[size : 2 * size, at] = mid
            w3[2 * size : 3 * size, at] = lo
        part = dot_nt(w3[:, start * d : (start + 8) * d], zm[:, start * d : (start + 8) * d])
        total = part if total is None else total + part
    own[...] = fold3(total)


def pick(sources, targets, sems):
    for i, (index, target) in enumerate(targets):
        for j, source in enumerate(sources):

            @pl.when(index == j)
            def _(source=source, target=target, i=i):
                pltpu.make_async_copy(source, target, sems.at[i]).start()


def await_picks(sources, targets, sems):
    for i, (_, target) in enumerate(targets):
        pltpu.make_async_copy(sources[0], target, sems.at[i]).wait()


def fold(inverse):
    half = inverse.shape[0] // 2
    return jnp.concatenate([inverse[0:half, :], inverse[half:, :]], axis=1)


def unfold(folded):
    size = folded.shape[1] // 2
    return jnp.concatenate([folded[:, :size], folded[:, size:]], axis=0)


def k_setup(
    grid, pairs, cols, ids, cap, vent, cond, cond_low, cond_high, rec,
    zm, own_inner, projected, face_y, *rest,
):
    n, d, w, layers = grid.rows, grid.depth, grid.width, grid.layers
    held = [zm.at[:, pl.ds((n - w) * d, w * d)], *rest[:-12]]
    coef, own, inverse, sent, pay, mine, wanted, vents, names, w3, v0, sems = rest[-12:]
    count = rec.shape[0]
    panel = w * d
    line = w + 2 * layers
    sibling = lax.bitwise_xor(ids[pairs], 1)
    names_lane = lax.broadcasted_iota(jnp.int32, (1, d), 1)
    targets = []
    for k in range(pairs):
        theirs = jnp.where(names_lane == k, rec[sibling, line : line + 1, :], 0.0)
        for partner, target in (
            (ids[k], mine.at[k]),
            (jnp.sum(theirs).astype(jnp.int32), wanted.at[:, pl.ds(k * panel, panel)]),
        ):
            index = lax.shift_right_logical(lax.bitwise_xor(partner, ids[pairs]), 1)
            targets.append((index, target))
    pick(held, targets, sems)

    upward = lax.bitwise_and(ids[pairs], 1) == 0
    for z in range(layers):
        low_face = zm[:, z * panel : z * panel + d]
        high_face = zm[:, (z + 1) * panel - d : (z + 1) * panel]
        at = slice(pairs * panel + z * d, pairs * panel + (z + 1) * d)
        wanted[:, at] = jnp.where(upward, high_face.astype(F32), low_face.astype(F32)).astype(BF16)
    for k in range(pairs):
        vents[k] = vent[...] * rec[ids[k], 0:w, :]
    up, down = jnp.minimum(ids[pairs] + 1, count - 1), jnp.maximum(ids[pairs] - 1, 0)
    lines = [rec[r, line : line + 1, :] for r in (up, down)]
    lines += [cond_high[n : n + 1, :], cond_low[n : n + 1, :]]
    lines += [rec[ids[k], line : line + 1, :] for k in range(pairs)]
    names[...] = jnp.concatenate(lines, axis=0)
    vent_sum, low_x, high_x = received(grid, ids, pairs, rec)
    row_at, col_at = ids[pairs], ids[pairs + 1]
    low_x = jnp.where(row_at > 0, low_x, 0.0)
    high_x = jnp.where(row_at < count - 1, high_x, 0.0)
    low_y = jnp.where(col_at > 0, cond_low[0:n, :], 0.0)
    high_y = jnp.where(col_at < cols - 1, cond_high[0:n, :], 0.0)
    uz, lz, ux, lx, uy, ly = conductances(grid, cond[0:n, :], low_x, high_x, low_y, high_y)
    plenum = vent[...] * vent_sum
    diagonal = cap[...] + uz + lz + ux + lx + uy + ly
    coef[0] = jnp.concatenate([diagonal[:-w], diagonal[-w:] + plenum], axis=0)
    for i, c in enumerate((uz, lz, ux, lx, uy, ly)):
        coef[i + 1] = c
    last, first = [ux[z * w + w - 1 :][:1] for z in range(layers)], [lx[z * w :][:1] for z in range(layers)]
    top = [plenum[x : x + 1] for x in range(w)]
    top[0] = top[0] + first[-1]
    top[-1] = top[-1] + last[-1]
    row = n - w
    tops = zm[:, row * d :]
    block = own_inner[...] + weighted_gram(
        w3, [tops[:, x * d : (x + 1) * d] for x in range(w)], top, tops
    )
    for at, weights in ((0, first[:-1]), (panel - d, last[:-1])):
        parts = [zm[:, z * panel + at : z * panel + at + d] for z in range(layers - 1)]
        block = block + weighted_gram(w3, parts, weights, jnp.concatenate(parts, axis=1))
    sides = face_y[...].astype(BF16)
    block = block + weighted_gram(w3, [sides], [y_weights(grid, ly, uy)], sides)
    own[...] = block
    inverse[...] = invert_spd(block)
    y0 = solve_own(inverse, jnp.sum(projected[...], axis=1, keepdims=True))
    expand(grid, zm, y0, v0)
    field = v0[...]
    sent[0:n, :] = field
    to_all(grid, pay, vent[...] * field[-w:], field, fold(inverse))
    await_picks(held, targets, sems)


def incoming(grid, pairs, ids, rec, low, high):
    coupled, low_x, high_x = received(grid, ids, pairs, rec)
    n = grid.rows
    return coupled, low_x, high_x, low[0:n, :], high[0:n, :]


def k_coarse(
    grid, pairs, ids, coef, vent, zm, inverse, field, rec, low, high, face_y, _,
    out, wide, pay, solves, scratch,
):
    n, w = grid.rows, grid.width
    beside = operate(grid, coef, vent[...], None, incoming(grid, pairs, ids, rec, low, high))
    expand(grid, zm, solve_own(inverse, project(grid, zm, beside)), scratch)
    result = field[0:n, :] - scratch[...]
    out[...] = result
    size, half = zm.shape[0], solves.shape[1]
    wide[0:n, :] = result
    wide[n : n + size, :] = face_y[...]
    wide[n + size : n + size + half, :] = fold(inverse)
    to_all(grid, pay, vent[...] * result[-w:], result)
    first = w + 2 * grid.layers
    row_at = ids[pairs]
    solves[0] = rec[jnp.minimum(row_at + 1, rec.shape[0] - 1), first : first + half, :]
    solves[1] = rec[jnp.maximum(row_at - 1, 0), first : first + half, :]
    for k in range(pairs):
        solves[2 + k] = rec[ids[k], first : first + half, :]


def chosen(grid, pairs, ids, mine, others, k, at):
    panel = grid.width * grid.depth
    same = lax.bitwise_and(lax.bitwise_xor(ids[k], ids[pairs]), 1) == 0
    there = slice(k * panel + at.start, k * panel + at.stop)
    return jnp.where(same, mine[k, :, at].astype(F32), others[:, there].astype(F32))


def x_faces(grid, pairs, ids, others, far):
    near = others[:, pairs * grid.width * grid.depth :].astype(F32)
    across = jnp.concatenate([part[...].astype(F32) for part in far], axis=1)
    upward = lax.bitwise_and(ids[pairs], 1) == 0
    return jnp.where(upward, near, across), jnp.where(upward, across, near)


def k_partials(
    grid, pairs, base, ids, coef, vent, field, far_a, far_b, rec, low, high, vents, zm, low2, high2, mine,
    others, *rest,
):
    n, d, w, layers = grid.rows, grid.depth, grid.width, grid.layers
    size = zm.shape[0]
    base_ref = rest[0] if base else None
    out, pay = rest[-2:]
    next_first, prev_last = x_faces(grid, pairs, ids, others, (far_a, far_b))
    v = operate(grid, coef, vent[...], field[...], incoming(grid, pairs, ids, rec, low, high))
    if base:
        v = base_ref[...] - v
    out[...] = v
    face, zero = jnp.zeros((layers, d), F32), jnp.zeros((n, d), F32)
    own = operate(grid, coef, vent[...], v, (jnp.zeros((w, d), F32), face, face, zero, zero))

    def along(basis, weights):
        total = None
        for i, weight in enumerate(weights):
            term = basis[:, i * d : (i + 1) * d].astype(F32) * weight
            total = term if total is None else total + term
        return total

    even = along(zm, [own[i : i + 1] for i in range(n)])
    ux, lx, uy, ly = [coef[i] * v for i in (3, 4, 5, 6)]
    sums = [
        even,
        -along(next_first, [ux[z * w + w - 1 : z * w + w] for z in range(layers)]),
        -along(prev_last, [lx[z * w : z * w + 1] for z in range(layers)]),
    ]
    toward = pltpu.roll(y_weights(grid, ly, uy), n, 1)
    lane = lax.broadcasted_iota(jnp.int32, (1, d), 1)
    sums.append(-(high2[n : n + size, :] * jnp.where(lane < n, toward, 0.0)))
    sums.append(-(low2[n : n + size, :] * jnp.where(lane < n, 0.0, toward)))
    top = v[-w:]
    for k in range(pairs):
        weight = vents[k] * top
        total = None
        for x in range(w):
            part = chosen(grid, pairs, ids, mine, others, k, slice(x * d, (x + 1) * d))
            term = part * weight[x : x + 1]
            total = term if total is None else total + term
        sums.append(-total)
    eye = lax.broadcasted_iota(jnp.int32, (size, size), 0) == lax.broadcasted_iota(
        jnp.int32, (size, size), 1
    )
    rows = [
        jnp.sum(
            jnp.where(eye, jnp.sum(q, axis=1, keepdims=True), 0.0), axis=0, keepdims=True
        )
        for q in sums
    ]
    if len(rows) % 2:
        rows.append(jnp.zeros((1, size), F32))
    block = jnp.concatenate(
        [jnp.concatenate(rows[i : i + 2], axis=1) for i in range(0, len(rows), 2)], axis=0
    )
    for slot in range(pay.shape[0]):
        pay[slot] = block


def k_combine(grid, table, rec, weights, zm, base, vent, out, wide, pay, scratch):
    size = zm.shape[0]
    count = weights.shape[0]
    total = None
    for j in range(count):
        sides = [None, None]
        for i in range(count):
            at = table[j * count + i]
            line, side = divmod(opposite(i), 2)
            term = rec[at, line : line + 1, :]
            sides[side] = term if sides[side] is None else sides[side] + term
        term = weights[j] * (sides[0][:, 0:size] + sides[1][:, size : 2 * size])
        total = term if total is None else total + term
    expand(grid, zm, jnp.sum(total, axis=1, keepdims=True), scratch)
    result = base[...] - scratch[...]
    out[...] = result
    wide[0 : grid.rows, :] = result
    to_all(grid, pay, vent[...] * result[-grid.width :], result)


def k_dots(grid, pairs, ids, coef, vent, field, rec, low, high, r0, p0, i0, out, pay):
    image = operate(grid, coef, vent[...], field[...], incoming(grid, pairs, ids, rec, low, high))
    out[...] = image
    d, r, p, i = field[...], r0[...], p0[...], i0[...]
    products = (r * r, p * i, r * i, i * i, d * i, d * image)
    lane = lax.broadcasted_iota(jnp.int32, pay.shape[1:], 1)
    block = jnp.zeros(pay.shape[1:], F32)
    for k, q in enumerate(products):
        total = jnp.sum(jnp.sum(q, axis=0, keepdims=True), axis=1, keepdims=True)
        block = jnp.where(lane == k, total, block)
    for slot in range(pay.shape[0]):
        pay[slot] = block


def k_last(rec, x0, r0, p0, i0, d, image, x2, r2):
    total = rec[0]
    for slot in range(1, rec.shape[0]):
        total = total + rec[slot]
    rr, pi, ri, ii, di, dd = [total[0:1, k : k + 1] for k in range(6)]
    a1 = rr / pi
    new = rr - 2.0 * a1 * ri + a1 * a1 * ii
    grow = 1.0 + new / rr
    a2 = new / (grow * grow * pi - 2.0 * grow * a1 * di + a1 * a1 * dd)
    x2[...] = x0[...] + (a1 + a2 * grow) * p0[...] - (a2 * a1) * d[...]
    r2[...] = r0[...] - (a1 + a2 * grow) * i0[...] + (a2 * a1) * image[...]


def k_blocks(
    grid, pairs, cols, scale, ids, coef, vents, names, zm, mine, others, x_far_a, x_far_b, own, inverse,
    face_y, low2, high2, solves, _, out, weights, table, w3,
):
    n, d, w, layers = grid.rows, grid.depth, grid.width, grid.layers
    rows, size = out.shape[0], out.shape[1]
    row_at = ids[pairs]
    up, down = jnp.minimum(row_at + 1, rows - 1), jnp.maximum(row_at - 1, 0)

    col_at = ids[pairs + 1]
    lane = lax.broadcasted_iota(jnp.int32, (1, d), 1)
    near = [(row_at, col_at), (row_at + 1, col_at), (row_at - 1, col_at)]
    near += [(row_at, col_at + 1), (row_at, col_at - 1)]
    near += [(ids[k], col_at) for k in range(pairs)]
    count = len(near)
    for j, (r, c) in enumerate(near):
        places = [(r, c), (r + 1, c), (r - 1, c), (r, c + 1), (r, c - 1)]
        for k in range(pairs):
            met = ids[k]
            if j > 0:
                met = jnp.sum(jnp.where(lane == k, names[j - 1 : j, :], 0.0)).astype(jnp.int32)
            places.append((met, c))
        for i, (pr, pc) in enumerate(places):
            table[j * count + i] = lax.rem(pr + 2 * rows, rows) * cols + lax.rem(pc + 2 * cols, cols)

    def dot(a, b):
        return lax.dot_general(
            a, b, (((1,), (0,)), ((), ())),
            precision=lax.Precision.HIGHEST, preferred_element_type=F32,
        )

    ux, lx, uy, ly = coef[3], coef[4], coef[5], coef[6]
    last = [z * w + w - 1 for z in range(layers)]
    first = [z * w for z in range(layers)]

    def basis_rows(at):
        return [zm[:, i * d : (i + 1) * d] for i in at]

    next_first, prev_last = [f.astype(BF16) for f in x_faces(grid, pairs, ids, others, (x_far_a, x_far_b))]
    found = [
        weighted_gram(w3, basis_rows(last), [-ux[i : i + 1] for i in last], next_first),
        weighted_gram(w3, basis_rows(first), [-lx[i : i + 1] for i in first], prev_last),
    ]
    toward = -pltpu.roll(y_weights(grid, ly, uy), n, 1)
    swapped = pltpu.roll(face_y[...], n, 1)
    for theirs, there in ((high2, lane < n), (low2, lane >= n)):
        weight = jnp.where(there, toward, 0.0)
        found.append(weighted_gram(w3, [swapped], [weight], theirs[n : n + size, :].astype(BF16)))
    top = basis_rows(range(n - w, n))
    for k in range(pairs):
        panel = chosen(grid, pairs, ids, mine, others, k, slice(0, w * d)).astype(BF16)
        found.append(weighted_gram(w3, top, [-vents[k, i : i + 1, :] for i in range(w)], panel))

    for slot in range(rows):
        out[slot] = jnp.zeros((size, size), F32)
    out[row_at] = own[...] * scale
    out[up] = out[up] + jnp.where(row_at < rows - 1, found[0] * scale, 0.0)
    out[down] = out[down] + jnp.where(row_at > 0, found[1] * scale, 0.0)
    for k in range(pairs):
        out[ids[k]] = out[ids[k]] + found[4 + k] * scale

    weights[0] = inverse[...]
    start, stop = n + size, n + size + size // 2
    folded = [solves[0], solves[1], high2[start:stop, :], low2[start:stop, :]]
    folded += [solves[2 + k] for k in range(pairs)]
    for j, (block, theirs) in enumerate(zip(found, folded)):
        weights[j + 1] = -dot(inverse[...], dot(block, unfold(theirs)))


def call(kernel, outs, operands, scratch=(), smem=0, free=(), smem_outs=(), cost=None):
    specs = [
        SMEM if i < smem else ANY if i in free else VMEM for i in range(len(operands))
    ]
    return pl.pallas_call(
        kernel,
        out_shape=tuple(jax.ShapeDtypeStruct(s, t) for s, t in outs),
        in_specs=specs,
        out_specs=tuple(SMEM if i in smem_outs else VMEM for i in range(len(outs))),
        scratch_shapes=list(scratch),
        compiler_params=pltpu.CompilerParams(vmem_limit_bytes=VMEM_LIMIT),
        cost_estimate=cost,
    )(*operands)


def body(forcing_right_hand, material, capacity, conductivity, vent_open, partners, subspace_basis):
    layers, width, depth = forcing_right_hand.shape
    size = subspace_basis.shape[0]
    grid = Grid(layers, width, depth)
    n, cells = grid.rows, forcing_right_hand.size
    row_count, col_count = lax.axis_size("row"), lax.axis_size("col")
    pairs = partners.shape[-1]
    ids = jnp.concatenate(
        [
            partners.reshape(-1),
            jnp.stack([lax.axis_index("row"), lax.axis_index("col")]).astype(jnp.int32),
        ]
    )
    rhs = forcing_right_hand.reshape(n, depth)
    classes = material.reshape(n, depth)
    basis = subspace_basis.reshape(size, n, depth)
    field = ((n, depth), F32)
    pay = ((row_count, width + 2 * layers, depth), F32)
    small = ((size, size), F32)
    wide = ((max(n + size + size // 2, row_count * (width + 2 * layers) + 8), depth), F32)

    def cyclic(value, axis, step):
        count = lax.axis_size(axis)
        return lax.ppermute(value, axis, [(i, (i + step) % count) for i in range(count)])

    def xor_step(value, axis, k):
        count = lax.axis_size(axis)
        return lax.ppermute(value, axis, [(i, i ^ k) for i in range(count)])

    def exchange(value, payload):
        low = cyclic(value, "col", 1)
        high = cyclic(value, "col", -1)
        rec = lax.all_to_all(payload, "row", 0, 0)
        return rec, low, high

    def rows_of(count):
        return ((row_count, width + 2 * layers + count, depth), F32)

    tables = jnp.concatenate([conductivity, capacity, partners.reshape(-1).astype(F32)])
    zm, panel, *face = call(
        functools.partial(k_order, grid),
        (
            ((size, n * depth), BF16),
            ((size, width * depth), BF16),
            ((size, layers // 2 * depth), BF16),
            ((size, (layers - layers // 2) * depth), BF16),
        ),
        (basis,),
        cost=pl.CostEstimate(flops=1000, bytes_accessed=1000, transcendentals=0),
    )
    held = [xor_step(panel, "row", k) for k in range(2, row_count, 2)]
    across = [(i, (i + 1 if i % 2 else i - 1) % row_count) for i in range(row_count)]
    x_far_a, x_far_b = [lax.ppermute(part, "row", across) for part in face]
    cond, cap, vent, pay0 = call(
        functools.partial(k_first, grid, pairs),
        (((n + 8, depth), F32), field, ((width, depth), F32), rows_of(8)),
        (tables, classes, vent_open),
        smem=1,
    )
    rec0, cond_low, cond_high = exchange(cond, pay0)

    own_inner, projected, face_y = call(
        functools.partial(k_basis, grid),
        (small, ((size, depth), F32), ((size, depth), F32)),
        (zm, rhs, cond, cap),
        scratch=(
            pltpu.VMEM((n, size, depth), F32),
            pltpu.VMEM((3 * size, n * depth), BF16),
            pltpu.VMEM((7, n, depth), F32),
        ),
        cost=pl.CostEstimate(flops=1000, bytes_accessed=1000, transcendentals=0),
    )

    panels = ((pairs, size, width * depth), BF16)
    coef, own, inverse, sent, pay1, mine, wanted, vents, names = call(
        functools.partial(k_setup, grid, pairs, col_count),
        (
            ((7, n, depth), F32),
            small,
            small,
            ((n + 8, depth), F32),
            rows_of(size // 2),
            panels,
            ((size, (pairs * width + layers) * depth), BF16),
            ((pairs, width, depth), F32),
            ((4 + pairs, depth), F32),
        ),
        (
            ids, cap, vent, cond, cond_low, cond_high, rec0, zm, own_inner, projected, face_y,
            *held,
        ),
        scratch=(
            pltpu.VMEM((3 * size, n * depth), BF16),
            pltpu.VMEM((n, depth), F32),
            pltpu.SemaphoreType.DMA((2 * pairs,)),
        ),
        smem=1,
        free=range(11, 11 + len(held)),
    )
    others = xor_step(wanted, "row", 1)
    rec1, low1, high1 = exchange(sent, pay1)
    places = 5 + pairs
    x0, wide2, pay2, solves = call(
        functools.partial(k_coarse, grid, pairs),
        (field, wide, pay, ((2 + pairs, size // 2, depth), F32)),
        (ids, coef, vent, zm, inverse, sent, rec1, low1, high1, face_y, others),
        scratch=(pltpu.VMEM((n, depth), F32),),
        smem=1,
        free=(10,),
    )
    pay2, x_far_a, x_far_b = lax.optimization_barrier((pay2, x_far_a, x_far_b))
    rec, low2, high2 = exchange(wide2, pay2)

    def everyone(lines):
        return ((row_count * col_count, lines, depth), F32)

    r0, pay3 = call(
        functools.partial(k_partials, grid, pairs, True),
        (field, everyone((places + 1) // 2)),
        (
            ids, coef, vent, x0, x_far_a, x_far_b, rec, low2, high2, vents, zm, low2, high2, mine, others, rhs,
        ),
        smem=1,
    )
    blocks, weights, table = call(
        functools.partial(k_blocks, grid, pairs, col_count, 1.0 / cells),
        (
            ((row_count, size, size), F32),
            ((places, size, size), F32),
            ((places * places,), jnp.int32),
        ),
        (
            ids, coef, vents, names, zm, mine, others, x_far_a, x_far_b, own, inverse, face_y, low2,
            high2, solves, pay3,
        ),
        scratch=(pltpu.VMEM((3 * size, width * depth), BF16),),
        smem=1,
        free=(15,),
        smem_outs=(2,),
        cost=pl.CostEstimate(flops=100_000_000, bytes_accessed=4_000_000, transcendentals=0),
    )
    sums = lax.all_to_all(pay3, ("row", "col"), 0, 0)
    p0, wide4, pay4 = call(
        functools.partial(k_combine, grid),
        (field, wide, pay),
        (table, sums, weights, zm, r0, vent),
        scratch=(pltpu.VMEM((n, depth), F32),),
        smem=1,
    )
    rec, low, high = exchange(wide4, pay4)
    i0, pay5 = call(
        functools.partial(k_partials, grid, pairs, False),
        (field, everyone((places + 1) // 2)),
        (
            ids, coef, vent, p0, x_far_a, x_far_b, rec, low, high, vents, zm, low2, high2, mine, others,
        ),
        smem=1,
    )
    sums = lax.all_to_all(pay5, ("row", "col"), 0, 0)
    d0, wide6, pay6 = call(
        functools.partial(k_combine, grid),
        (field, wide, pay),
        (table, sums, weights, zm, i0, vent),
        scratch=(pltpu.VMEM((n, depth), F32),),
        smem=1,
    )
    rec, low, high = exchange(wide6, pay6)
    image, pay7 = call(
        functools.partial(k_dots, grid, pairs),
        (field, everyone(2)),
        (ids, coef, vent, d0, rec, low, high, r0, p0, i0),
        smem=1,
    )
    total = lax.all_to_all(pay7, ("row", "col"), 0, 0)
    x2, r2 = call(k_last, (field, field), (total, x0, r0, p0, i0, d0, image))
    shape = forcing_right_hand.shape
    return x2.reshape(shape), r2.reshape(shape), blocks[None, None]


def solution(mesh):
    return jax.shard_map(
        body,
        mesh=mesh,
        in_specs=(
            P(None, "row", "col"),
            P(None, "row", "col"),
            P(),
            P(),
            P("row", "col"),
            P("row", "col", None),
            P(None, None, "row", "col"),
        ),
        out_specs=(P(None, "row", "col"), P(None, "row", "col"), P("row", "col", None, None, None)),
        check_vma=False,
    )
```

```python
import functools

import jax
import jax.numpy as jnp
from jax import lax
from jax.experimental import pallas as pl
from jax.experimental.pallas import tpu as pltpu
from jax.sharding import PartitionSpec as P

F32 = jnp.float32
BF16 = jnp.bfloat16
VMEM = pl.BlockSpec(memory_space=pltpu.VMEM)
SMEM = pl.BlockSpec(memory_space=pltpu.SMEM)
ANY = pl.BlockSpec(memory_space=pl.ANY)
VMEM_LIMIT = 16 * 1024 * 1024


def harmonic(a, b):
    return 2.0 * a * b / (a + b)


def lookup(material, table):
    result = jnp.zeros(material.shape, F32)
    for class_id in range(len(table)):
        result = jnp.where(material == class_id, table[class_id], result)
    return result


class Grid:
    def __init__(self, layers, width, depth):
        self.layers, self.width, self.depth = layers, width, depth
        self.rows = layers * width

    def masks(self):
        shape = (self.rows, self.depth)
        row = lax.broadcasted_iota(jnp.int32, shape, 0)
        lane = lax.broadcasted_iota(jnp.int32, shape, 1)
        return lax.rem(row, self.width), lane, row

    def spread(self, face):
        parts = [
            jnp.broadcast_to(face[z : z + 1], (self.width, self.depth)) for z in range(self.layers)
        ]
        return jnp.concatenate(parts, axis=0)

    def faces(self, v):
        w = self.width
        last = [v[z * w + w - 1 : z * w + w] for z in range(self.layers)]
        first = [v[z * w : z * w + 1] for z in range(self.layers)]
        return last + first

    def payload(self, top, v):
        return jnp.concatenate([top] + self.faces(v), axis=0)

    def around(self, v, low_x, high_x, low_y, high_y):
        xi, lane, _ = self.masks()
        n, d = self.rows, self.depth
        zero = jnp.zeros((n, d), F32)
        own = zero if v is None else v
        plus = zero if v is None else pltpu.roll(v, n - 1, 0)
        minus = zero if v is None else pltpu.roll(v, 1, 0)
        up_x = jnp.where(xi == self.width - 1, self.spread(high_x), plus)
        down_x = jnp.where(xi == 0, self.spread(low_x), minus)
        up_y = pltpu.roll(jnp.where(lane == 0, high_y, own), d - 1, 1)
        down_y = pltpu.roll(jnp.where(lane == d - 1, low_y, own), 1, 1)
        return up_x, down_x, up_y, down_y

    def shifted_z(self, v):
        w = self.width
        return jnp.concatenate([v[w:], v[:w]], axis=0), jnp.concatenate([v[-w:], v[:-w]], axis=0)


def received(grid, ids, pairs, rec):
    count = rec.shape[0]
    w, layers = grid.width, grid.layers
    coupled = rec[ids[0], 0:w, :]
    for k in range(1, pairs):
        coupled = coupled + rec[ids[k], 0:w, :]
    row_at = ids[pairs]
    low = rec[jnp.maximum(row_at - 1, 0), w : w + layers, :]
    high = rec[jnp.minimum(row_at + 1, count - 1), w + layers : w + 2 * layers, :]
    return coupled, low, high


def operate(grid, coef, vent, v, rest):
    coupled, low_x, high_x, low_y, high_y = rest
    up_x, down_x, up_y, down_y = grid.around(v, low_x, high_x, low_y, high_y)
    beside = coef[3] * up_x + coef[4] * down_x + coef[5] * up_y + coef[6] * down_y
    if v is None:
        xi, lane, _ = grid.masks()
        result = -beside
    else:
        up_z, down_z = grid.shifted_z(v)
        result = coef[0] * v - (beside + coef[1] * up_z + coef[2] * down_z)
    w = grid.width
    return jnp.concatenate([result[:-w], result[-w:] - vent * coupled], axis=0)


def project(grid, zm, v):
    d = grid.depth
    parts = [None, None]
    for row in range(grid.rows):
        term = zm[:, row * d : (row + 1) * d].astype(F32) * v[row : row + 1, :]
        k = row % 2
        parts[k] = term if parts[k] is None else parts[k] + term
    return jnp.sum(parts[0] + parts[1], axis=1, keepdims=True)


def solve_own(inverse, column):
    size = inverse.shape[0]
    along = jnp.sum(inverse[...] * column, axis=0, keepdims=True)
    eye = lax.broadcasted_iota(jnp.int32, (size, size), 0) == lax.broadcasted_iota(
        jnp.int32, (size, size), 1
    )
    return jnp.sum(jnp.where(eye, along, 0.0), axis=1, keepdims=True)


def expand(grid, zm, column, out):
    d = grid.depth
    wide = jnp.broadcast_to(column, (column.shape[0], d))
    for row in range(grid.rows):
        out[row : row + 1, :] = jnp.sum(
            zm[:, row * d : (row + 1) * d].astype(F32) * wide, axis=0, keepdims=True
        )


def to_all(grid, pay, top, v, *more):
    block = jnp.concatenate([grid.payload(top, v), *more], axis=0)
    for slot in range(pay.shape[0]):
        pay[slot] = block


def split3(w):
    hi = w.astype(BF16)
    rest = w - hi.astype(F32)
    mid = rest.astype(BF16)
    lo = (rest - mid.astype(F32)).astype(BF16)
    return hi, mid, lo


def dot_nt(a, b):
    return lax.dot_general(a, b, (((1,), (1,)), ((), ())), preferred_element_type=F32)


def fold3(stacked):
    size = stacked.shape[0] // 3
    return stacked[:size] + (stacked[size : 2 * size] + stacked[2 * size :])


def weighted_gram(w3, parts, weights, other):
    size = other.shape[0]
    k = other.shape[1] // len(weights)
    for i, (part, weight) in enumerate(zip(parts, weights)):
        at = slice(i * k, (i + 1) * k)
        hi, mid, lo = split3(part.astype(F32) * weight)
        w3[0:size, at] = hi
        w3[size : 2 * size, at] = mid
        w3[2 * size : 3 * size, at] = lo
    return fold3(dot_nt(w3[:, : len(weights) * k], other))


def y_weights(grid, first, last):
    n, d = grid.rows, grid.depth
    row = lax.broadcasted_iota(jnp.int32, (n, d), 0)
    lane = lax.broadcasted_iota(jnp.int32, (n, d), 1)
    wide = jnp.where(lane == row, first[:, 0:1], 0.0)
    wide = wide + jnp.where(lane == n + row, last[:, d - 1 : d], 0.0)
    return jnp.sum(wide, axis=0, keepdims=True)


def invert_spd(m, ahead=5):
    size = m.shape[0]
    row_id = lax.broadcasted_iota(jnp.int32, (size, size), 0)
    col_id = lax.broadcasted_iota(jnp.int32, (size, size), 1)

    def column(k):
        return jnp.broadcast_to(m[:, k : k + 1], (size, size))

    waiting = {k: column(k) for k in range(min(ahead + 1, size))}
    for k in range(size):
        col = waiting.pop(k)
        inv = 1.0 / col[k : k + 1, :]
        for j in list(waiting):
            at_row = col[j : j + 1, :] * inv
            waiting[j] = jnp.where(row_id == k, at_row, waiting[j] - col * at_row)
        scaled_row = jnp.where(col_id[:1] == k, -inv, m[k : k + 1, :] * inv)
        m = jnp.where(row_id == k, scaled_row, jnp.where(col_id == k, 0.0, m) - col * scaled_row)
        if k + ahead + 1 < size:
            waiting[k + ahead + 1] = column(k + ahead + 1)
    return -m


def opposite(place):
    return {1: 2, 2: 1, 3: 4, 4: 3}.get(place, place)


def k_first(
    grid, pairs, tables, material, vent, cond_out, cap_out, vent_out, pay
):
    classes = (tables.shape[0] - pairs) // 2
    conductivity = [tables[i] for i in range(classes)]
    capacity = [tables[classes + i] for i in range(classes)]
    cond = lookup(material[...], conductivity)
    lane = lax.broadcasted_iota(jnp.int32, (8, grid.depth), 1)
    names = jnp.zeros((8, grid.depth), F32)
    for k in range(pairs):
        names = jnp.where(lane == k, tables[2 * classes + k], names)
    cond_out[0 : grid.rows, :] = cond
    cond_out[grid.rows :, :] = names
    cap_out[...] = lookup(material[...], capacity)
    vent_out[...] = vent[...]
    to_all(grid, pay, vent[...], cond, names[0:1])


def conductances(grid, cond, low_x, high_x, low_y, high_y):
    _, _, row = grid.masks()
    up_z, down_z = grid.shifted_z(cond)
    uz = jnp.where(row < grid.rows - grid.width, harmonic(cond, up_z), 0.0)
    lz = jnp.where(row >= grid.width, harmonic(cond, down_z), 0.0)
    ux, lx, uy, ly = [harmonic(cond, c) for c in grid.around(cond, low_x, high_x, low_y, high_y)]
    return uz, lz, ux, lx, uy, ly


def k_order(grid, basis, zm, panel, face_a, face_b):
    n, d, w, layers = grid.rows, grid.depth, grid.width, grid.layers
    size = basis.shape[0]
    odd = lax.bitwise_and(lax.axis_index("row"), 1) == 1

    for row in range(0, n, w):
        for a in range(0, size, w):
            turned = jnp.swapaxes(basis[a : a + w, row : row + w, :], 0, 1)
            for i in range(w):
                zm[a : a + w, (row + i) * d : (row + i + 1) * d] = turned[i]
    panel[...] = zm[:, (n - w) * d :]
    for z in range(layers):
        start = z * w * d
        first = zm[:, start : start + d].astype(F32)
        last = zm[:, start + (w - 1) * d : start + w * d].astype(F32)
        half = layers // 2
        face, at = (face_a, z) if z < half else (face_b, z - half)
        face[:, at * d : (at + 1) * d] = jnp.where(odd, last, first).astype(BF16)


def k_basis(grid, zm, rhs, cond_ref, cap_ref, own, projected, face_y, zr, w3, coef):
    n, d, w = grid.rows, grid.depth, grid.width
    size = zm.shape[0]
    cond = cond_ref[0:n, :]
    zero_face = jnp.zeros((grid.layers, d), F32)
    zero = jnp.zeros((n, d), F32)
    uz, lz, ux, lx, uy, ly = conductances(grid, cond, zero_face, zero_face, zero, zero)
    coef[0] = cap_ref[...] + uz + lz + ux + lx + uy + ly
    for i, c in enumerate((uz, lz, ux, lx, uy, ly)):
        coef[i + 1] = c

    parts = [None, None]
    lane = lax.broadcasted_iota(jnp.int32, (size, d), 1)
    sides = jnp.zeros((size, d), F32)
    for row in range(n):
        z = zm[:, row * d : (row + 1) * d].astype(F32)
        zr[row] = z
        sides = jnp.where(lane == row, z[:, 0:1], sides)
        sides = jnp.where(lane == n + row, z[:, d - 1 : d], sides)
        term = z * rhs[row : row + 1, :]
        parts[row % 2] = term if parts[row % 2] is None else parts[row % 2] + term
    projected[...] = parts[0] + parts[1]
    face_y[...] = sides
    total = None
    for start in range(0, n, 8):
        for row in range(start, start + 8):
            z = zr[row]

            def c(i):
                return coef[i, row : row + 1, :]

            acc = c(0) * z
            if row + w < n:
                acc = acc - c(1) * zr[row + w]
            if row >= w:
                acc = acc - c(2) * zr[row - w]
            if row % w < w - 1:
                acc = acc - c(3) * zr[row + 1]
            if row % w > 0:
                acc = acc - c(4) * zr[row - 1]
            acc = acc - c(5) * pltpu.roll(z, d - 1, 1) - c(6) * pltpu.roll(z, 1, 1)
            at = slice(row * d, (row + 1) * d)
            hi, mid, lo = split3(acc)
            w3[0:size, at] = hi
            w3[size : 2 * size, at] = mid
            w3[2 * size : 3 * size, at] = lo
        part = dot_nt(w3[:, start * d : (start + 8) * d], zm[:, start * d : (start + 8) * d])
        total = part if total is None else total + part
    own[...] = fold3(total)


def pick(sources, targets, sems):
    for i, (index, target) in enumerate(targets):
        for j, source in enumerate(sources):

            @pl.when(index == j)
            def _(source=source, target=target, i=i):
                pltpu.make_async_copy(source, target, sems.at[i]).start()


def await_picks(sources, targets, sems):
    for i, (_, target) in enumerate(targets):
        pltpu.make_async_copy(sources[0], target, sems.at[i]).wait()


def fold(inverse):
    half = inverse.shape[0] // 2
    return jnp.concatenate([inverse[0:half, :], inverse[half:, :]], axis=1)


def unfold(folded):
    size = folded.shape[1] // 2
    return jnp.concatenate([folded[:, :size], folded[:, size:]], axis=0)


def k_setup(
    grid, pairs, cols, ids, cap, vent, cond, cond_low, cond_high, rec,
    zm, own_inner, projected, face_y, *rest,
):
    n, d, w, layers = grid.rows, grid.depth, grid.width, grid.layers
    held = [zm.at[:, pl.ds((n - w) * d, w * d)], *rest[:-12]]
    coef, own, inverse, sent, pay, mine, wanted, vents, names, w3, v0, sems = rest[-12:]
    count = rec.shape[0]
    panel = w * d
    line = w + 2 * layers
    sibling = lax.bitwise_xor(ids[pairs], 1)
    names_lane = lax.broadcasted_iota(jnp.int32, (1, d), 1)
    targets = []
    for k in range(pairs):
        theirs = jnp.where(names_lane == k, rec[sibling, line : line + 1, :], 0.0)
        for partner, target in (
            (ids[k], mine.at[k]),
            (jnp.sum(theirs).astype(jnp.int32), wanted.at[:, pl.ds(k * panel, panel)]),
        ):
            index = lax.shift_right_logical(lax.bitwise_xor(partner, ids[pairs]), 1)
            targets.append((index, target))
    pick(held, targets, sems)

    upward = lax.bitwise_and(ids[pairs], 1) == 0
    for z in range(layers):
        low_face = zm[:, z * panel : z * panel + d]
        high_face = zm[:, (z + 1) * panel - d : (z + 1) * panel]
        at = slice(pairs * panel + z * d, pairs * panel + (z + 1) * d)
        wanted[:, at] = jnp.where(upward, high_face.astype(F32), low_face.astype(F32)).astype(BF16)
    for k in range(pairs):
        vents[k] = vent[...] * rec[ids[k], 0:w, :]
    up, down = jnp.minimum(ids[pairs] + 1, count - 1), jnp.maximum(ids[pairs] - 1, 0)
    lines = [rec[r, line : line + 1, :] for r in (up, down)]
    lines += [cond_high[n : n + 1, :], cond_low[n : n + 1, :]]
    lines += [rec[ids[k], line : line + 1, :] for k in range(pairs)]
    names[...] = jnp.concatenate(lines, axis=0)
    vent_sum, low_x, high_x = received(grid, ids, pairs, rec)
    row_at, col_at = ids[pairs], ids[pairs + 1]
    low_x = jnp.where(row_at > 0, low_x, 0.0)
    high_x = jnp.where(row_at < count - 1, high_x, 0.0)
    low_y = jnp.where(col_at > 0, cond_low[0:n, :], 0.0)
    high_y = jnp.where(col_at < cols - 1, cond_high[0:n, :], 0.0)
    uz, lz, ux, lx, uy, ly = conductances(grid, cond[0:n, :], low_x, high_x, low_y, high_y)
    plenum = vent[...] * vent_sum
    diagonal = cap[...] + uz + lz + ux + lx + uy + ly
    coef[0] = jnp.concatenate([diagonal[:-w], diagonal[-w:] + plenum], axis=0)
    for i, c in enumerate((uz, lz, ux, lx, uy, ly)):
        coef[i + 1] = c
    last, first = [ux[z * w + w - 1 :][:1] for z in range(layers)], [lx[z * w :][:1] for z in range(layers)]
    top = [plenum[x : x + 1] for x in range(w)]
    top[0] = top[0] + first[-1]
    top[-1] = top[-1] + last[-1]
    row = n - w
    tops = zm[:, row * d :]
    block = own_inner[...] + weighted_gram(
        w3, [tops[:, x * d : (x + 1) * d] for x in range(w)], top, tops
    )
    for at, weights in ((0, first[:-1]), (panel - d, last[:-1])):
        parts = [zm[:, z * panel + at : z * panel + at + d] for z in range(layers - 1)]
        block = block + weighted_gram(w3, parts, weights, jnp.concatenate(parts, axis=1))
    sides = face_y[...].astype(BF16)
    block = block + weighted_gram(w3, [sides], [y_weights(grid, ly, uy)], sides)
    own[...] = block
    inverse[...] = invert_spd(block)
    y0 = solve_own(inverse, jnp.sum(projected[...], axis=1, keepdims=True))
    expand(grid, zm, y0, v0)
    field = v0[...]
    sent[0:n, :] = field
    to_all(grid, pay, vent[...] * field[-w:], field, fold(inverse))
    await_picks(held, targets, sems)


def incoming(grid, pairs, ids, rec, low, high):
    coupled, low_x, high_x = received(grid, ids, pairs, rec)
    n = grid.rows
    return coupled, low_x, high_x, low[0:n, :], high[0:n, :]


def k_coarse(
    grid, pairs, ids, coef, vent, zm, inverse, field, rec, low, high, face_y, _,
    out, wide, pay, solves, scratch,
):
    n, w = grid.rows, grid.width
    beside = operate(grid, coef, vent[...], None, incoming(grid, pairs, ids, rec, low, high))
    expand(grid, zm, solve_own(inverse, project(grid, zm, beside)), scratch)
    result = field[0:n, :] - scratch[...]
    out[...] = result
    size, half = zm.shape[0], solves.shape[1]
    wide[0:n, :] = result
    wide[n : n + size, :] = face_y[...]
    wide[n + size : n + size + half, :] = fold(inverse)
    to_all(grid, pay, vent[...] * result[-w:], result)
    first = w + 2 * grid.layers
    row_at = ids[pairs]
    solves[0] = rec[jnp.minimum(row_at + 1, rec.shape[0] - 1), first : first + half, :]
    solves[1] = rec[jnp.maximum(row_at - 1, 0), first : first + half, :]
    for k in range(pairs):
        solves[2 + k] = rec[ids[k], first : first + half, :]


def chosen(grid, pairs, ids, mine, others, k, at):
    panel = grid.width * grid.depth
    same = lax.bitwise_and(lax.bitwise_xor(ids[k], ids[pairs]), 1) == 0
    there = slice(k * panel + at.start, k * panel + at.stop)
    return jnp.where(same, mine[k, :, at].astype(F32), others[:, there].astype(F32))


def x_faces(grid, pairs, ids, others, far):
    near = others[:, pairs * grid.width * grid.depth :].astype(F32)
    across = jnp.concatenate([part[...].astype(F32) for part in far], axis=1)
    upward = lax.bitwise_and(ids[pairs], 1) == 0
    return jnp.where(upward, near, across), jnp.where(upward, across, near)


def k_partials(
    grid, pairs, base, ids, coef, vent, field, far_a, far_b, rec, low, high, vents, zm, low2, high2, mine,
    others, *rest,
):
    n, d, w, layers = grid.rows, grid.depth, grid.width, grid.layers
    size = zm.shape[0]
    base_ref = rest[0] if base else None
    out, pay = rest[-2:]
    next_first, prev_last = x_faces(grid, pairs, ids, others, (far_a, far_b))
    v = operate(grid, coef, vent[...], field[...], incoming(grid, pairs, ids, rec, low, high))
    if base:
        v = base_ref[...] - v
    out[...] = v
    face, zero = jnp.zeros((layers, d), F32), jnp.zeros((n, d), F32)
    own = operate(grid, coef, vent[...], v, (jnp.zeros((w, d), F32), face, face, zero, zero))

    def along(basis, weights):
        total = None
        for i, weight in enumerate(weights):
            term = basis[:, i * d : (i + 1) * d].astype(F32) * weight
            total = term if total is None else total + term
        return total

    even = along(zm, [own[i : i + 1] for i in range(n)])
    ux, lx, uy, ly = [coef[i] * v for i in (3, 4, 5, 6)]
    sums = [
        even,
        -along(next_first, [ux[z * w + w - 1 : z * w + w] for z in range(layers)]),
        -along(prev_last, [lx[z * w : z * w + 1] for z in range(layers)]),
    ]
    toward = pltpu.roll(y_weights(grid, ly, uy), n, 1)
    lane = lax.broadcasted_iota(jnp.int32, (1, d), 1)
    sums.append(-(high2[n : n + size, :] * jnp.where(lane < n, toward, 0.0)))
    sums.append(-(low2[n : n + size, :] * jnp.where(lane < n, 0.0, toward)))
    top = v[-w:]
    for k in range(pairs):
        weight = vents[k] * top
        total = None
        for x in range(w):
            part = chosen(grid, pairs, ids, mine, others, k, slice(x * d, (x + 1) * d))
            term = part * weight[x : x + 1]
            total = term if total is None else total + term
        sums.append(-total)
    eye = lax.broadcasted_iota(jnp.int32, (size, size), 0) == lax.broadcasted_iota(
        jnp.int32, (size, size), 1
    )
    rows = [
        jnp.sum(
            jnp.where(eye, jnp.sum(q, axis=1, keepdims=True), 0.0), axis=0, keepdims=True
        )
        for q in sums
    ]
    if len(rows) % 2:
        rows.append(jnp.zeros((1, size), F32))
    block = jnp.concatenate(
        [jnp.concatenate(rows[i : i + 2], axis=1) for i in range(0, len(rows), 2)], axis=0
    )
    for slot in range(pay.shape[0]):
        pay[slot] = block


def k_combine(grid, table, rec, weights, zm, base, vent, out, wide, pay, scratch):
    size = zm.shape[0]
    count = weights.shape[0]
    total = None
    for j in range(count):
        sides = [None, None]
        for i in range(count):
            at = table[j * count + i]
            line, side = divmod(opposite(i), 2)
            term = rec[at, line : line + 1, :]
            sides[side] = term if sides[side] is None else sides[side] + term
        term = weights[j] * (sides[0][:, 0:size] + sides[1][:, size : 2 * size])
        total = term if total is None else total + term
    expand(grid, zm, jnp.sum(total, axis=1, keepdims=True), scratch)
    result = base[...] - scratch[...]
    out[...] = result
    wide[0 : grid.rows, :] = result
    to_all(grid, pay, vent[...] * result[-grid.width :], result)


def k_dots(grid, pairs, ids, coef, vent, field, rec, low, high, r0, p0, i0, out, pay):
    image = operate(grid, coef, vent[...], field[...], incoming(grid, pairs, ids, rec, low, high))
    out[...] = image
    d, r, p, i = field[...], r0[...], p0[...], i0[...]
    products = (r * r, p * i, r * i, i * i, d * i, d * image)
    lane = lax.broadcasted_iota(jnp.int32, pay.shape[1:], 1)
    block = jnp.zeros(pay.shape[1:], F32)
    for k, q in enumerate(products):
        total = jnp.sum(jnp.sum(q, axis=0, keepdims=True), axis=1, keepdims=True)
        block = jnp.where(lane == k, total, block)
    for slot in range(pay.shape[0]):
        pay[slot] = block


def k_last(rec, x0, r0, p0, i0, d, image, x2, r2):
    total = rec[0]
    for slot in range(1, rec.shape[0]):
        total = total + rec[slot]
    rr, pi, ri, ii, di, dd = [total[0:1, k : k + 1] for k in range(6)]
    a1 = rr / pi
    new = rr - 2.0 * a1 * ri + a1 * a1 * ii
    grow = 1.0 + new / rr
    a2 = new / (grow * grow * pi - 2.0 * grow * a1 * di + a1 * a1 * dd)
    x2[...] = x0[...] + (a1 + a2 * grow) * p0[...] - (a2 * a1) * d[...]
    r2[...] = r0[...] - (a1 + a2 * grow) * i0[...] + (a2 * a1) * image[...]


def k_blocks(
    grid, pairs, cols, scale, ids, coef, vents, names, zm, mine, others, x_far_a, x_far_b, own, inverse,
    face_y, low2, high2, solves, _, out, weights, table, w3,
):
    n, d, w, layers = grid.rows, grid.depth, grid.width, grid.layers
    rows, size = out.shape[0], out.shape[1]
    row_at = ids[pairs]
    up, down = jnp.minimum(row_at + 1, rows - 1), jnp.maximum(row_at - 1, 0)

    col_at = ids[pairs + 1]
    lane = lax.broadcasted_iota(jnp.int32, (1, d), 1)
    near = [(row_at, col_at), (row_at + 1, col_at), (row_at - 1, col_at)]
    near += [(row_at, col_at + 1), (row_at, col_at - 1)]
    near += [(ids[k], col_at) for k in range(pairs)]
    count = len(near)
    for j, (r, c) in enumerate(near):
        places = [(r, c), (r + 1, c), (r - 1, c), (r, c + 1), (r, c - 1)]
        for k in range(pairs):
            met = ids[k]
            if j > 0:
                met = jnp.sum(jnp.where(lane == k, names[j - 1 : j, :], 0.0)).astype(jnp.int32)
            places.append((met, c))
        for i, (pr, pc) in enumerate(places):
            table[j * count + i] = lax.rem(pr + 2 * rows, rows) * cols + lax.rem(pc + 2 * cols, cols)

    def dot(a, b):
        return lax.dot_general(
            a, b, (((1,), (0,)), ((), ())),
            precision=lax.Precision.HIGHEST, preferred_element_type=F32,
        )

    ux, lx, uy, ly = coef[3], coef[4], coef[5], coef[6]
    last = [z * w + w - 1 for z in range(layers)]
    first = [z * w for z in range(layers)]

    def basis_rows(at):
        return [zm[:, i * d : (i + 1) * d] for i in at]

    next_first, prev_last = [f.astype(BF16) for f in x_faces(grid, pairs, ids, others, (x_far_a, x_far_b))]
    found = [
        weighted_gram(w3, basis_rows(last), [-ux[i : i + 1] for i in last], next_first),
        weighted_gram(w3, basis_rows(first), [-lx[i : i + 1] for i in first], prev_last),
    ]
    toward = -pltpu.roll(y_weights(grid, ly, uy), n, 1)
    swapped = pltpu.roll(face_y[...], n, 1)
    for theirs, there in ((high2, lane < n), (low2, lane >= n)):
        weight = jnp.where(there, toward, 0.0)
        found.append(weighted_gram(w3, [swapped], [weight], theirs[n : n + size, :].astype(BF16)))
    top = basis_rows(range(n - w, n))
    for k in range(pairs):
        panel = chosen(grid, pairs, ids, mine, others, k, slice(0, w * d)).astype(BF16)
        found.append(weighted_gram(w3, top, [-vents[k, i : i + 1, :] for i in range(w)], panel))

    for slot in range(rows):
        out[slot] = jnp.zeros((size, size), F32)
    out[row_at] = own[...] * scale
    out[up] = out[up] + jnp.where(row_at < rows - 1, found[0] * scale, 0.0)
    out[down] = out[down] + jnp.where(row_at > 0, found[1] * scale, 0.0)
    for k in range(pairs):
        out[ids[k]] = out[ids[k]] + found[4 + k] * scale

    weights[0] = inverse[...]
    start, stop = n + size, n + size + size // 2
    folded = [solves[0], solves[1], high2[start:stop, :], low2[start:stop, :]]
    folded += [solves[2 + k] for k in range(pairs)]
    for j, (block, theirs) in enumerate(zip(found, folded)):
        weights[j + 1] = -dot(inverse[...], dot(block, unfold(theirs)))


def call(kernel, outs, operands, scratch=(), smem=0, free=(), smem_outs=(), cost=None):
    specs = [
        SMEM if i < smem else ANY if i in free else VMEM for i in range(len(operands))
    ]
    return pl.pallas_call(
        kernel,
        out_shape=tuple(jax.ShapeDtypeStruct(s, t) for s, t in outs),
        in_specs=specs,
        out_specs=tuple(SMEM if i in smem_outs else VMEM for i in range(len(outs))),
        scratch_shapes=list(scratch),
        compiler_params=pltpu.CompilerParams(vmem_limit_bytes=VMEM_LIMIT),
        cost_estimate=cost,
    )(*operands)


def body(forcing_right_hand, material, capacity, conductivity, vent_open, partners, subspace_basis):
    layers, width, depth = forcing_right_hand.shape
    size = subspace_basis.shape[0]
    grid = Grid(layers, width, depth)
    n, cells = grid.rows, forcing_right_hand.size
    row_count, col_count = lax.axis_size("row"), lax.axis_size("col")
    pairs = partners.shape[-1]
    ids = jnp.concatenate(
        [
            partners.reshape(-1),
            jnp.stack([lax.axis_index("row"), lax.axis_index("col")]).astype(jnp.int32),
        ]
    )
    rhs = forcing_right_hand.reshape(n, depth)
    classes = material.reshape(n, depth)
    basis = subspace_basis.reshape(size, n, depth)
    field = ((n, depth), F32)
    pay = ((row_count, width + 2 * layers, depth), F32)
    small = ((size, size), F32)
    wide = ((max(n + size + size // 2, row_count * (width + 2 * layers) + 8), depth), F32)

    def cyclic(value, axis, step):
        count = lax.axis_size(axis)
        return lax.ppermute(value, axis, [(i, (i + step) % count) for i in range(count)])

    def xor_step(value, axis, k):
        count = lax.axis_size(axis)
        return lax.ppermute(value, axis, [(i, i ^ k) for i in range(count)])

    def exchange(value, payload):
        low = cyclic(value, "col", 1)
        high = cyclic(value, "col", -1)
        rec = lax.all_to_all(payload, "row", 0, 0)
        return rec, low, high

    def rows_of(count):
        return ((row_count, width + 2 * layers + count, depth), F32)

    tables = jnp.concatenate([conductivity, capacity, partners.reshape(-1).astype(F32)])
    zm, panel, *face = call(
        functools.partial(k_order, grid),
        (
            ((size, n * depth), BF16),
            ((size, width * depth), BF16),
            ((size, layers // 2 * depth), BF16),
            ((size, (layers - layers // 2) * depth), BF16),
        ),
        (basis,),
        cost=pl.CostEstimate(flops=1000, bytes_accessed=1000, transcendentals=0),
    )
    held = [xor_step(panel, "row", k) for k in range(2, row_count, 2)]
    across = [(i, (i + 1 if i % 2 else i - 1) % row_count) for i in range(row_count)]
    x_far_a, x_far_b = [lax.ppermute(part, "row", across) for part in face]
    cond, cap, vent, pay0 = call(
        functools.partial(k_first, grid, pairs),
        (((n + 8, depth), F32), field, ((width, depth), F32), rows_of(1)),
        (tables, classes, vent_open),
        smem=1,
    )
    rec0, cond_low, cond_high = exchange(cond, pay0)

    own_inner, projected, face_y = call(
        functools.partial(k_basis, grid),
        (small, ((size, depth), F32), ((size, depth), F32)),
        (zm, rhs, cond, cap),
        scratch=(
            pltpu.VMEM((n, size, depth), F32),
            pltpu.VMEM((3 * size, n * depth), BF16),
            pltpu.VMEM((7, n, depth), F32),
        ),
        cost=pl.CostEstimate(flops=1000, bytes_accessed=1000, transcendentals=0),
    )

    panels = ((pairs, size, width * depth), BF16)
    coef, own, inverse, sent, pay1, mine, wanted, vents, names = call(
        functools.partial(k_setup, grid, pairs, col_count),
        (
            ((7, n, depth), F32),
            small,
            small,
            ((n + 8, depth), F32),
            rows_of(size // 2),
            panels,
            ((size, (pairs * width + layers) * depth), BF16),
            ((pairs, width, depth), F32),
            ((4 + pairs, depth), F32),
        ),
        (
            ids, cap, vent, cond, cond_low, cond_high, rec0, zm, own_inner, projected, face_y,
            *held,
        ),
        scratch=(
            pltpu.VMEM((3 * size, n * depth), BF16),
            pltpu.VMEM((n, depth), F32),
            pltpu.SemaphoreType.DMA((2 * pairs,)),
        ),
        smem=1,
        free=range(11, 11 + len(held)),
    )
    others = xor_step(wanted, "row", 1)
    rec1, low1, high1 = exchange(sent, pay1)
    places = 5 + pairs
    x0, wide2, pay2, solves = call(
        functools.partial(k_coarse, grid, pairs),
        (field, wide, pay, ((2 + pairs, size // 2, depth), F32)),
        (ids, coef, vent, zm, inverse, sent, rec1, low1, high1, face_y, others),
        scratch=(pltpu.VMEM((n, depth), F32),),
        smem=1,
        free=(10,),
    )
    pay2, x_far_a, x_far_b = lax.optimization_barrier((pay2, x_far_a, x_far_b))
    rec, low2, high2 = exchange(wide2, pay2)

    def everyone(lines):
        return ((row_count * col_count, lines, depth), F32)

    r0, pay3 = call(
        functools.partial(k_partials, grid, pairs, True),
        (field, everyone((places + 1) // 2)),
        (
            ids, coef, vent, x0, x_far_a, x_far_b, rec, low2, high2, vents, zm, low2, high2, mine, others, rhs,
        ),
        smem=1,
    )
    blocks, weights, table = call(
        functools.partial(k_blocks, grid, pairs, col_count, 1.0 / cells),
        (
            ((row_count, size, size), F32),
            ((places, size, size), F32),
            ((places * places,), jnp.int32),
        ),
        (
            ids, coef, vents, names, zm, mine, others, x_far_a, x_far_b, own, inverse, face_y, low2,
            high2, solves, pay3,
        ),
        scratch=(pltpu.VMEM((3 * size, width * depth), BF16),),
        smem=1,
        free=(15,),
        smem_outs=(2,),
        cost=pl.CostEstimate(flops=100_000_000, bytes_accessed=4_000_000, transcendentals=0),
    )
    sums = lax.all_to_all(pay3, ("row", "col"), 0, 0)
    p0, wide4, pay4 = call(
        functools.partial(k_combine, grid),
        (field, wide, pay),
        (table, sums, weights, zm, r0, vent),
        scratch=(pltpu.VMEM((n, depth), F32),),
        smem=1,
    )
    rec, low, high = exchange(wide4, pay4)
    i0, pay5 = call(
        functools.partial(k_partials, grid, pairs, False),
        (field, everyone((places + 1) // 2)),
        (
            ids, coef, vent, p0, x_far_a, x_far_b, rec, low, high, vents, zm, low2, high2, mine, others,
        ),
        smem=1,
    )
    sums = lax.all_to_all(pay5, ("row", "col"), 0, 0)
    d0, wide6, pay6 = call(
        functools.partial(k_combine, grid),
        (field, wide, pay),
        (table, sums, weights, zm, i0, vent),
        scratch=(pltpu.VMEM((n, depth), F32),),
        smem=1,
    )
    rec, low, high = exchange(wide6, pay6)
    image, pay7 = call(
        functools.partial(k_dots, grid, pairs),
        (field, everyone(2)),
        (ids, coef, vent, d0, rec, low, high, r0, p0, i0),
        smem=1,
    )
    total = lax.all_to_all(pay7, ("row", "col"), 0, 0)
    x2, r2 = call(k_last, (field, field), (total, x0, r0, p0, i0, d0, image))
    shape = forcing_right_hand.shape
    return x2.reshape(shape), r2.reshape(shape), blocks[None, None]


def solution(mesh):
    return jax.shard_map(
        body,
        mesh=mesh,
        in_specs=(
            P(None, "row", "col"),
            P(None, "row", "col"),
            P(),
            P(),
            P("row", "col"),
            P("row", "col", None),
            P(None, None, "row", "col"),
        ),
        out_specs=(P(None, "row", "col"), P(None, "row", "col"), P("row", "col", None, None, None)),
        check_vma=False,
    )
```
